32 devices in a mesh: dp: 2 (over x), wide: 4 (over z), narrow: 4 (over y, core).
Axes of the slice: x: 2, y: 2, z: 4, core: 2. Of those that a mesh axis runs over, the one named last changes fastest.
Arguments:
- hidden_in: bfloat16 [2, 8, 1024, 768], P(None, ('dp', 'wide'), 'narrow'), may hold values from -6 to 6
- encoder_out: bfloat16 [2, 8, 512, 768], P(None, ('dp', 'wide'), 'narrow'), may hold values from -6 to 6
- cotangent: bfloat16 [2, 8, 1024, 768], P(None, ('dp', 'wide'), 'narrow'), may hold values from -6 to 6
- piece_starts: int32 [2, 8], P(None, ('dp', 'wide')), may hold values from 0 to 768
- valid_lengths: int32 [2, 8], P(None, ('dp', 'wide')), may hold values from 512 to 1024
- bucket_table: int32 [2047], replicated, may hold values from 0 to 31
- gain_self: float32 [768], replicated, may hold values from 0.5 to 1.5
- gain_cross: float32 [768], replicated, may hold values from 0.5 to 1.5
- gain_feed: float32 [768], replicated, may hold values from 0.5 to 1.5
- relative_bias: float32 [32, 12], P(None, 'narrow'), may hold values from -4 to 4
- self_query: bfloat16 [768, 768], P('wide', 'narrow'), may hold values from -0.0546875 to 0.0546875
- self_key: bfloat16 [768, 768], P('wide', 'narrow'), may hold values from -0.21875 to 0.21875
- self_value: bfloat16 [768, 768], P('wide', 'narrow'), may hold values from -0.21875 to 0.21875
- self_output: bfloat16 [768, 768], P('wide', 'narrow'), may hold values from -0.875 to 0.875
- cross_query: bfloat16 [768, 768], P('wide', 'narrow'), may hold values from -0.0546875 to 0.0546875
- cross_key: bfloat16 [768, 768], P('wide', 'narrow'), may hold values from -0.21875 to 0.21875
- cross_value: bfloat16 [768, 768], P('wide', 'narrow'), may hold values from -0.21875 to 0.21875
- cross_output: bfloat16 [768, 768], P('wide', 'narrow'), may hold values from -0.875 to 0.875
- gate_weight: bfloat16 [768, 2048], P('wide', 'narrow'), may hold values from -0.21875 to 0.21875
- up_weight: bfloat16 [768, 2048], P('wide', 'narrow'), may hold values from -0.21875 to 0.21875
- down_weight: bfloat16 [768, 2048], P('wide', 'narrow'), may hold values from -0.125 to 0.125
Outputs:
- output: bfloat16 [2, 8, 1024, 768], P(None, ('dp', 'wide'), 'narrow')
- grad_input: float32 [2, 8, 1024, 768], P(None, ('dp', 'wide'), 'narrow')
- grad_encoder: float32 [2, 8, 512, 768], P(None, ('dp', 'wide'), 'narrow')
- grad_gain_self: float32 [768], replicated
- grad_gain_cross: float32 [768], replicated
- grad_gain_feed: float32 [768], replicated
- grad_relative_bias: float32 [32, 12], P(None, 'narrow')
- grad_self_query: float32 [768, 768], P('wide', 'narrow')
- grad_self_key: float32 [768, 768], P('wide', 'narrow')
- grad_self_value: float32 [768, 768], P('wide', 'narrow')
- grad_self_output: float32 [768, 768], P('wide', 'narrow')
- grad_cross_query: float32 [768, 768], P('wide', 'narrow')
- grad_cross_key: float32 [768, 768], P('wide', 'narrow')
- grad_cross_value: float32 [768, 768], P('wide', 'narrow')
- grad_cross_output: float32 [768, 768], P('wide', 'narrow')
- grad_gate_weight: float32 [768, 2048], P('wide', 'narrow')
- grad_up_weight: float32 [768, 2048], P('wide', 'narrow')
- grad_down_weight: float32 [768, 2048], P('wide', 'narrow')
The draws below stay inside these ranges and needn't reach their ends.
Inputs may be any that keep to these rules, and one draw needn't show every extreme that they name: `piece_starts`: each sequence's picture piece of 256 tokens lies inside the sequence. `valid_lengths`: keys at or past a sequence's valid length are padding. `bucket_table`: entry j - i + 1023 is the bucket of offset j - i.
All inputs are finite; a program needn't handle non-finite values.
Results may differ from the reference program's by a relative error of at most 0.025.
Values may be sent and summed in bfloat16 or wider, within the bound.
A program may use at most 256 MiB of HBM per device.

```python
import jax
import jax.numpy as jnp
from jax import lax

D = 768
HEADS = 12
DHEAD = 64
FF = 2048
BUCKETS = 32
LEN = 1024
ENC = 512
PIC = 256
MICRO = 2
HD = 768
SEQ_MB = 8


def place_ends(values, rng, low, high):
    longest = values.shape.index(max(values.shape))
    spots = []
    for shift in (0, 1):
        where = [jax.random.randint(jax.random.fold_in(rng, axis), (), 0, length) for axis, length in enumerate(values.shape)]
        where[longest] = (where[longest] + shift) % values.shape[longest]
        spots.append(tuple(where))
    return values.at[spots[0]].set(low).at[spots[1]].set(high)


def shard_levels(own_key, dims, shards, least, top_value):
    def one(dim, blocks):
        heights = jax.random.uniform(jax.random.fold_in(jax.random.fold_in(own_key, 6), dim), (blocks,), jnp.float32, least / len(shards), top_value / len(shards))
        return jnp.repeat(jnp.exp(heights), dims[dim] // blocks).reshape((-1,) + (1,) * (len(dims) - dim - 1))

    level = one(*shards[0])
    for cut in shards[1:]:
        level = level * one(*cut)
    return level


def scatter_about(stream_key, extent, width, reach, split=(), kind=jnp.bfloat16):
    values = width * jax.random.normal(stream_key, extent, jnp.float32)
    if split:
        values = values * shard_levels(stream_key, extent, split, -0.22, 0.18)
    return jnp.clip(values, -reach, reach).astype(kind)


def setup_inputs(seed: int = 0) -> dict:
    keys = jax.random.split(jax.random.key(seed), 22)
    hidden_in = scatter_about(keys[0], (MICRO, SEQ_MB, LEN, D), 1.0, 6.0, ((1, 8), (2, 4)))
    encoder_out = scatter_about(keys[1], (MICRO, SEQ_MB, ENC, D), 1.0, 6.0, ((1, 8), (2, 4)))
    cotangent = scatter_about(keys[2], (MICRO, SEQ_MB, LEN, D), 1.0, 6.0, ((1, 8), (2, 4)))
    piece_starts = place_ends(jax.random.randint(keys[3], (MICRO, SEQ_MB), 0, LEN - PIC + 1), jax.random.fold_in(keys[3], 1), 0, LEN - PIC).astype(jnp.int32)
    valid_lengths = place_ends(jax.random.randint(keys[4], (MICRO, SEQ_MB), LEN // 2, LEN + 1), jax.random.fold_in(keys[4], 1), LEN // 2, LEN).astype(jnp.int32)
    bucket_table = place_ends(jax.random.randint(keys[5], (2 * LEN - 1,), 0, BUCKETS), jax.random.fold_in(keys[5], 1), 0, BUCKETS - 1).astype(jnp.int32)
    gain_self = jnp.clip(1.0 + 0.1 * jax.random.normal(keys[6], (D,), jnp.float32), 0.5, 1.5)
    gain_cross = jnp.clip(1.0 + 0.1 * jax.random.normal(keys[7], (D,), jnp.float32), 0.5, 1.5)
    gain_feed = jnp.clip(1.0 + 0.1 * jax.random.normal(keys[8], (D,), jnp.float32), 0.5, 1.5)
    relative_bias = scatter_about(keys[9], (BUCKETS, HEADS), 1.0, 4.0, ((1, 4),), jnp.float32)
    self_query = scatter_about(keys[10], (D, HD), (16 * D) ** -0.5, 0.0546875, ((0, 4), (1, 4)))
    self_key = scatter_about(keys[11], (D, HD), D ** -0.5, 0.21875, ((0, 4), (1, 4)))
    self_value = scatter_about(keys[12], (D, HD), D ** -0.5, 0.21875, ((0, 4), (1, 4)))
    self_output = scatter_about(keys[13], (D, HD), (HD // 16) ** -0.5, 0.875, ((0, 4), (1, 4)))
    cross_query = scatter_about(keys[14], (D, HD), (16 * D) ** -0.5, 0.0546875, ((0, 4), (1, 4)))
    cross_key = scatter_about(keys[15], (D, HD), D ** -0.5, 0.21875, ((0, 4), (1, 4)))
    cross_value = scatter_about(keys[16], (D, HD), D ** -0.5, 0.21875, ((0, 4), (1, 4)))
    cross_output = scatter_about(keys[17], (D, HD), (HD // 16) ** -0.5, 0.875, ((0, 4), (1, 4)))
    gate_weight = scatter_about(keys[18], (D, FF), D ** -0.5, 0.21875, ((0, 4), (1, 4)))
    up_weight = scatter_about(keys[19], (D, FF), D ** -0.5, 0.21875, ((0, 4), (1, 4)))
    down_weight = scatter_about(keys[20], (D, FF), FF ** -0.5, 0.125, ((0, 4), (1, 4)))
    return dict(hidden_in=hidden_in, encoder_out=encoder_out, cotangent=cotangent, piece_starts=piece_starts, valid_lengths=valid_lengths, bucket_table=bucket_table, gain_self=gain_self, gain_cross=gain_cross, gain_feed=gain_feed, relative_bias=relative_bias, self_query=self_query, self_key=self_key, self_value=self_value, self_output=self_output, cross_query=cross_query, cross_key=cross_key, cross_value=cross_value, cross_output=cross_output, gate_weight=gate_weight, up_weight=up_weight, down_weight=down_weight)


precise = lax.Precision.HIGHEST
epsilon = 1e-06
masked_value = -1e+30

@jax.custom_vjp
def low(v):
    return lax.optimization_barrier(v.astype(jnp.bfloat16)).astype(jnp.float32)

@jax.custom_vjp
def low_back(v):
    return v

def low_keep(v):
    return (low(v), None)

def low_pass(kept, grad):
    return (grad,)

def back_keep(v):
    return (v, None)

def back_low(kept, grad):
    return (low(grad),)
low.defvjp(low_keep, low_pass)
low_back.defvjp(back_keep, back_low)

def rounded(matrix_in):
    return low_back(low(matrix_in))

def rms_norm(hidden, gain):
    return hidden * lax.rsqrt(lax.optimization_barrier(jnp.mean(hidden * hidden, axis=-1, keepdims=True)) + epsilon) * gain

def project(left_arg, right_arg):
    return jnp.dot(left_arg, right_arg, precision=precise)

def split_heads(matrix_in):
    return matrix_in.reshape(matrix_in.shape[0], HEADS, DHEAD)

def attend(queries, keys_in, values_in, bias_full, allowed):
    scores = low_back(jnp.einsum('qhd,khd->hqk', queries, keys_in, precision=precise))
    if bias_full is not None:
        scores = jnp.where(allowed[None], scores + bias_full, masked_value)
    largest = lax.optimization_barrier(jnp.max(scores, axis=-1, keepdims=True))
    shifted = jnp.exp(scores - largest)
    probability = shifted / lax.optimization_barrier(jnp.sum(shifted, axis=-1, keepdims=True))
    attended = jnp.einsum('hqk,khd->qhd', low(probability), values_in, precision=precise)
    return rounded(attended).reshape(queries.shape[0], HEADS * DHEAD)

def one_sequence(params, tokens, memory, seq_start, length, offsets):
    gain_self, gain_cross, gain_feed, self_query, self_key, self_value, self_output, cross_query, cross_key, cross_value, cross_output, gate_weight, up_weight, down_weight = params
    positions = jnp.arange(LEN)
    query_pos = positions[:, None]
    key_pos = positions[None, :]
    in_piece = (positions >= seq_start) & (positions < seq_start + PIC)
    allowed = ((key_pos <= query_pos) | in_piece[:, None] & in_piece[None, :]) & (key_pos < length)
    bias_full = jnp.transpose(offsets[key_pos - query_pos + LEN - 1], (2, 0, 1))
    normed_one = low(rms_norm(tokens, gain_self))
    attn_one = attend(split_heads(rounded(project(normed_one, self_query))), split_heads(rounded(project(normed_one, self_key))), split_heads(rounded(project(normed_one, self_value))), bias_full, allowed)
    hidden_one = tokens + low_back(project(attn_one, self_output.T))
    normed_two = low(rms_norm(hidden_one, gain_cross))
    attn_two = attend(split_heads(rounded(project(normed_two, cross_query))), split_heads(rounded(project(memory, cross_key))), split_heads(rounded(project(memory, cross_value))), None, None)
    hidden_two = hidden_one + low_back(project(attn_two, cross_output.T))
    normed_three = low(rms_norm(hidden_two, gain_feed))
    gate_pre = low_back(project(normed_three, gate_weight))
    up_pre = low_back(project(normed_three, up_weight))
    activated = low(jax.nn.gelu(gate_pre, approximate=True) * up_pre)
    return hidden_two + low_back(project(activated, down_weight.T))

def reference(hidden_in, encoder_out, cotangent, piece_starts, valid_lengths, bucket_table, gain_self, gain_cross, gain_feed, relative_bias, self_query, self_key, self_value, self_output, cross_query, cross_key, cross_value, cross_output, gate_weight, up_weight, down_weight):
    matrices = tuple((matrix.astype(jnp.float32) for matrix in (self_query, self_key, self_value, self_output, cross_query, cross_key, cross_value, cross_output, gate_weight, up_weight, down_weight)))

    def forward(tokens, memory, gains, bias_table, weights_in):
        offsets = bias_table[bucket_table]
        params = gains + weights_in

        def per_sequence(seq_items):
            return one_sequence(params, seq_items[0], seq_items[1], seq_items[2], seq_items[3], offsets)
        results = lax.map(jax.checkpoint(per_sequence), (tokens.reshape(-1, LEN, D), memory.reshape(-1, ENC, D), piece_starts.reshape(-1), valid_lengths.reshape(-1)))
        return results.reshape(tokens.shape)
    result, pull_back = jax.vjp(forward, hidden_in.astype(jnp.float32), encoder_out.astype(jnp.float32), (gain_self, gain_cross, gain_feed), relative_bias, matrices)
    grad_tokens, grad_memory, grad_gains, grad_table, grad_mats = pull_back(cotangent.astype(jnp.float32))
    return (result.astype(jnp.bfloat16), grad_tokens, grad_memory, grad_gains[0], grad_gains[1], grad_gains[2], grad_table, grad_mats[0], grad_mats[1], grad_mats[2], grad_mats[3], grad_mats[4], grad_mats[5], grad_mats[6], grad_mats[7], grad_mats[8], grad_mats[9], grad_mats[10])
```

```python
from functools import partial

import jax
import jax.numpy as jnp
from jax import lax
from jax.experimental import pallas as pl
from jax.experimental.pallas import tpu as pltpu
from jax.sharding import PartitionSpec as P

D = 768
HD = 192
HEADS = 12
DHEAD = 64
FFB = 512
BUCKETS = 32
LEN = 1024
ENC = 512
PIC = 256
TILES = 11
ROWS = 32

precise = lax.Precision.HIGHEST
epsilon = 1e-06
masked_value = -1e30
f32 = jnp.float32
bf16 = jnp.bfloat16
MESH = pl.DeviceIdType.MESH
ANY = pl.BlockSpec(memory_space=pl.ANY)
VMEM_LIMIT = 60 << 20


def nn(a, b):
    return lax.dot_general(a, b, (((1,), (0,)), ((), ())), preferred_element_type=f32)


def nt(a, b):
    return lax.dot_general(a, b, (((1,), (1,)), ((), ())), preferred_element_type=f32)


def tn(a, b):
    return lax.dot_general(a, b, (((0,), (0,)), ((), ())), preferred_element_type=f32)


def rows_loop(total, step, body, unroll=1):
    def run(i, carry):
        body(pl.ds(pl.multiple_of(i * step, step), step))
        return carry

    lax.fori_loop(0, total // step, run, 0, unroll=unroll)


def normed(x, gain):
    factor = lax.rsqrt(jnp.mean(x * x, axis=1, keepdims=True) + epsilon)
    return x * factor * gain


def norm_back(x, gain, upstream):
    factor = lax.rsqrt(jnp.mean(x * x, axis=1, keepdims=True) + epsilon)
    weighted = upstream * gain
    inner = jnp.sum(weighted * x, axis=1, keepdims=True)
    dx = weighted * factor - x * (factor * factor * factor * inner * (1.0 / D))
    return dx, jnp.sum(upstream * x * factor, axis=0, keepdims=True)


def own_blocks():
    me = lax.axis_index("narrow")
    return (me, 3 - me)


def block_rows(blk):
    return pl.ds(pl.multiple_of(blk * 256, 256), 256)


def softmax_rows(v):
    e = jnp.exp(v - jnp.max(v, axis=1, keepdims=True))
    return e * (1.0 / jnp.sum(e, axis=1, keepdims=True))


def self_forward_kernel(
    info, xf, w, off, gain, q_o, kv_o, at_o, p_o, h1_o, nf, mask, tb, s
):
    n = pl.program_id(0)
    blks = own_blocks()

    @pl.when(n == 0)
    def _():
        def norm_rows(r):
            nf[r, :] = normed(xf[r, :].astype(f32), gain[...]).astype(bf16)

        rows_loop(LEN, 64, norm_rows)
        start, length = info[0], info[1]
        for i in range(2):
            h1_o[i * 256 : (i + 1) * 256, :] = xf[block_rows(blks[i]), :].astype(f32)

            def mask_rows(r, i=i):
                shape = (ROWS, LEN)
                qi = blks[i] * 256 + r.start + lax.broadcasted_iota(jnp.int32, shape, 0)
                kj = lax.broadcasted_iota(jnp.int32, shape, 1)
                inside = (qi >= start) & (qi < start + PIC) & (kj >= start) & (kj < start + PIC)
                allowed = ((kj <= qi) | inside) & (kj < length)
                mask[pl.ds(i * 256 + r.start, ROWS), :] = jnp.where(allowed, 0.0, masked_value)

            rows_loop(256, ROWS, mask_rows)

    kv_o[0] = nn(nf[...], w[0, :, 384:768]).astype(bf16).T
    for i in range(2):
        q_o[0, i * 256 : (i + 1) * 256, :] = nn(nf[block_rows(blks[i]), :], w[0, :, 0:192]).astype(bf16)
    for h in range(3):
        for t in range(TILES):
            line = jnp.broadcast_to(off[0, h : h + 1, 128 * t : 128 * t + 256], (128, 256))
            tb[t] = pltpu.roll(line, 129, 1, stride=1, stride_axis=0)[:, :128]
        hs = slice(h * DHEAD, (h + 1) * DHEAD)
        vs = slice(HD + h * DHEAD, HD + (h + 1) * DHEAD)
        for i in range(2):
            s[...] = nn(q_o[0, i * 256 : (i + 1) * 256, hs], kv_o[0, hs, :])
            for r in range(2):
                idx = [jnp.minimum(kb - 2 * blks[i] - r, 3) + 7 for kb in range(8)]

                def soft_rows(rr, i=i, r=r, h=h, idx=idx):
                    bias = jnp.concatenate([tb[idx[kb], rr, :] for kb in range(8)], axis=1)
                    v = s[pl.ds(r * 128 + rr.start, ROWS), :] + bias
                    v = v + mask[pl.ds(i * 256 + r * 128 + rr.start, ROWS), :]
                    p_o[0, h, pl.ds(i * 256 + r * 128 + rr.start, ROWS), :] = softmax_rows(v).astype(bf16)

                rows_loop(128, ROWS, soft_rows)
            at_o[0, i * 256 : (i + 1) * 256, hs] = nt(
                p_o[0, h, i * 256 : (i + 1) * 256, :], kv_o[0, vs, :]
            ).astype(bf16)
    h1_o[...] += nt(at_o[0], w[0, :, 192:384])


def whole(shape):
    zero = (0,) * len(shape)
    return pl.BlockSpec(shape, lambda n: zero)


def slab(shape):
    zero = (0,) * len(shape)
    return pl.BlockSpec((1,) + shape, lambda n: (n,) + zero)


def params():
    return pltpu.CompilerParams(
        dimension_semantics=("arbitrary",), vmem_limit_bytes=VMEM_LIMIT
    )


def out(shape, dtype):
    return jax.ShapeDtypeStruct(shape, dtype)


SMEM = pl.BlockSpec(memory_space=pltpu.SMEM)


def cost(gflop):
    return pl.CostEstimate(flops=int(gflop * 1e9), bytes_accessed=20 << 20, transcendentals=0)


def self_forward(info, xf, w, off, gain):
    return pl.pallas_call(
        self_forward_kernel,
        grid=(4,),
        in_specs=[SMEM, whole((LEN, D)), slab((D, D)), slab((3, 2048)), whole((1, D))],
        out_specs=[slab((512, HD)), slab((2 * HD, LEN)), slab((512, HD)), slab((3, 512, LEN)), whole((512, D))],
        out_shape=[
            out((4, 512, HD), bf16),
            out((4, 2 * HD, LEN), bf16),
            out((4, 512, HD), bf16),
            out((4, 3, 512, LEN), bf16),
            out((512, D), f32),
        ],
        scratch_shapes=[
            pltpu.VMEM((LEN, D), bf16),
            pltpu.VMEM((512, LEN), f32),
            pltpu.VMEM((TILES, 128, 128), f32),
            pltpu.VMEM((256, LEN), f32),
        ],
        compiler_params=params(),
        cost_estimate=cost(20),
        name="self_forward",
    )(info, xf, w, off, gain)


def cross_forward_kernel(h1, ef, w, gain, q_o, kv_o, at_o, p_o, h2_o, nc, s):
    n = pl.program_id(0)

    @pl.when(n == 0)
    def _():
        def norm_rows(r):
            x = h1[r, :]
            nc[r, :] = normed(x, gain[...]).astype(bf16)
            h2_o[r, :] = x

        rows_loop(512, 64, norm_rows)

    kv_o[0] = nn(ef[...], w[0, :, 384:768]).astype(bf16).T
    q_o[0] = nn(nc[...], w[0, :, 0:192]).astype(bf16)
    for h in range(3):
        hs = slice(h * DHEAD, (h + 1) * DHEAD)
        vs = slice(HD + h * DHEAD, HD + (h + 1) * DHEAD)
        s[...] = nn(q_o[0, :, hs], kv_o[0, hs, :])

        def soft_rows(r, h=h):
            p_o[0, h, r, :] = softmax_rows(s[r, :]).astype(bf16)

        rows_loop(512, 64, soft_rows)
        at_o[0, :, hs] = nt(p_o[0, h], kv_o[0, vs, :]).astype(bf16)
    h2_o[...] += nt(at_o[0], w[0, :, 192:384])


def cross_forward(h1, ef, w, gain):
    return pl.pallas_call(
        cross_forward_kernel,
        grid=(4,),
        in_specs=[whole((512, D)), whole((ENC, D)), slab((D, D)), whole((1, D))],
        out_specs=[slab((512, HD)), slab((2 * HD, ENC)), slab((512, HD)), slab((3, 512, ENC)), whole((512, D))],
        out_shape=[
            out((4, 512, HD), bf16),
            out((4, 2 * HD, ENC), bf16),
            out((4, 512, HD), bf16),
            out((4, 3, 512, ENC), bf16),
            out((512, D), f32),
        ],
        scratch_shapes=[pltpu.VMEM((512, D), bf16), pltpu.VMEM((512, ENC), f32)],
        compiler_params=params(),
        cost_estimate=cost(10),
        name="cross_forward",
    )(h1, ef, w, gain)


GELU_A = 0.7978845608028654
GELU_B = 0.044715


def feed_kernel(h2, cf, w, gain, gw_o, out_o, d2_o, gg_o, nf, nft, ct, gu, da, act, dgu, acc):
    n = pl.program_id(0)

    @pl.when(n == 0)
    def _():
        def norm_rows(r):
            x = h2[r, :]
            nf[r, :] = normed(x, gain[...]).astype(bf16)
            acc[r, :] = x
            d2_o[r, :] = jnp.zeros((64, D), f32)

        rows_loop(512, 64, norm_rows)
        nft[...] = nf[...].T
        ct[...] = cf[...].T

    gu[...] = nn(nf[...], w[0, :, : 2 * FFB])
    da[...] = nn(cf[...], w[0, :, 2 * FFB :])

    def gelu_rows(r):
        gate = gu[r, :FFB]
        up = gu[r, FFB:]
        d_act = da[r, :]
        sq = gate * gate
        th = jnp.tanh(GELU_A * gate * (1.0 + GELU_B * sq))
        half = 0.5 + 0.5 * th
        gelu = gate * half
        slope = half + 0.5 * GELU_A * gate * (1.0 - th * th) * (1.0 + 3.0 * GELU_B * sq)
        act[r, :] = (gelu * up).astype(bf16)
        dgu[r, :FFB] = (d_act * up * slope).astype(bf16)
        dgu[r, FFB:] = (d_act * gelu).astype(bf16)

    rows_loop(512, 16, gelu_rows)
    acc[...] += nt(act[...], w[0, :, 2 * FFB :])
    gw_o[0, :, : 2 * FFB] = nn(nft[...], dgu[...]).astype(bf16)
    gw_o[0, :, 2 * FFB :] = nn(ct[...], act[...]).astype(bf16)
    d2_o[...] += nt(dgu[...], w[0, :, : 2 * FFB])

    @pl.when(n == 3)
    def _():
        gg_o[...] = jnp.zeros((1, D), f32)

        def back_rows(r):
            dx, gg = norm_back(h2[r, :], gain[...], d2_o[r, :])
            d2_o[r, :] = cf[r, :].astype(f32) + dx
            gg_o[...] += gg
            out_o[r, :] = acc[r, :].astype(bf16)

        rows_loop(512, 64, back_rows)


def feed(h2, cf, w, gain):
    return pl.pallas_call(
        feed_kernel,
        grid=(4,),
        in_specs=[whole((512, D)), whole((512, D)), slab((D, 3 * FFB)), whole((1, D))],
        out_specs=[slab((D, 3 * FFB)), whole((512, D)), whole((512, D)), whole((1, D))],
        out_shape=[out((4, D, 3 * FFB), bf16), out((512, D), bf16), out((512, D), f32), out((1, D), f32)],
        scratch_shapes=[
            pltpu.VMEM((512, D), bf16),
            pltpu.VMEM((D, 512), bf16),
            pltpu.VMEM((D, 512), bf16),
            pltpu.VMEM((512, 2 * FFB), f32),
            pltpu.VMEM((512, FFB), f32),
            pltpu.VMEM((512, FFB), bf16),
            pltpu.VMEM((512, 2 * FFB), bf16),
            pltpu.VMEM((512, D), f32),
        ],
        compiler_params=params(),
        cost_estimate=cost(30),
        name="feed",
    )(h2, cf, w, gain)


def cross_backward_kernel(
    h1, ef, d2, w, gain, q, kv, at, p, gw_o, d1_o, gg_o, ge_o, gep_o, d2b, d2t, nct, eft, get, do, dp, ds, dq, dkv
):
    n = pl.program_id(0)

    @pl.when(n == 0)
    def _():
        def norm_rows(r):
            d2b[r, :] = d2[r, :].astype(bf16)
            d1_o[r, :] = jnp.zeros((64, D), f32)
            dp[r, :] = normed(h1[r, :], gain[...])

        rows_loop(512, 64, norm_rows)
        nct[...] = dp[...].astype(bf16).T
        d2t[...] = d2b[...].T
        eft[...] = ef[...].T
        get[...] = jnp.zeros((D, ENC), f32)

    do[...] = nn(d2b[...], w[0, :, 192:384]).astype(bf16)
    for h in range(3):
        hs = slice(h * DHEAD, (h + 1) * DHEAD)
        vs = slice(HD + h * DHEAD, HD + (h + 1) * DHEAD)
        dp[:, :ENC] = nn(do[:, hs], kv[0, vs, :])

        def grad_rows(r, h=h, hs=hs):
            delta = jnp.sum(do[r, hs].astype(f32) * at[0, r, hs].astype(f32), axis=1, keepdims=True)
            ds[r, :] = (p[0, h, r, :].astype(f32) * (dp[r, :ENC] - delta)).astype(bf16)

        rows_loop(512, 64, grad_rows)
        dq[:, hs] = nt(ds[...], kv[0, hs, :]).astype(bf16)
        dkv[hs, :] = tn(q[0, :, hs], ds[...]).astype(bf16)
        dkv[vs, :] = tn(do[:, hs], p[0, h]).astype(bf16)
    d1_o[...] += nt(dq[...], w[0, :, 0:192])
    get[...] += nn(w[0, :, 384:768], dkv[...])
    gw_o[0, :, 0:384] = jnp.concatenate([nn(nct[...], dq[...]), nn(d2t[...], at[0])], axis=1).astype(bf16)
    gw_o[0, :, 384:768] = nt(eft[...], dkv[...]).astype(bf16)

    @pl.when(n == 3)
    def _():
        gg_o[...] = jnp.zeros((1, D), f32)

        def back_rows(r):
            dx, gg = norm_back(h1[r, :], gain[...], d1_o[r, :])
            d1_o[r, :] = d2[r, :] + dx
            gg_o[...] += gg

        rows_loop(512, 64, back_rows)
        me = lax.axis_index("narrow")
        pn = me + 1 - 2 * lax.rem(me, 2)
        for i in range(2):
            half = slice(i * 128, (i + 1) * 128)
            cols = lambda blk: pl.ds(pl.multiple_of(blk * 128, 128), 128)
            ge_o[half, :] = get[:, cols((me, 3 - me)[i])].T
            gep_o[half, :] = get[:, cols((pn, 3 - pn)[i])].T.astype(bf16)


def cross_backward(h1, ef, d2, w, gain, q, kv, at, p):
    return pl.pallas_call(
        cross_backward_kernel,
        grid=(4,),
        in_specs=[
            whole((512, D)),
            whole((ENC, D)),
            whole((512, D)),
            slab((D, D)),
            whole((1, D)),
            slab((512, HD)),
            slab((2 * HD, ENC)),
            slab((512, HD)),
            slab((3, 512, ENC)),
        ],
        out_specs=[slab((D, D)), whole((512, D)), whole((1, D)), whole((256, D)), whole((256, D))],
        out_shape=[out((4, D, D), bf16), out((512, D), f32), out((1, D), f32), out((256, D), f32), out((256, D), bf16)],
        scratch_shapes=[
            pltpu.VMEM((512, D), bf16),
            pltpu.VMEM((D, 512), bf16),
            pltpu.VMEM((D, 512), bf16),
            pltpu.VMEM((D, ENC), bf16),
            pltpu.VMEM((D, ENC), f32),
            pltpu.VMEM((512, HD), bf16),
            pltpu.VMEM((512, D), f32),
            pltpu.VMEM((512, ENC), bf16),
            pltpu.VMEM((512, HD), bf16),
            pltpu.VMEM((2 * HD, ENC), bf16),
        ],
        compiler_params=params(),
        cost_estimate=cost(14),
        name="cross_backward",
    )(h1, ef, d2, w, gain, q, kv, at, p)


def self_backward_kernel(
    xf, d1, w, gain, q, kv, at, p, gw_o, g_o, gp_o, dl_o, d1b, d1t, nft, nqt, gt, gq, do, dp, ds, dq, dkv, dt
):
    n = pl.program_id(0)
    blks = own_blocks()

    @pl.when(n == 0)
    def _():
        def cast_rows(r):
            d1b[r, :] = d1[r, :].astype(bf16)
            gq[r, :] = jnp.zeros((64, D), f32)

        rows_loop(512, 64, cast_rows)
        d1t[...] = d1b[...].T
        for i in range(4):
            part = normed(xf[i * 256 : (i + 1) * 256, :].astype(f32), gain[...]).astype(bf16)
            nft[:, i * 256 : (i + 1) * 256] = part.T
        for i in range(2):
            part = normed(xf[block_rows(blks[i]), :].astype(f32), gain[...]).astype(bf16)
            nqt[:, i * 256 : (i + 1) * 256] = part.T
        gt[...] = jnp.zeros((D, LEN), f32)

    do[...] = nn(d1b[...], w[0, :, 192:384]).astype(bf16)
    for h in range(3):
        hs = slice(h * DHEAD, (h + 1) * DHEAD)
        vs = slice(HD + h * DHEAD, HD + (h + 1) * DHEAD)
        dt[...] = jnp.zeros((TILES, 128, 128), f32)
        dk = jnp.zeros((DHEAD, LEN), f32)
        dv = jnp.zeros((DHEAD, LEN), f32)
        for i in range(2):
            half = slice(i * 256, (i + 1) * 256)
            dp[...] = nn(do[half, hs], kv[0, vs, :])
            for r in range(2):
                idx = [jnp.minimum(kb - 2 * blks[i] - r, 3) + 7 for kb in range(8)]

                def grad_rows(rr, i=i, r=r, h=h, hs=hs, idx=idx):
                    rows = pl.ds(i * 256 + r * 128 + rr.start, ROWS)
                    local = pl.ds(r * 128 + rr.start, ROWS)
                    delta = jnp.sum(
                        do[rows, hs].astype(f32) * at[0, rows, hs].astype(f32), axis=1, keepdims=True
                    )
                    grad = p[0, h, rows, :].astype(f32) * (dp[local, :] - delta)
                    ds[local, :] = grad.astype(bf16)
                    for kb in range(8):
                        dt[idx[kb], rr, :] += grad[:, kb * 128 : (kb + 1) * 128]

                rows_loop(128, ROWS, grad_rows)
            dq[half, hs] = nt(ds[...], kv[0, hs, :]).astype(bf16)
            dk = dk + tn(q[0, half, hs], ds[...])
            dv = dv + tn(do[half, hs], p[0, h, half, :])
        dkv[hs, :] = dk.astype(bf16)
        dkv[vs, :] = dv.astype(bf16)
        for t in range(TILES):
            part = jnp.concatenate([dt[t], jnp.zeros((128, 128), f32)], axis=1)
            height = 128
            while height > 1:
                height //= 2
                part = part[:height] + pltpu.roll(part[height:], 256 - height, 1)
            dl_o[0, h * TILES + t : h * TILES + t + 1, :] = pltpu.roll(part, 127, 1)
    gq[...] += nt(dq[...], w[0, :, 0:192])
    gt[...] += nn(w[0, :, 384:768], dkv[...])
    gw_o[0, :, 0:384] = jnp.concatenate([nn(nqt[...], dq[...]), nn(d1t[...], at[0])], axis=1).astype(bf16)
    gw_o[0, :, 384:768] = nt(nft[...], dkv[...]).astype(bf16)

    @pl.when(n == 3)
    def _():
        pn = blks[0] + 1 - 2 * lax.rem(blks[0], 2)
        for i in range(2):
            half = slice(i * 256, (i + 1) * 256)
            g_o[half, :] = gq[half, :] + gt[:, block_rows(blks[i])].T
            gp_o[half, :] = gt[:, block_rows((pn, 3 - pn)[i])].T.astype(bf16)


def self_backward(xf, d1, w, gain, q, kv, at, p):
    return pl.pallas_call(
        self_backward_kernel,
        grid=(4,),
        in_specs=[
            whole((LEN, D)),
            whole((512, D)),
            slab((D, D)),
            whole((1, D)),
            slab((512, HD)),
            slab((2 * HD, LEN)),
            slab((512, HD)),
            slab((3, 512, LEN)),
        ],
        out_specs=[slab((D, D)), whole((512, D)), whole((512, D)), slab((3 * TILES, 256))],
        out_shape=[out((4, D, D), bf16), out((512, D), f32), out((512, D), bf16), out((4, 3 * TILES, 256), f32)],
        scratch_shapes=[
            pltpu.VMEM((512, D), bf16),
            pltpu.VMEM((D, 512), bf16),
            pltpu.VMEM((D, LEN), bf16),
            pltpu.VMEM((D, 512), bf16),
            pltpu.VMEM((D, LEN), f32),
            pltpu.VMEM((512, D), f32),
            pltpu.VMEM((512, HD), bf16),
            pltpu.VMEM((256, LEN), f32),
            pltpu.VMEM((256, LEN), bf16),
            pltpu.VMEM((512, HD), bf16),
            pltpu.VMEM((2 * HD, LEN), bf16),
            pltpu.VMEM((TILES, 128, 128), f32),
        ],
        compiler_params=params(),
        cost_estimate=cost(25),
        name="self_backward",
    )(xf, d1, w, gain, q, kv, at, p)


def place_here():
    d, w, n = lax.axis_index("dp"), lax.axis_index("wide"), lax.axis_index("narrow")
    return d, w, n, n + 1 - 2 * lax.rem(n, 2), lax.rem(n + 2, 4), 3 - n


def remote(src, dst, send, recv, dev):
    return pltpu.make_async_remote_copy(
        src_ref=src, dst_ref=dst, send_sem=send, recv_sem=recv, device_id=dev, device_id_type=MESH
    )


def greet(wide):
    d, w, n, pn, yn, dn = place_here()
    barrier = pltpu.get_barrier_semaphore()
    for dev in ((d, w, pn), (d, w, yn), (d, w, dn), (1 - d, w, n)):
        pl.semaphore_signal(barrier, inc=1, device_id=dev, device_id_type=MESH)

    def line(k, carry):
        dev = (d, lax.rem(w + k, wide), n)
        pl.semaphore_signal(barrier, inc=1, device_id=dev, device_id_type=MESH)
        return carry

    lax.fori_loop(1, wide, line, 0)
    pl.semaphore_wait(barrier, wide + 3)


def loop(lo, hi, body):
    def run(k, carry):
        body(k)
        return carry

    lax.fori_loop(lo, hi, run, 0)


def gather_kernel(
    wide, hid, enc, cot, tab, ps, pc, pf, xf, ef, cf, tabs, gs, gc, gf, ls, ins, inr, zs, zr, ys, yr, xs, xr, cs, cr
):
    d, w, n, pn, yn, dn = place_here()
    y = n // 2
    groups = ((ps, gs, 0, 768, True), (pc, gc, 0, 768, True), (pf, gf, 0, 512, True), (pf, gf, 512, 1024, False))

    def cols(s, which):
        start, width, split = groups[s][2:]
        if which == 2 or not split:
            return pl.ds(start, width)
        half = width // 2
        pos = d if which == 0 else 1 - d
        return pl.ds(pl.multiple_of(start + pos * half, 128), half)

    def own(s, which):
        return groups[s][0].at[:, cols(s, which)]

    def spot(s, slab, row, which):
        return groups[s][1].at[slab, row, :, cols(s, which)]

    def zcopy(s, k):
        return remote(own(s, 0), spot(s, n, w, 0), zs.at[s, k], zr.at[s, w], (d, lax.rem(w + k, wide), n))

    def zgot(s, row):
        return remote(spot(s, n, row, 0), spot(s, n, row, 0), zs.at[s, 0], zr.at[s, row], (1 - d, w, n))

    def ycopy(s, row, src):
        return remote(src, spot(s, n, row, 0), ys.at[s, row], yr.at[s, row], (d, w, yn))

    def ygot(s, row):
        return remote(spot(s, yn, row, 0), spot(s, yn, row, 0), ys.at[s, row], yr.at[s, row], (d, w, yn))

    def slab_of(side):
        return n if side == 0 else yn

    def xcopy(s, side, row):
        ref = spot(s, slab_of(side), row, 0)
        return remote(ref, ref, xs.at[s, side, row], xr.at[s, side, row], (1 - d, w, n))

    def xgot(s, side, row):
        ref = spot(s, slab_of(side), row, 1)
        return remote(ref, ref, xs.at[s, side, row], xr.at[s, side, row], (1 - d, w, n))

    def ccopy(s, side, row, src=None):
        ref = spot(s, slab_of(side), row, 2)
        return remote(ref if src is None else src, ref, cs.at[s, side, row], cr.at[s, side, row], (d, w, pn))

    def cgot(s, side, row):
        ref = spot(s, pn if side == 0 else 3 - n, row, 2)
        return remote(ref, ref, cs.at[s, side, row], cr.at[s, side, row], (d, w, pn))

    local = [
        pltpu.make_async_copy(src, dst, ls.at[i])
        for i, (src, dst) in enumerate(
            (
                (ps, gs.at[n, w]),
                (pc, gc.at[n, w]),
                (pf, gf.at[n, w]),
                (hid.at[y], xf.at[n]),
                (enc.at[y], ef.at[n]),
                (cot.at[y], cf.at[0]),
                (tab, tabs.at[n]),
            )
        )
    ]
    for copy in local:
        copy.start()
    greet(wide)
    diag, pair = (d, w, dn), (d, w, pn)
    first = [
        remote(hid.at[1 - y], xf.at[n], ins.at[0], inr.at[0], diag),
        remote(enc.at[1 - y], ef.at[n], ins.at[1], inr.at[1], diag),
        remote(cot.at[1 - y], cf.at[1], ins.at[2], inr.at[2], diag),
        remote(tab, tabs.at[n], ins.at[3], inr.at[3], pair),
        remote(tab, tabs.at[n], ins.at[4], inr.at[4], (d, w, yn)),
        remote(tab, tabs.at[n], ins.at[5], inr.at[5], diag),
        remote(hid.at[y], xf.at[n], ins.at[6], inr.at[6], pair),
        remote(enc.at[y], ef.at[n], ins.at[7], inr.at[7], pair),
    ]
    got = [
        remote(xf.at[dn], xf.at[dn], ins.at[0], inr.at[0], diag),
        remote(ef.at[dn], ef.at[dn], ins.at[1], inr.at[1], diag),
        remote(cf.at[1], cf.at[1], ins.at[2], inr.at[2], diag),
        remote(tabs.at[pn], tabs.at[pn], ins.at[3], inr.at[3], pair),
        remote(tabs.at[yn], tabs.at[yn], ins.at[4], inr.at[4], (d, w, yn)),
        remote(tabs.at[dn], tabs.at[dn], ins.at[5], inr.at[5], diag),
        remote(xf.at[pn], xf.at[pn], ins.at[6], inr.at[6], pair),
        remote(ef.at[pn], ef.at[pn], ins.at[7], inr.at[7], pair),
        remote(xf.at[yn], xf.at[yn], ins.at[8], inr.at[8], pair),
        remote(ef.at[yn], ef.at[yn], ins.at[9], inr.at[9], pair),
    ]
    later = [
        remote(xf.at[dn], xf.at[dn], ins.at[8], inr.at[8], pair),
        remote(ef.at[dn], ef.at[dn], ins.at[9], inr.at[9], pair),
    ]
    for copy in first:
        copy.start()
    for s in range(4):
        loop(1, wide, lambda k, s=s: zcopy(s, k).start())
        ycopy(s, w, own(s, 0)).start()
        ccopy(s, 0, w, own(s, 2)).start()
    got[0].wait_recv()
    later[0].start()
    got[1].wait_recv()
    later[1].start()

    def zstep(s):
        def one(k):
            row = lax.rem(w + k, wide)
            zgot(s, row).wait_recv()
            ycopy(s, row, spot(s, n, row, 0)).start()
            if groups[s][4]:
                xcopy(s, 0, row).start()
            else:
                ccopy(s, 0, row).start()

        loop(1, wide, one)

    def ystep(s):
        def one(k):
            row = lax.rem(w + k, wide)
            ygot(s, row).wait_recv()
            if groups[s][4]:
                xcopy(s, 1, row).start()
            else:
                ccopy(s, 1, row).start()

        loop(0, wide, one)

    def xstep(s):
        def one(side):
            def step(k):
                row = lax.rem(w + k, wide)
                xgot(s, side, row).wait_recv()
                ccopy(s, side, row).start()

            return step

        loop(1, wide, one(0))
        loop(0, wide, one(1))

    zstep(0)
    ystep(0)
    zstep(1)
    ystep(1)
    xstep(0)
    zstep(2)
    ystep(2)
    xstep(1)
    zstep(3)
    ystep(3)
    xstep(2)
    for copy in got[2:]:
        copy.wait_recv()
    for copy in local:
        copy.wait()
    for copy in first + later:
        copy.wait_send()

    def finish(k):
        row = lax.rem(w + k, wide)
        for s in range(4):
            for side in range(2):
                cgot(s, side, row).wait_recv()
                ccopy(s, side, row).wait_send()
            ycopy(s, row, spot(s, n, row, 0)).wait_send()
            if groups[s][4]:
                xcopy(s, 1, row).wait_send()

    loop(0, wide, finish)

    def finish_line(k):
        row = lax.rem(w + k, wide)
        for s in range(4):
            zcopy(s, k).wait_send()
            if groups[s][4]:
                xcopy(s, 0, row).wait_send()

    loop(1, wide, finish_line)


def gather(wide, hid, enc, cot, tab, ps, pc, pf):
    rl = ps.shape[0]
    sem = pltpu.SemaphoreType.DMA
    return pl.pallas_call(
        partial(gather_kernel, wide),
        in_specs=[ANY] * 7,
        out_specs=[ANY] * 7,
        out_shape=[
            out((4, 256, D), bf16),
            out((4, 128, D), bf16),
            out((2, 256, D), bf16),
            out((4, 32, 128), f32),
            out((4, wide, rl, D), bf16),
            out((4, wide, rl, D), bf16),
            out((4, wide, rl, 2 * D), bf16),
        ],
        scratch_shapes=[
            sem((7,)),
            sem((10,)),
            sem((10,)),
            sem((4, wide)),
            sem((4, wide)),
            sem((4, wide)),
            sem((4, wide)),
            sem((4, 2, wide)),
            sem((4, 2, wide)),
            sem((4, 2, wide)),
            sem((4, 2, wide)),
        ],
        compiler_params=pltpu.CompilerParams(collective_id=0, has_side_effects=True),
        name="gather",
    )(hid, enc, cot, tab, ps, pc, pf)


SHARE = (512, 256, 512, 256)


def reduce_kernel(
    wide, rl, ff, cr, se, outp, gxo, gxp, geo, gep, xf, d1, gain, gfeed, gcross, tg,
    out_o, gin_o, gen_o, sg_o, st_o, f0, f1, f2, f3, *scratch
):
    d, w, n, pn, yn, dn = place_here()
    y = n // 2
    pair, line_y, diag, line_x = (d, w, pn), (d, w, yn), (d, w, dn), (1 - d, w, n)
    it = iter(scratch)
    take = lambda count: [next(it) for _ in range(count)]
    acc, rc, rx, ry1, ry2, rz1, rz2, fin, rf = (take(4) for _ in range(9))
    rgx, rge, tmp_in, tmp_en, back_in, back_en, rows_f = take(7)
    sg, st, rsg, rst, rsgz, rstz = take(6)
    ls, lin, cs, crv, xs, xr, ys, yr, zs, zr, fs, fr, ms, mr, ss, sr, os = take(17)
    source = ((ff, 0), (ff, D), (cr, 0), (se, 0))
    final = (f0, f1, f2, f3)
    step_rows = 64 if rl % 64 == 0 else rl
    parts = rl // step_rows

    def rows(j):
        return pl.ds(pl.multiple_of(j * step_rows, 8), step_rows)

    def half(g, mine):
        a = SHARE[g] // 2
        pos = d if mine else 1 - d
        return pl.ds(pl.multiple_of(pos * a, 128), a)

    def rest(g):
        return pl.ds(SHARE[g], D - SHARE[g])

    def slab(g, k):
        ref, start = source[g]
        return ref.at[k, :, :, pl.ds(start, D)]

    loads = [
        [pltpu.make_async_copy(slab(g, k), acc[g].at[i], ls.at[g, i]) for i, k in enumerate((n, yn))]
        for g in range(4)
    ]
    core = [
        [remote(slab(g, k), rc[g].at[i], cs.at[g, i], crv.at[g, i], pair) for i, k in enumerate((pn, 3 - n))]
        for g in range(4)
    ]
    for g in range(4):
        for copy in loads[g]:
            copy.start()
    out_local = pltpu.make_async_copy(outp.at[0], out_o.at[y], os.at[0])
    out_local.start()
    greet(wide)
    cross = [
        remote(gxp, rgx, ms.at[0], mr.at[0], pair),
        remote(gep, rge, ms.at[1], mr.at[1], pair),
        remote(outp.at[1], out_o.at[y], ms.at[2], mr.at[2], diag),
    ]
    out_got = remote(out_o.at[1 - y], out_o.at[1 - y], ms.at[2], mr.at[2], diag)
    for copy in cross:
        copy.start()
    for g in range(4):
        for copy in core[g]:
            copy.start()

    xcopy = [
        remote(acc[g].at[:, :, :, half(g, False)], rx[g], xs.at[g], xr.at[g], line_x) for g in range(4)
    ]
    y1 = [
        remote(acc[g].at[1, :, :, half(g, True)], ry1[g], ys.at[g, 0], yr.at[g, 0], line_y) for g in range(4)
    ]
    y2 = [remote(acc[g].at[1, :, :, rest(g)], ry2[g], ys.at[g, 1], yr.at[g, 1], line_y) for g in range(4)]

    def zcopy(g, path, k):
        row = lax.rem(w + k, wide)
        if path == 0:
            src, dst = acc[g].at[0, row, :, half(g, True)], rz1[g].at[w]
        else:
            src, dst = acc[g].at[0, row, :, rest(g)], rz2[g].at[w]
        return remote(src, dst, zs.at[g, path, k], zr.at[g, path, w], (d, row, n))

    def zgot(g, path, row):
        ref = (rz1, rz2)[path][g].at[row]
        return remote(ref, ref, zs.at[g, path, 0], zr.at[g, path, row], line_x)

    x1 = [
        remote(fin[g].at[:, half(g, True)], fin[g].at[:, half(g, True)], fs.at[g, 0], fr.at[g, 0], line_x)
        for g in range(4)
    ]
    x1_got = [
        remote(fin[g].at[:, half(g, False)], fin[g].at[:, half(g, False)], fs.at[g, 0], fr.at[g, 0], line_x)
        for g in range(4)
    ]
    x2 = [remote(fin[g].at[:, rest(g)], rf[g], fs.at[g, 1], fr.at[g, 1], line_x) for g in range(4)]

    lins = [
        pltpu.make_async_copy(geo, tmp_en, lin.at[0]),
    ]
    for copy in lins:
        copy.start()
    sg[...] = jnp.zeros((8, D), f32)
    sg[1:2, :] = gcross[...]
    sg[2:3, :] = gfeed[...]
    st[...] = tg[...]

    def core_step(g):
        for i in range(2):
            loads[g][i].wait()
            core[g][i].wait_recv()

        def add(k):
            for i in range(2):
                for j in range(parts):
                    r = rows(j)
                    acc[g][i, k, r, :] = (acc[g][i, k, r, :].astype(f32) + rc[g][i, k, r, :].astype(f32)).astype(bf16)

        loop(0, wide, add)
        xcopy[g].start()
        y2[g].start()

    def x_step(g):
        xcopy[g].wait_recv()
        c = half(g, True)

        def add(k):
            for i in range(2):
                for j in range(parts):
                    r = rows(j)
                    acc[g][i, k, r, c] = (acc[g][i, k, r, c].astype(f32) + rx[g][i, k, r, :].astype(f32)).astype(bf16)

        loop(0, wide, add)
        y1[g].start()

    def y_step(g, path):
        (y1, y2)[path][g].wait_recv()
        c = half(g, True) if path == 0 else rest(g)
        ry = (ry1, ry2)[path][g]

        def add(k):
            for j in range(parts):
                r = rows(j)
                acc[g][0, k, r, c] = (acc[g][0, k, r, c].astype(f32) + ry[k, r, :].astype(f32)).astype(bf16)

        loop(0, wide, add)
        loop(1, wide, lambda k: zcopy(g, path, k).start())

    def z_step(g, path):
        loop(1, wide, lambda k: zgot(g, path, lax.rem(w + k, wide)).wait_recv())
        c = half(g, True) if path == 0 else rest(g)
        rz = (rz1, rz2)[path][g]
        for j in range(parts):
            r = rows(j)

            def add(k, total):
                return total + rz[lax.rem(w + k, wide), r, :].astype(f32)

            total = lax.fori_loop(1, wide, add, acc[g][0, w, r, c].astype(f32))
            fin[g][r, c] = total.astype(bf16)
        (x1, x2)[path][g].start()

    def last_step(g):
        x1_got[g].wait_recv()
        x2[g].wait_recv()
        for j in range(parts):
            r = rows(j)
            final[g][r, 0 : SHARE[g]] = fin[g][r, 0 : SHARE[g]].astype(f32)
            final[g][r, SHARE[g] :] = fin[g][r, SHARE[g] :].astype(f32) + rf[g][r, :].astype(f32)

    cross[0].wait_recv()
    own = (n, dn)
    for i in range(2):

        def back(r, i=i):
            x = xf[own[i], r, :].astype(f32)
            dx, gg = norm_back(x, gain[...], gxo[i, r, :] + rgx[i, r, :].astype(f32))
            total = d1[i, r, :] + dx
            sg[0:1, :] += gg
            if i == 0:
                rows_f[r, :] = total
            else:
                tmp_in[r, :] = total.astype(bf16)

        rows_loop(256, 64, back)
    in_local = pltpu.make_async_copy(rows_f, gin_o.at[y], os.at[1])
    in_local.start()
    in_send = remote(tmp_in, back_in, ms.at[3], mr.at[3], diag)
    in_send.start()
    cross[1].wait_recv()
    lins[0].wait()
    tmp_en[0] = tmp_en[0] + rge[0].astype(f32)
    en_bf = back_en.at[0]
    back_en[0] = (tmp_en[1] + rge[1].astype(f32)).astype(bf16)
    en_local = pltpu.make_async_copy(tmp_en.at[0], gen_o.at[y], os.at[2])
    en_local.start()
    en_send = remote(en_bf, back_en.at[1], ms.at[4], mr.at[4], diag)
    en_send.start()

    for g in range(4):
        core_step(g)

    for j, dev in enumerate((pair, line_y, line_x)):
        a = remote(sg, rsg.at[j], ss.at[0, j], sr.at[0, j], dev)
        b = remote(st, rst.at[j], ss.at[1, j], sr.at[1, j], dev)
        a.start()
        b.start()
        a.wait()
        b.wait()
        sg[...] += rsg[j]
        st[...] += rst[j]

    def small(k):
        dev = (d, lax.rem(w + k, wide), n)
        return (
            remote(sg, rsgz.at[w], ss.at[0, 3 + k], sr.at[0, 3 + w], dev),
            remote(st, rstz.at[w], ss.at[1, 3 + k], sr.at[1, 3 + w], dev),
        )

    def small_start(k):
        for copy in small(k):
            copy.start()

    loop(1, wide, small_start)
    rsgz[w] = sg[...]
    rstz[w] = st[...]

    for g in range(4):
        x_step(g)
        y_step(g, 1)
    for g in range(4):
        y_step(g, 0)
        z_step(g, 1)

    def small_wait(k):
        row = lax.rem(w + k, wide)
        for i, ref in enumerate((rsgz, rstz)):
            remote(ref.at[row], ref.at[row], ss.at[i, 3], sr.at[i, 3 + row], line_x).wait_recv()

    loop(1, wide, small_wait)
    sg_o[...] = lax.fori_loop(1, wide, lambda k, t: t + rsgz[k], rsgz[0])
    st_o[...] = lax.fori_loop(1, wide, lambda k, t: t + rstz[k], rstz[0])

    in_send.wait_recv()
    in_local.wait()

    def widen(r):
        rows_f[r, :] = back_in[r, :].astype(f32)

    rows_loop(256, 64, widen)
    in_last = pltpu.make_async_copy(rows_f, gin_o.at[1 - y], os.at[3])
    in_last.start()
    en_send.wait_recv()
    tmp_en[1] = back_en[1].astype(f32)
    en_last = pltpu.make_async_copy(tmp_en.at[1], gen_o.at[1 - y], os.at[4])
    en_last.start()
    out_got.wait_recv()
    for g in range(4):
        z_step(g, 0)
    for g in range(4):
        last_step(g)

    for copy in (out_local, en_local, in_last, en_last):
        copy.wait()
    for copy in (*cross, in_send, en_send):
        copy.wait_send()
    for g in range(4):
        for copy in (*core[g], xcopy[g], y1[g], y2[g], x1[g], x2[g]):
            copy.wait_send()

    def finish(k):
        for g in range(4):
            for path in range(2):
                zcopy(g, path, k).wait_send()
        for copy in small(k):
            copy.wait_send()

    loop(1, wide, finish)


def reduce_all(wide, ff, cr, se, outp, gxo, gxp, geo, gep, xf, d1, gain, gfeed, gcross, tg):
    rl = D // wide
    ff, cr, se = (g.reshape(4, wide, rl, g.shape[-1]) for g in (ff, cr, se))
    sem = pltpu.SemaphoreType.DMA
    V = pl.BlockSpec(memory_space=pltpu.VMEM)
    each = lambda shape: [pltpu.VMEM(shape(SHARE[g] // 2, D - SHARE[g]), bf16) for g in range(4)]
    return pl.pallas_call(
        partial(reduce_kernel, wide, rl),
        in_specs=[ANY, ANY, ANY, ANY, V, ANY, ANY, ANY, V, V, V, V, V, V],
        out_specs=[ANY, ANY, ANY, V, V, V, V, V, V],
        out_shape=[
            out((2, 256, D), bf16),
            out((2, 256, D), f32),
            out((2, 128, D), f32),
            out((8, D), f32),
            out((32, 128), f32),
        ]
        + [out((rl, D), f32)] * 4,
        scratch_shapes=[
            *each(lambda a, b: (2, wide, rl, D)),
            *each(lambda a, b: (2, wide, rl, D)),
            *each(lambda a, b: (2, wide, rl, a)),
            *each(lambda a, b: (wide, rl, a)),
            *each(lambda a, b: (wide, rl, b)),
            *each(lambda a, b: (wide, rl, a)),
            *each(lambda a, b: (wide, rl, b)),
            *each(lambda a, b: (rl, D)),
            *each(lambda a, b: (rl, b)),
            pltpu.VMEM((2, 256, D), bf16),
            pltpu.VMEM((2, 128, D), bf16),
            pltpu.VMEM((256, D), bf16),
            pltpu.VMEM((2, 128, D), f32),
            pltpu.VMEM((256, D), bf16),
            pltpu.VMEM((2, 128, D), bf16),
            pltpu.VMEM((256, D), f32),
            pltpu.VMEM((8, D), f32),
            pltpu.VMEM((32, 128), f32),
            pltpu.VMEM((3, 8, D), f32),
            pltpu.VMEM((3, 32, 128), f32),
            pltpu.VMEM((wide, 8, D), f32),
            pltpu.VMEM((wide, 32, 128), f32),
            sem((4, 2)),
            sem((1,)),
            sem((4, 2)),
            sem((4, 2)),
            sem((4,)),
            sem((4,)),
            sem((4, 2)),
            sem((4, 2)),
            sem((4, 2, wide)),
            sem((4, 2, wide)),
            sem((4, 2)),
            sem((4, 2)),
            sem((5,)),
            sem((5,)),
            sem((2, 3 + wide)),
            sem((2, 3 + wide)),
            sem((5,)),
        ],
        compiler_params=pltpu.CompilerParams(
            collective_id=1, has_side_effects=True, vmem_limit_bytes=VMEM_LIMIT
        ),
        name="reduce_all",
    )(ff, cr, se, outp, gxo, gxp, geo, gep, xf, d1, gain, gfeed, gcross, tg)


def on_device(
    wide, hidden_in, encoder_out, cotangent, piece_starts, valid_lengths, bucket_table,
    gain_self, gain_cross, gain_feed, relative_bias, *mats
):
    me = lax.axis_index("narrow")
    micro = me // 2
    sq, sk, sv, so, cq, ck, cv, co, gate, up, down = mats
    ps = jnp.concatenate((sq, so, sk, sv), axis=1)
    pc = jnp.concatenate((cq, co, ck, cv), axis=1)
    pf = jnp.concatenate((gate, up, down), axis=1)
    tab = jnp.pad(relative_bias.T, ((0, 29), (0, 96)))
    xf, ef, cf, tabs, ws, wc, wf = gather(
        wide, hidden_in[:, 0], encoder_out[:, 0], cotangent[:, 0], tab, ps, pc, pf
    )
    ws, wc, wf = (g.reshape(4, D, g.shape[-1]) for g in (ws, wc, wf))
    xs, es, cs = xf.reshape(LEN, D), ef.reshape(ENC, D), cf.reshape(512, D)
    table = tabs[:, :3, :32].reshape(12, 32)
    one_hot = (bucket_table[:, None] == jnp.arange(BUCKETS)[None, :]).astype(f32)
    off = lax.dot_general(table, one_hot, (((1,), (1,)), ((), ())), precision=precise)
    off = jnp.pad(off, ((0, 0), (0, 1))).reshape(4, 3, 2048)
    info = jnp.stack([piece_starts[micro, 0], valid_lengths[micro, 0]])
    gains = [g.reshape(1, D) for g in (gain_self, gain_cross, gain_feed)]

    q, kv, at, p, h1 = self_forward(info, xs, ws, off, gains[0])
    cq, ckv, cat, cp, h2 = cross_forward(h1, es, wc, gains[1])
    gff, outp, d2, gg_feed = feed(h2, cs, wf, gains[2])
    gcr, d1, gg_cross, geo, gep = cross_backward(h1, es, d2, wc, gains[1], cq, ckv, cat, cp)
    gse, gxo, gxp, dl = self_backward(xs, d1, ws, gains[0], q, kv, at, p)

    doff = dl.reshape(12, TILES, 256)
    doff = jnp.pad(doff[:, :, :128], ((0, 0), (0, 1), (0, 0))) + jnp.pad(doff[:, :, 128:], ((0, 0), (1, 0), (0, 0)))
    doff = doff.reshape(12, (TILES + 1) * 128)
    tg = lax.dot_general(one_hot[: (TILES + 1) * 128], doff, (((0,), (1,)), ((), ())), precision=precise)
    tg = jnp.pad(tg, ((0, 0), (0, 116)))
    two = lambda a: a.reshape(2, -1, D)
    outs, gin, gen, sg, st, f0, f1, b, a = reduce_all(
        wide, gff, gcr, gse, two(outp), two(gxo), two(gxp), two(geo), two(gep), xf, two(d1), gains[0], gg_feed, gg_cross, tg
    )
    tg = lax.dynamic_slice_in_dim(st, me * 3, 3, axis=1)
    return (
        outs[:, None], gin[:, None], gen[:, None],
        sg[0], sg[1], sg[2], tg,
        a[:, :192], a[:, 384:576], a[:, 576:], a[:, 192:384],
        b[:, :192], b[:, 384:576], b[:, 576:], b[:, 192:384],
        f0[:, :512], jnp.concatenate([f0[:, 512:], f1[:, :256]], axis=1), f1[:, 256:],
    )


def solution(mesh):
    rows = P(None, ("dp", "wide"), "narrow", None)
    mat = P("wide", "narrow")
    return jax.shard_map(
        partial(on_device, mesh.shape["wide"]),
        mesh=mesh,
        in_specs=(rows, rows, rows, P(None, ("dp", "wide")), P(None, ("dp", "wide")), P(), P(), P(), P(), P(None, "narrow"))
        + (mat,) * 11,
        out_specs=(rows, rows, rows, P(), P(), P(), P(None, "narrow")) + (mat,) * 11,
        check_vma=False,
    )
```

```python
from functools import partial

import jax
import jax.numpy as jnp
from jax import lax
from jax.experimental import pallas as pl
from jax.experimental.pallas import tpu as pltpu
from jax.sharding import PartitionSpec as P

D = 768
HD = 192
HEADS = 12
DHEAD = 64
FFB = 512
BUCKETS = 32
LEN = 1024
ENC = 512
PIC = 256
TILES = 11
SPAN = 1280
ROWS = 16

precise = lax.Precision.HIGHEST
epsilon = 1e-06
masked_value = -1e30
f32 = jnp.float32
bf16 = jnp.bfloat16
MESH = pl.DeviceIdType.MESH
ANY = pl.BlockSpec(memory_space=pl.ANY)
VMEM_LIMIT = 60 << 20


def nn(a, b):
    return lax.dot_general(a, b, (((1,), (0,)), ((), ())), preferred_element_type=f32)


def nt(a, b):
    return lax.dot_general(a, b, (((1,), (1,)), ((), ())), preferred_element_type=f32)


def tn(a, b):
    return lax.dot_general(a, b, (((0,), (0,)), ((), ())), preferred_element_type=f32)


def rows_loop(total, step, body, unroll=1):
    def run(i, carry):
        body(pl.ds(pl.multiple_of(i * step, step), step))
        return carry

    lax.fori_loop(0, total // step, run, 0, unroll=unroll)


def normed(x, gain):
    factor = lax.rsqrt(jnp.mean(x * x, axis=1, keepdims=True) + epsilon)
    return x * factor * gain


def norm_back(x, gain, upstream):
    factor = lax.rsqrt(jnp.mean(x * x, axis=1, keepdims=True) + epsilon)
    weighted = upstream * gain
    inner = jnp.sum(weighted * x, axis=1, keepdims=True)
    dx = weighted * factor - x * (factor * factor * factor * inner * (1.0 / D))
    return dx, jnp.sum(upstream * x * factor, axis=0, keepdims=True)


def own_blocks():
    me = lax.axis_index("narrow")
    return (me, 3 - me)


def block_rows(blk):
    return pl.ds(pl.multiple_of(blk * 256, 256), 256)


def softmax_rows(v):
    e = jnp.exp(v - jnp.max(v, axis=1, keepdims=True))
    return e * (1.0 / jnp.sum(e, axis=1, keepdims=True))


def place_here():
    d, w, n = lax.axis_index("dp"), lax.axis_index("wide"), lax.axis_index("narrow")
    return d, w, n, n + 1 - 2 * lax.rem(n, 2), lax.rem(n + 2, 4), 3 - n


def remote(src, dst, send, recv, dev):
    return pltpu.make_async_remote_copy(
        src_ref=src, dst_ref=dst, send_sem=send, recv_sem=recv, device_id=dev, device_id_type=MESH
    )


def greet(devs, wide=1):
    d, w, n = place_here()[:3]
    barrier = pltpu.get_barrier_semaphore()
    for dev in devs:
        pl.semaphore_signal(barrier, inc=1, device_id=dev, device_id_type=MESH)

    def line(k, carry):
        dev = (d, lax.rem(w + k, wide), n)
        pl.semaphore_signal(barrier, inc=1, device_id=dev, device_id_type=MESH)
        return carry

    lax.fori_loop(1, wide, line, 0)
    pl.semaphore_wait(barrier, wide - 1 + len(devs))


def loop(lo, hi, body):
    def run(k, carry):
        body(k)
        return carry

    lax.fori_loop(lo, hi, run, 0)


def add_into(dst, src):
    shape = dst.shape
    rl = shape[-2]
    step = 64 if rl % 64 == 0 else rl
    lead = shape[:-2]

    def one(*index):
        for j in range(rl // step):
            spot = index + (slice(j * step, (j + 1) * step), slice(None))
            dst[spot] = dst[spot] + src[spot]

    if len(lead) == 1:
        loop(0, lead[0], one)
    else:
        for i in range(lead[0]):
            loop(0, lead[1], partial(one, i))


def sum_line(wide, own, parts, store):
    w = lax.axis_index("wide")
    rl = own.shape[0]
    step = 64 if rl % 64 == 0 else rl
    for j in range(rl // step):
        r = slice(j * step, (j + 1) * step)

        def add(k, total, r=r):
            return total + parts[lax.rem(w + k, wide), r, :].astype(f32)

        store(r, lax.fori_loop(1, wide, add, own[r, :].astype(f32)))


def core_devs():
    d, w, n, pn, yn, dn = place_here()
    return (d, w, pn)


class CoreSum:
    def __init__(self, step, buf, landed, send, recv):
        self.step, self.buf, self.landed, self.send, self.recv = step, buf, landed, send, recv
        self.side = step // 2

    def copy(self):
        return remote(
            self.buf.at[0], self.landed.at[self.side], self.send.at[0], self.recv.at[self.side], core_devs()
        )

    def finish(self, result):
        @pl.when(lax.rem(self.step, 2) == 0)
        def _():
            self.copy().start()

        @pl.when(lax.rem(self.step, 2) == 1)
        def _():
            self.copy().wait_recv()

            def add(r):
                result[0, r, :] = self.buf[1, r, :] + self.landed[self.side, r, :]

            rows_loop(D, 64, add)
            self.copy().wait_send()


def self_forward_kernel(
    info, xf, w, off, gain, q_o, kv_o, at_o, p_o, h1_o, nf, mask, tb, s
):
    n = pl.program_id(0)
    blks = own_blocks()

    @pl.when(n == 0)
    def _():
        def norm_rows(r):
            nf[r, :] = normed(xf[r, :].astype(f32), gain[...]).astype(bf16)

        rows_loop(LEN, 64, norm_rows)
        start, length = info[0], info[1]
        for i in range(2):
            h1_o[i * 256 : (i + 1) * 256, :] = xf[block_rows(blks[i]), :].astype(f32)

            def mask_rows(r, i=i):
                shape = (ROWS, LEN)
                qi = blks[i] * 256 + r.start + lax.broadcasted_iota(jnp.int32, shape, 0)
                kj = lax.broadcasted_iota(jnp.int32, shape, 1)
                inside = (qi >= start) & (qi < start + PIC) & (kj >= start) & (kj < start + PIC)
                allowed = ((kj <= qi) | inside) & (kj < length)
                mask[pl.ds(i * 256 + r.start, ROWS), :] = jnp.where(allowed, 0.0, masked_value)

            rows_loop(256, ROWS, mask_rows)

    kv_o[0] = nn(nf[...], w[0, :, 384:768]).astype(bf16).T
    for i in range(2):
        q_o[0, i * 256 : (i + 1) * 256, :] = nn(nf[block_rows(blks[i]), :], w[0, :, 0:192]).astype(bf16)
    for h in range(3):
        for t in range(TILES):
            line = jnp.broadcast_to(off[0, h : h + 1, 128 * t : 128 * t + 256], (128, 256))
            tb[t] = pltpu.roll(line, 129, 1, stride=1, stride_axis=0)[:, :128]
        hs = slice(h * DHEAD, (h + 1) * DHEAD)
        vs = slice(HD + h * DHEAD, HD + (h + 1) * DHEAD)
        for i in range(2):
            s[...] = nn(q_o[0, i * 256 : (i + 1) * 256, hs], kv_o[0, hs, :])
            for r in range(2):
                idx = [jnp.minimum(kb - 2 * blks[i] - r, 3) + 7 for kb in range(8)]

                def soft_rows(rr, i=i, r=r, h=h, idx=idx):
                    bias = jnp.concatenate([tb[idx[kb], rr, :] for kb in range(8)], axis=1)
                    v = s[pl.ds(r * 128 + rr.start, ROWS), :] + bias
                    v = v + mask[pl.ds(i * 256 + r * 128 + rr.start, ROWS), :]
                    p_o[0, h, pl.ds(i * 256 + r * 128 + rr.start, ROWS), :] = softmax_rows(v).astype(bf16)

                rows_loop(128, ROWS, soft_rows, unroll=8)
            at_o[0, i * 256 : (i + 1) * 256, hs] = nt(
                p_o[0, h, i * 256 : (i + 1) * 256, :], kv_o[0, vs, :]
            ).astype(bf16)
    h1_o[...] += nt(at_o[0], w[0, :, 192:384])


def whole(shape):
    zero = (0,) * len(shape)
    return pl.BlockSpec(shape, lambda n: zero)


def slab(shape):
    zero = (0,) * len(shape)
    return pl.BlockSpec((1,) + shape, lambda n: (n,) + zero)


def pair_slab(shape):
    zero = (0,) * len(shape)
    return pl.BlockSpec((1,) + shape, lambda n: (n // 2,) + zero)


def params(collective_id=None):
    if collective_id is None:
        return pltpu.CompilerParams(dimension_semantics=("arbitrary",), vmem_limit_bytes=VMEM_LIMIT)
    return pltpu.CompilerParams(
        dimension_semantics=("arbitrary",),
        vmem_limit_bytes=VMEM_LIMIT,
        collective_id=collective_id,
        has_side_effects=True,
    )


def out(shape, dtype):
    return jax.ShapeDtypeStruct(shape, dtype)


SMEM = pl.BlockSpec(memory_space=pltpu.SMEM)


def cost(gflop):
    return pl.CostEstimate(flops=int(gflop * 1e9), bytes_accessed=20 << 20, transcendentals=0)


def self_forward(info, xf, w, off, gain):
    return pl.pallas_call(
        self_forward_kernel,
        grid=(4,),
        in_specs=[SMEM, whole((LEN, D)), slab((D, D)), slab((3, 2048)), whole((1, D))],
        out_specs=[slab((512, HD)), slab((2 * HD, LEN)), slab((512, HD)), slab((3, 512, LEN)), whole((512, D))],
        out_shape=[
            out((4, 512, HD), bf16),
            out((4, 2 * HD, LEN), bf16),
            out((4, 512, HD), bf16),
            out((4, 3, 512, LEN), bf16),
            out((512, D), f32),
        ],
        scratch_shapes=[
            pltpu.VMEM((LEN, D), bf16),
            pltpu.VMEM((512, LEN), f32),
            pltpu.VMEM((TILES, 128, 128), f32),
            pltpu.VMEM((256, LEN), f32),
        ],
        compiler_params=params(),
        cost_estimate=cost(20),
        name="self_forward",
    )(info, xf, w, off, gain)


def cross_forward_kernel(h1, ef, w, gain, q_o, kv_o, at_o, p_o, h2_o, nc, s):
    n = pl.program_id(0)

    @pl.when(n == 0)
    def _():
        def norm_rows(r):
            x = h1[r, :]
            nc[r, :] = normed(x, gain[...]).astype(bf16)
            h2_o[r, :] = x

        rows_loop(512, 64, norm_rows)

    kv_o[0] = nn(ef[...], w[0, :, 384:768]).astype(bf16).T
    q_o[0] = nn(nc[...], w[0, :, 0:192]).astype(bf16)
    for h in range(3):
        hs = slice(h * DHEAD, (h + 1) * DHEAD)
        vs = slice(HD + h * DHEAD, HD + (h + 1) * DHEAD)
        s[...] = nn(q_o[0, :, hs], kv_o[0, hs, :])

        def soft_rows(r, h=h):
            p_o[0, h, r, :] = softmax_rows(s[r, :]).astype(bf16)

        rows_loop(512, 16, soft_rows, unroll=32)
        at_o[0, :, hs] = nt(p_o[0, h], kv_o[0, vs, :]).astype(bf16)
    h2_o[...] += nt(at_o[0], w[0, :, 192:384])


def cross_forward(h1, ef, w, gain):
    return pl.pallas_call(
        cross_forward_kernel,
        grid=(4,),
        in_specs=[whole((512, D)), whole((ENC, D)), slab((D, D)), whole((1, D))],
        out_specs=[slab((512, HD)), slab((2 * HD, ENC)), slab((512, HD)), slab((3, 512, ENC)), whole((512, D))],
        out_shape=[
            out((4, 512, HD), bf16),
            out((4, 2 * HD, ENC), bf16),
            out((4, 512, HD), bf16),
            out((4, 3, 512, ENC), bf16),
            out((512, D), f32),
        ],
        scratch_shapes=[pltpu.VMEM((512, D), bf16), pltpu.VMEM((512, ENC), f32)],
        compiler_params=params(),
        cost_estimate=cost(10),
        name="cross_forward",
    )(h1, ef, w, gain)


GELU_A = 0.7978845608028654
GELU_B = 0.044715


def feed_kernel(
    h2, cf, w, gain, gw_o, out_o, d2_o, gg_o, nf, nft, ct, gu, da, act, dgu, acc, buf, landed, send, recv
):
    n = pl.program_id(0)
    slot = lax.rem(n, 2)
    core = CoreSum(n, buf, landed, send, recv)

    @pl.when(n == 0)
    def _():
        def norm_rows(r):
            x = h2[r, :]
            nf[r, :] = normed(x, gain[...]).astype(bf16)
            acc[r, :] = x
            d2_o[r, :] = jnp.zeros((64, D), f32)

        greet((core_devs(),))
        rows_loop(512, 64, norm_rows)
        nft[...] = nf[...].T
        ct[...] = cf[...].T

    gu[...] = nn(nf[...], w[0, :, : 2 * FFB])
    da[...] = nn(cf[...], w[0, :, 2 * FFB :])

    def gelu_rows(r):
        gate = gu[r, :FFB]
        up = gu[r, FFB:]
        d_act = da[r, :]
        sq = gate * gate
        th = jnp.tanh(GELU_A * gate * (1.0 + GELU_B * sq))
        half = 0.5 + 0.5 * th
        gelu = gate * half
        slope = half + 0.5 * GELU_A * gate * (1.0 - th * th) * (1.0 + 3.0 * GELU_B * sq)
        act[r, :] = (gelu * up).astype(bf16)
        dgu[r, :FFB] = (d_act * up * slope).astype(bf16)
        dgu[r, FFB:] = (d_act * gelu).astype(bf16)

    rows_loop(512, 16, gelu_rows, unroll=32)
    acc[...] += nt(act[...], w[0, :, 2 * FFB :])
    buf[slot, :, : 2 * FFB] = nn(nft[...], dgu[...]).astype(bf16)
    buf[slot, :, 2 * FFB :] = nn(ct[...], act[...]).astype(bf16)
    d2_o[...] += nt(dgu[...], w[0, :, : 2 * FFB])
    core.finish(gw_o)

    @pl.when(n == 3)
    def _():
        gg_o[...] = jnp.zeros((1, D), f32)

        def back_rows(r):
            dx, gg = norm_back(h2[r, :], gain[...], d2_o[r, :])
            d2_o[r, :] = cf[r, :].astype(f32) + dx
            gg_o[...] += gg
            out_o[r, :] = acc[r, :].astype(bf16)

        rows_loop(512, 64, back_rows)


def feed(h2, cf, w, gain):
    return pl.pallas_call(
        feed_kernel,
        grid=(4,),
        in_specs=[whole((512, D)), whole((512, D)), slab((D, 3 * FFB)), whole((1, D))],
        out_specs=[pair_slab((D, 3 * FFB)), whole((512, D)), whole((512, D)), whole((1, D))],
        out_shape=[out((2, D, 3 * FFB), bf16), out((512, D), bf16), out((512, D), f32), out((1, D), f32)],
        scratch_shapes=[
            pltpu.VMEM((512, D), bf16),
            pltpu.VMEM((D, 512), bf16),
            pltpu.VMEM((D, 512), bf16),
            pltpu.VMEM((512, 2 * FFB), f32),
            pltpu.VMEM((512, FFB), f32),
            pltpu.VMEM((512, FFB), bf16),
            pltpu.VMEM((512, 2 * FFB), bf16),
            pltpu.VMEM((512, D), f32),
            pltpu.VMEM((2, D, 3 * FFB), bf16),
            pltpu.VMEM((2, D, 3 * FFB), bf16),
            pltpu.SemaphoreType.DMA((1,)),
            pltpu.SemaphoreType.DMA((2,)),
        ],
        compiler_params=params(2),
        cost_estimate=cost(30),
        name="feed",
    )(h2, cf, w, gain)


def cross_backward_kernel(
    h1, ef, d2, w, gain, q, kv, at, p, gff,
    gw_o, d1_o, gg_o, ge_o, gep_o, o1, o2,
    d2b, d2t, nct, eft, get, do, dp, ds, dq, dkv, buf, landed, rx, ry, send, recv, load, fs, fr,
):
    n = pl.program_id(0)
    slot = lax.rem(n, 2)
    core = CoreSum(n, buf, landed, send, recv)
    d, wi, me, pn, yn, dn = place_here()
    y = me // 2
    mine = pl.ds(pl.multiple_of(d * 384, 128), 384)
    other = pl.ds(pl.multiple_of(384 - d * 384, 128), 384)
    late = pl.ds(D, D)
    loads = [
        pltpu.make_async_copy(gff.at[:, :, :, mine], o1, load.at[0]),
        pltpu.make_async_copy(gff.at[y, :, :, late], o2, load.at[1]),
    ]
    sends = [
        remote(gff.at[:, :, :, other], rx, fs.at[0], fr.at[0], (1 - d, wi, me)),
        remote(gff.at[1 - y, :, :, late], ry, fs.at[1], fr.at[1], (d, wi, yn)),
    ]

    @pl.when(n == 0)
    def _():
        def norm_rows(r):
            d2b[r, :] = d2[r, :].astype(bf16)
            d1_o[r, :] = jnp.zeros((64, D), f32)
            dp[r, :] = normed(h1[r, :], gain[...])

        for copy in loads:
            copy.start()
        greet(((d, wi, pn), (d, wi, yn), (1 - d, wi, me)))
        for copy in sends:
            copy.start()
        rows_loop(512, 64, norm_rows)
        nct[...] = dp[...].astype(bf16).T
        d2t[...] = d2b[...].T
        eft[...] = ef[...].T
        get[...] = jnp.zeros((D, ENC), f32)

    do[...] = nn(d2b[...], w[0, :, 192:384]).astype(bf16)
    for h in range(3):
        hs = slice(h * DHEAD, (h + 1) * DHEAD)
        vs = slice(HD + h * DHEAD, HD + (h + 1) * DHEAD)
        dp[:, :ENC] = nn(do[:, hs], kv[0, vs, :])

        def grad_rows(r, h=h, hs=hs):
            delta = jnp.sum(do[r, hs].astype(f32) * at[0, r, hs].astype(f32), axis=1, keepdims=True)
            ds[r, :] = (p[0, h, r, :].astype(f32) * (dp[r, :ENC] - delta)).astype(bf16)

        rows_loop(512, 16, grad_rows, unroll=32)
        dq[:, hs] = nt(ds[...], kv[0, hs, :]).astype(bf16)
        dkv[hs, :] = tn(q[0, :, hs], ds[...]).astype(bf16)
        dkv[vs, :] = tn(do[:, hs], p[0, h]).astype(bf16)
    d1_o[...] += nt(dq[...], w[0, :, 0:192])
    get[...] += nn(w[0, :, 384:768], dkv[...])
    buf[slot, :, 0:384] = jnp.concatenate([nn(nct[...], dq[...]), nn(d2t[...], at[0])], axis=1).astype(bf16)
    buf[slot, :, 384:768] = nt(eft[...], dkv[...]).astype(bf16)
    core.finish(gw_o)

    @pl.when(n == 3)
    def _():
        gg_o[...] = jnp.zeros((1, D), f32)

        def back_rows(r):
            dx, gg = norm_back(h1[r, :], gain[...], d1_o[r, :])
            d1_o[r, :] = d2[r, :] + dx
            gg_o[...] += gg

        rows_loop(512, 64, back_rows)
        for i in range(2):
            half = slice(i * 128, (i + 1) * 128)
            cols = lambda blk: pl.ds(pl.multiple_of(blk * 128, 128), 128)
            ge_o[half, :] = get[:, cols((me, 3 - me)[i])].T
            gep_o[half, :] = get[:, cols((pn, 3 - pn)[i])].T.astype(bf16)
        for copy in loads:
            copy.wait()
        for copy in sends:
            copy.wait()
        add_into(o1, rx)
        add_into(o2, ry)


def cross_backward(wide, h1, ef, d2, w, gain, q, kv, at, p, gff):
    rl = D // wide
    return pl.pallas_call(
        cross_backward_kernel,
        grid=(4,),
        in_specs=[
            whole((512, D)),
            whole((ENC, D)),
            whole((512, D)),
            slab((D, D)),
            whole((1, D)),
            slab((512, HD)),
            slab((2 * HD, ENC)),
            slab((512, HD)),
            slab((3, 512, ENC)),
            ANY,
        ],
        out_specs=[
            pair_slab((D, D)),
            whole((512, D)),
            whole((1, D)),
            whole((256, D)),
            whole((256, D)),
            whole((2, wide, rl, 384)),
            whole((wide, rl, D)),
        ],
        out_shape=[
            out((2, D, D), bf16),
            out((512, D), f32),
            out((1, D), f32),
            out((256, D), f32),
            out((256, D), bf16),
            out((2, wide, rl, 384), bf16),
            out((wide, rl, D), bf16),
        ],
        scratch_shapes=[
            pltpu.VMEM((512, D), bf16),
            pltpu.VMEM((D, 512), bf16),
            pltpu.VMEM((D, 512), bf16),
            pltpu.VMEM((D, ENC), bf16),
            pltpu.VMEM((D, ENC), f32),
            pltpu.VMEM((512, HD), bf16),
            pltpu.VMEM((512, D), f32),
            pltpu.VMEM((512, ENC), bf16),
            pltpu.VMEM((512, HD), bf16),
            pltpu.VMEM((2 * HD, ENC), bf16),
            pltpu.VMEM((2, D, D), bf16),
            pltpu.VMEM((2, D, D), bf16),
            pltpu.VMEM((2, wide, rl, 384), bf16),
            pltpu.VMEM((wide, rl, D), bf16),
            pltpu.SemaphoreType.DMA((1,)),
            pltpu.SemaphoreType.DMA((2,)),
            pltpu.SemaphoreType.DMA((2,)),
            pltpu.SemaphoreType.DMA((2,)),
            pltpu.SemaphoreType.DMA((2,)),
        ],
        compiler_params=params(3),
        cost_estimate=cost(14),
        name="cross_backward",
    )(h1, ef, d2, w, gain, q, kv, at, p, gff.reshape(2, wide, rl, 3 * FFB))


def self_backward_kernel(
    wide, xf, d1, w, gain, q, kv, at, p, gcr, o1, o2,
    gw_o, g_o, gp_o, dl_o, c1, c2, e1, e2,
    d1b, d1t, nft, nqt, gt, gq, do, dp, ds, dq, dkv, buf, landed, s1, f2, rx, ry, ry1, rz1, rz2,
    send, recv, load, fs, fr, zs, zr,
):
    n = pl.program_id(0)
    blks = own_blocks()
    slot = lax.rem(n, 2)
    core = CoreSum(n, buf, landed, send, recv)
    d, wi, me, pn, yn, dn = place_here()
    y = me // 2
    mine = pl.ds(pl.multiple_of(d * 256, 128), 256)
    other = pl.ds(pl.multiple_of(256 - d * 256, 128), 256)
    late = pl.ds(512, 256)
    loads = [
        pltpu.make_async_copy(gcr.at[:, :, :, mine], c1, load.at[0]),
        pltpu.make_async_copy(gcr.at[y, :, :, late], c2, load.at[1]),
        pltpu.make_async_copy(o1.at[y], s1, load.at[2]),
        pltpu.make_async_copy(o2.at[wi], f2, load.at[3]),
    ]
    sends = [
        remote(o1.at[1 - y], ry1, fs.at[0], fr.at[0], (d, wi, yn)),
        remote(gcr.at[:, :, :, other], rx, fs.at[1], fr.at[1], (1 - d, wi, me)),
        remote(gcr.at[1 - y, :, :, late], ry, fs.at[2], fr.at[2], (d, wi, yn)),
    ]

    def zcopy(path, k):
        row = lax.rem(wi + k, wide)
        src, dst = ((s1, rz1), (o2, rz2))[path]
        return remote(src.at[row], dst.at[wi], zs.at[path, k], zr.at[path, wi], (d, row, me))

    def zgot(path, k):
        row = lax.rem(wi + k, wide)
        ref = (rz1, rz2)[path].at[row]
        return remote(ref, ref, zs.at[path, k], zr.at[path, row], (d, row, me))

    @pl.when(n == 0)
    def _():
        def cast_rows(r):
            d1b[r, :] = d1[r, :].astype(bf16)
            gq[r, :] = jnp.zeros((64, D), f32)

        for copy in loads:
            copy.start()
        greet(((d, wi, pn), (d, wi, yn), (1 - d, wi, me)), wide)
        for copy in sends:
            copy.start()
        loop(1, wide, lambda k: zcopy(1, k).start())
        rows_loop(512, 64, cast_rows)
        d1t[...] = d1b[...].T
        for i in range(4):
            part = normed(xf[i * 256 : (i + 1) * 256, :].astype(f32), gain[...]).astype(bf16)
            nft[:, i * 256 : (i + 1) * 256] = part.T
        for i in range(2):
            part = normed(xf[block_rows(blks[i]), :].astype(f32), gain[...]).astype(bf16)
            nqt[:, i * 256 : (i + 1) * 256] = part.T
        gt[...] = jnp.zeros((D, LEN), f32)

    @pl.when(n == 2)
    def _():
        loads[2].wait()
        sends[0].wait_recv()
        add_into(s1, ry1)
        loop(1, wide, lambda k: zcopy(0, k).start())

    dl_o[0] = jnp.zeros((3, 2048), f32)
    do[...] = nn(d1b[...], w[0, :, 192:384]).astype(bf16)
    for h in range(3):
        hs = slice(h * DHEAD, (h + 1) * DHEAD)
        vs = slice(HD + h * DHEAD, HD + (h + 1) * DHEAD)
        dk = jnp.zeros((DHEAD, LEN), f32)
        dv = jnp.zeros((DHEAD, LEN), f32)
        for i in range(2):
            half = slice(i * 256, (i + 1) * 256)
            dp[...] = nn(do[half, hs], kv[0, vs, :])

            def grad_rows(rr, i=i, h=h, hs=hs):
                rows = pl.ds(i * 256 + rr.start, ROWS)
                delta = jnp.sum(do[rows, hs].astype(f32) * at[0, rows, hs].astype(f32), axis=1, keepdims=True)
                ds[rr, :] = (p[0, h, rows, :].astype(f32) * (dp[rr, :] - delta)).astype(bf16)

            rows_loop(256, ROWS, grad_rows, unroll=16)
            upper, lower = ds[:128, :].astype(f32), ds[128:, :].astype(f32)
            part = jnp.concatenate(
                [
                    upper[:, :896] + lower[:, 128:],
                    upper[:, 896:],
                    jnp.zeros((128, 128), f32),
                    lower[:, :128],
                ],
                axis=1,
            )
            height = 128
            while height > 1:
                height //= 2
                part = part[:height] + pltpu.roll(part[height:], SPAN - height, 1)
            where = pl.ds(pl.multiple_of(768 - 256 * blks[i], 128), SPAN)
            dl_o[0, h : h + 1, where] += pltpu.roll(part, 255, 1)
            dq[half, hs] = nt(ds[...], kv[0, hs, :]).astype(bf16)
            dk = dk + tn(q[0, half, hs], ds[...])
            dv = dv + tn(do[half, hs], p[0, h, half, :])
        dkv[hs, :] = dk.astype(bf16)
        dkv[vs, :] = dv.astype(bf16)
    gq[...] += nt(dq[...], w[0, :, 0:192])
    gt[...] += nn(w[0, :, 384:768], dkv[...])
    buf[slot, :, 0:384] = jnp.concatenate([nn(nqt[...], dq[...]), nn(d1t[...], at[0])], axis=1).astype(bf16)
    buf[slot, :, 384:768] = nt(nft[...], dkv[...]).astype(bf16)
    core.finish(gw_o)

    @pl.when(n == 3)
    def _():
        for i in range(2):
            half = slice(i * 256, (i + 1) * 256)
            g_o[half, :] = gq[half, :] + gt[:, block_rows(blks[i])].T
            gp_o[half, :] = gt[:, block_rows((pn, 3 - pn)[i])].T.astype(bf16)
        loads[0].wait()
        sends[1].wait_recv()
        add_into(c1, rx)
        loads[1].wait()
        sends[2].wait_recv()
        add_into(c2, ry)
        loads[3].wait()
        for path in (1, 0):
            loop(1, wide, lambda k, path=path: zgot(path, k).wait_recv())

        def put(ref):
            def store(r, total):
                ref[r, :] = total.astype(bf16)

            return store

        sum_line(wide, s1.at[wi], rz1, put(e1))
        sum_line(wide, f2, rz2, put(e2))
        for copy in sends:
            copy.wait_send()
        for path in (0, 1):
            loop(1, wide, lambda k, path=path: zcopy(path, k).wait_send())


def self_backward(wide, xf, d1, w, gain, q, kv, at, p, gcr, o1, o2):
    rl = D // wide
    return pl.pallas_call(
        partial(self_backward_kernel, wide),
        grid=(4,),
        in_specs=[
            whole((LEN, D)),
            whole((512, D)),
            slab((D, D)),
            whole((1, D)),
            slab((512, HD)),
            slab((2 * HD, LEN)),
            slab((512, HD)),
            slab((3, 512, LEN)),
            ANY,
            ANY,
            ANY,
        ],
        out_specs=[
            pair_slab((D, D)),
            whole((512, D)),
            whole((512, D)),
            slab((3, 2048)),
            whole((2, wide, rl, 256)),
            whole((wide, rl, 256)),
            whole((rl, 384)),
            whole((rl, D)),
        ],
        out_shape=[
            out((2, D, D), bf16),
            out((512, D), f32),
            out((512, D), bf16),
            out((4, 3, 2048), f32),
            out((2, wide, rl, 256), bf16),
            out((wide, rl, 256), bf16),
            out((rl, 384), bf16),
            out((rl, D), bf16),
        ],
        scratch_shapes=[
            pltpu.VMEM((512, D), bf16),
            pltpu.VMEM((D, 512), bf16),
            pltpu.VMEM((D, LEN), bf16),
            pltpu.VMEM((D, 512), bf16),
            pltpu.VMEM((D, LEN), f32),
            pltpu.VMEM((512, D), f32),
            pltpu.VMEM((512, HD), bf16),
            pltpu.VMEM((256, LEN), f32),
            pltpu.VMEM((256, LEN), bf16),
            pltpu.VMEM((512, HD), bf16),
            pltpu.VMEM((2 * HD, LEN), bf16),
            pltpu.VMEM((2, D, D), bf16),
            pltpu.VMEM((2, D, D), bf16),
            pltpu.VMEM((wide, rl, 384), bf16),
            pltpu.VMEM((rl, D), bf16),
            pltpu.VMEM((2, wide, rl, 256), bf16),
            pltpu.VMEM((wide, rl, 256), bf16),
            pltpu.VMEM((wide, rl, 384), bf16),
            pltpu.VMEM((wide, rl, 384), bf16),
            pltpu.VMEM((wide, rl, D), bf16),
            pltpu.SemaphoreType.DMA((1,)),
            pltpu.SemaphoreType.DMA((2,)),
            pltpu.SemaphoreType.DMA((4,)),
            pltpu.SemaphoreType.DMA((3,)),
            pltpu.SemaphoreType.DMA((3,)),
            pltpu.SemaphoreType.DMA((2, wide)),
            pltpu.SemaphoreType.DMA((2, wide)),
        ],
        compiler_params=params(4),
        cost_estimate=cost(25),
        name="self_backward",
    )(xf, d1, w, gain, q, kv, at, p, gcr.reshape(2, wide, rl, D), o1, o2)


def gather_kernel(
    wide, hid, enc, cot, tab, ps, pc, pf, xf, ef, cf, tabs, gs, gc, gf, ls, ins, inr, zs, zr, ys, yr, xs, xr, cs, cr
):
    d, w, n, pn, yn, dn = place_here()
    y = n // 2
    keep, give = (2 * y + 1, 3 - 2 * y), (2 * y, 2 - 2 * y)
    groups = ((ps, gs, 0, 768, True), (pc, gc, 0, 768, True), (pf, gf, 0, 512, True), (pf, gf, 512, 1024, False))

    def cols(s, which):
        start, width, split = groups[s][2:]
        if which == 2 or not split:
            return pl.ds(start, width)
        half = width // 2
        pos = d if which == 0 else 1 - d
        return pl.ds(pl.multiple_of(start + pos * half, 128), half)

    def own(s, which):
        return groups[s][0].at[:, cols(s, which)]

    def spot(s, slab, row, which):
        return groups[s][1].at[slab, row, :, cols(s, which)]

    def zcopy(s, k):
        return remote(own(s, 0), spot(s, keep[0], w, 0), zs.at[s, k], zr.at[s, w], (d, lax.rem(w + k, wide), n))

    def zgot(s, row):
        return remote(spot(s, keep[0], row, 0), spot(s, keep[0], row, 0), zs.at[s, 0], zr.at[s, row], (1 - d, w, n))

    def ycopy(s, row, src):
        return remote(src, spot(s, keep[0], row, 0), ys.at[s, row], yr.at[s, row], (d, w, yn))

    def ygot(s, row):
        return remote(spot(s, keep[1], row, 0), spot(s, keep[1], row, 0), ys.at[s, row], yr.at[s, row], (d, w, yn))

    def xcopy(s, side, row):
        ref = spot(s, keep[side], row, 0)
        return remote(ref, ref, xs.at[s, side, row], xr.at[s, side, row], (1 - d, w, n))

    def xgot(s, side, row):
        ref = spot(s, keep[side], row, 1)
        return remote(ref, ref, xs.at[s, side, row], xr.at[s, side, row], (1 - d, w, n))

    def ccopy(s, side, row, src=None):
        ref = spot(s, keep[side], row, 2)
        return remote(ref if src is None else src, spot(s, give[side], row, 2), cs.at[s, side, row], cr.at[s, side, row], (d, w, pn))

    def cgot(s, side, row):
        ref = spot(s, give[side], row, 2)
        return remote(ref, ref, cs.at[s, side, row], cr.at[s, side, row], (d, w, pn))

    local = [
        pltpu.make_async_copy(src, dst, ls.at[i])
        for i, (src, dst) in enumerate(
            (
                (ps, gs.at[keep[0], w]),
                (pc, gc.at[keep[0], w]),
                (pf, gf.at[keep[0], w]),
                (hid.at[y], xf.at[n]),
                (enc.at[y], ef.at[n]),
                (cot.at[y], cf.at[0]),
                (tab, tabs.at[keep[0]]),
            )
        )
    ]
    for copy in local:
        copy.start()
    diag, pair = (d, w, dn), (d, w, pn)
    greet((pair, (d, w, yn), diag, (1 - d, w, n)), wide)
    first = [
        remote(hid.at[1 - y], xf.at[n], ins.at[0], inr.at[0], diag),
        remote(enc.at[1 - y], ef.at[n], ins.at[1], inr.at[1], diag),
        remote(cot.at[1 - y], cf.at[1], ins.at[2], inr.at[2], diag),
        remote(tab, tabs.at[give[0]], ins.at[3], inr.at[3], pair),
        remote(tab, tabs.at[keep[0]], ins.at[4], inr.at[4], (d, w, yn)),
        remote(tab, tabs.at[give[0]], ins.at[5], inr.at[5], diag),
        remote(hid.at[y], xf.at[n], ins.at[6], inr.at[6], pair),
        remote(enc.at[y], ef.at[n], ins.at[7], inr.at[7], pair),
    ]
    got = [
        remote(xf.at[dn], xf.at[dn], ins.at[0], inr.at[0], diag),
        remote(ef.at[dn], ef.at[dn], ins.at[1], inr.at[1], diag),
        remote(cf.at[1], cf.at[1], ins.at[2], inr.at[2], diag),
        remote(tabs.at[give[0]], tabs.at[give[0]], ins.at[3], inr.at[3], pair),
        remote(tabs.at[keep[1]], tabs.at[keep[1]], ins.at[4], inr.at[4], (d, w, yn)),
        remote(tabs.at[give[1]], tabs.at[give[1]], ins.at[5], inr.at[5], diag),
        remote(xf.at[pn], xf.at[pn], ins.at[6], inr.at[6], pair),
        remote(ef.at[pn], ef.at[pn], ins.at[7], inr.at[7], pair),
        remote(xf.at[yn], xf.at[yn], ins.at[8], inr.at[8], pair),
        remote(ef.at[yn], ef.at[yn], ins.at[9], inr.at[9], pair),
    ]
    later = [
        remote(xf.at[dn], xf.at[dn], ins.at[8], inr.at[8], pair),
        remote(ef.at[dn], ef.at[dn], ins.at[9], inr.at[9], pair),
    ]
    for copy in first:
        copy.start()
    for s in range(4):
        loop(1, wide, lambda k, s=s: zcopy(s, k).start())
        ycopy(s, w, own(s, 0)).start()
        ccopy(s, 0, w, own(s, 2)).start()
    got[0].wait_recv()
    later[0].start()
    got[1].wait_recv()
    later[1].start()

    def zstep(s):
        def one(k):
            row = lax.rem(w + k, wide)
            zgot(s, row).wait_recv()
            ycopy(s, row, spot(s, keep[0], row, 0)).start()
            if groups[s][4]:
                xcopy(s, 0, row).start()
            else:
                ccopy(s, 0, row).start()

        loop(1, wide, one)

    def ystep(s):
        def one(k):
            row = lax.rem(w + k, wide)
            ygot(s, row).wait_recv()
            if groups[s][4]:
                xcopy(s, 1, row).start()
            else:
                ccopy(s, 1, row).start()

        loop(0, wide, one)

    def xstep(s):
        def one(side):
            def step(k):
                row = lax.rem(w + k, wide)
                xgot(s, side, row).wait_recv()
                ccopy(s, side, row).start()

            return step

        loop(1, wide, one(0))
        loop(0, wide, one(1))

    zstep(0)
    ystep(0)
    zstep(1)
    ystep(1)
    xstep(0)
    zstep(2)
    ystep(2)
    xstep(1)
    zstep(3)
    ystep(3)
    xstep(2)
    for copy in got[2:]:
        copy.wait_recv()
    for copy in local:
        copy.wait()
    for copy in first + later:
        copy.wait_send()

    def finish(k):
        row = lax.rem(w + k, wide)
        for s in range(4):
            for side in range(2):
                cgot(s, side, row).wait_recv()
                ccopy(s, side, row).wait_send()
            ycopy(s, row, spot(s, keep[0], row, 0)).wait_send()
            if groups[s][4]:
                xcopy(s, 1, row).wait_send()

    loop(0, wide, finish)

    def finish_line(k):
        row = lax.rem(w + k, wide)
        for s in range(4):
            zcopy(s, k).wait_send()
            if groups[s][4]:
                xcopy(s, 0, row).wait_send()

    loop(1, wide, finish_line)


def gather(wide, hid, enc, cot, tab, ps, pc, pf):
    rl = ps.shape[0]
    sem = pltpu.SemaphoreType.DMA
    return pl.pallas_call(
        partial(gather_kernel, wide),
        in_specs=[ANY] * 7,
        out_specs=[ANY] * 7,
        out_shape=[
            out((4, 256, D), bf16),
            out((4, 128, D), bf16),
            out((2, 256, D), bf16),
            out((4, 32, 128), f32),
            out((4, wide, rl, D), bf16),
            out((4, wide, rl, D), bf16),
            out((4, wide, rl, 2 * D), bf16),
        ],
        scratch_shapes=[
            sem((7,)),
            sem((10,)),
            sem((10,)),
            sem((4, wide)),
            sem((4, wide)),
            sem((4, wide)),
            sem((4, wide)),
            sem((4, 2, wide)),
            sem((4, 2, wide)),
            sem((4, 2, wide)),
            sem((4, 2, wide)),
        ],
        compiler_params=pltpu.CompilerParams(collective_id=0, has_side_effects=True),
        name="gather",
    )(hid, enc, cot, tab, ps, pc, pf)


def reduce_kernel(
    wide, se, c1, c2, e1, e2, outp, gxo, gxp, geo, gep, xf, d1, gain, gfeed, gcross, tg,
    out_o, gin_o, gen_o, sg_o, st_o, ff_o, cr_o, se_o,
    a1, a2, rx, ry, ry1, cy1, b1, rzs1, rzs2, rzc1, rzc2, fs, fc, xs1, xs2, xc1, xc2, x1, x2,
    rgx, rge, tmp_in, tmp_en, back_in, back_en, rows_f, sg, st, rsg, rst, rsgz, rstz,
    load, ms, mr, ts, tr, zs, zr, ss, sr, os,
):
    d, w, n, pn, yn, dn = place_here()
    y = n // 2
    pair, line_y, diag, line_x = (d, w, pn), (d, w, yn), (d, w, dn), (1 - d, w, n)
    mine = pl.ds(pl.multiple_of(d * 256, 128), 256)
    other = pl.ds(pl.multiple_of(256 - d * 256, 128), 256)
    late = pl.ds(512, 256)
    loads = [
        pltpu.make_async_copy(se.at[:, :, :, mine], a1, load.at[0]),
        pltpu.make_async_copy(se.at[y, :, :, late], a2, load.at[1]),
        pltpu.make_async_copy(c1.at[y], b1, load.at[2]),
        pltpu.make_async_copy(geo, tmp_en, load.at[3]),
        pltpu.make_async_copy(outp.at[0], out_o.at[y], load.at[4]),
    ]
    for copy in loads:
        copy.start()
    greet((pair, line_y, diag, line_x), wide)
    turn = lambda i, src, dst, dev: remote(src, dst, ts.at[i], tr.at[i], dev)
    put = [
        turn(0, se.at[:, :, :, other], rx, line_x),
        turn(1, c1.at[1 - y], cy1, line_y),
        turn(2, se.at[1 - y, :, :, late], ry, line_y),
        turn(3, e1, x1, line_x),
        turn(4, e2, x2, line_x),
    ]
    cross = [
        remote(gxp, rgx, ms.at[0], mr.at[0], pair),
        remote(gep, rge, ms.at[1], mr.at[1], pair),
        remote(outp.at[1], out_o.at[y], ms.at[2], mr.at[2], diag),
    ]
    out_got = remote(out_o.at[1 - y], out_o.at[1 - y], ms.at[2], mr.at[2], diag)
    z_refs = ((a1, rzs1), (a2, rzs2), (b1, rzc1), (c2, rzc2))

    def zcopy(path, k):
        row = lax.rem(w + k, wide)
        src, dst = z_refs[path]
        src = src.at[y, row] if path == 0 else src.at[row]
        return remote(src, dst.at[w], zs.at[path, k], zr.at[path, w], (d, row, n))

    def zgot(path, k):
        row = lax.rem(w + k, wide)
        ref = z_refs[path][1].at[row]
        return remote(ref, ref, zs.at[path, k], zr.at[path, row], (d, row, n))

    def zstart(path):
        loop(1, wide, lambda k: zcopy(path, k).start())

    def zwait(path):
        loop(1, wide, lambda k: zgot(path, k).wait_recv())

    cross[0].start()
    cross[1].start()
    put[0].start()
    put[1].start()
    put[2].start()
    zstart(3)
    cross[2].start()
    put[3].start()
    put[4].start()

    sg[...] = jnp.zeros((8, D), f32)
    sg[1:2, :] = gcross[...]
    sg[2:3, :] = gfeed[...]
    st[...] = tg[...]
    cross[0].wait_recv()
    own = (n, dn)
    for i in (1, 0):

        def back(r, i=i):
            x = xf[own[i], r, :].astype(f32)
            dx, gg = norm_back(x, gain[...], gxo[i, r, :] + rgx[i, r, :].astype(f32))
            total = d1[i, r, :] + dx
            sg[0:1, :] += gg
            if i == 0:
                rows_f[0, r, :] = total
            else:
                tmp_in[r, :] = total.astype(bf16)

        rows_loop(256, 32, back, unroll=2)
        if i == 1:
            in_send = remote(tmp_in, back_in, ms.at[3], mr.at[3], diag)
            in_send.start()
    in_local = pltpu.make_async_copy(rows_f.at[0], gin_o.at[y], os.at[0])
    in_local.start()
    cross[1].wait_recv()
    loads[3].wait()
    back_en[0] = (tmp_en[1] + rge[1].astype(f32)).astype(bf16)
    en_send = remote(back_en.at[0], back_en.at[1], ms.at[4], mr.at[4], diag)
    en_send.start()
    tmp_en[0] = tmp_en[0] + rge[0].astype(f32)
    en_local = pltpu.make_async_copy(tmp_en.at[0], gen_o.at[y], os.at[1])
    en_local.start()

    def small(j, dev):
        return (
            remote(sg, rsg.at[j], ss.at[0, j], sr.at[0, j], dev),
            remote(st, rst.at[j], ss.at[1, j], sr.at[1, j], dev),
        )

    def small_add(j, dev):
        for copy in small(j, dev):
            copy.wait()
        sg[...] += rsg[j]
        st[...] += rst[j]

    def small_line(k):
        dev = (d, lax.rem(w + k, wide), n)
        return (
            remote(sg, rsgz.at[w], ss.at[0, 3 + k], sr.at[0, 3 + w], dev),
            remote(st, rstz.at[w], ss.at[1, 3 + k], sr.at[1, 3 + w], dev),
        )

    def start_all(copies):
        for copy in copies:
            copy.start()

    start_all(small(0, pair))
    small_add(0, pair)
    start_all(small(1, line_y))

    loads[2].wait()
    put[1].wait_recv()
    add_into(b1, cy1)
    zstart(2)
    small_add(1, line_y)
    start_all(small(2, line_x))
    loads[1].wait()
    put[2].wait_recv()
    add_into(a2, ry)
    zstart(1)
    small_add(2, line_x)
    loop(1, wide, lambda k: start_all(small_line(k)))
    rsgz[w] = sg[...]
    rstz[w] = st[...]
    loads[0].wait()
    put[0].wait_recv()
    add_into(a1, rx)
    y1 = turn(5, a1.at[1 - y], ry1, line_y)
    y1.start()

    def keep(ref, cols):
        def store(r, total):
            ref[r, cols] = total.astype(bf16)

        return store

    everything = slice(None)
    zwait(3)
    sum_line(wide, c2.at[w], rzc2, keep(fc, late))
    f_c2 = turn(6, fc.at[:, late], xc2, line_x)
    f_c2.start()
    zwait(2)
    sum_line(wide, b1.at[w], rzc1, keep(fc, mine))
    f_c1 = turn(7, fc.at[:, mine], xc1, line_x)
    f_c1.start()
    y1.wait_recv()
    rl = e1.shape[0]

    def add_side(k):
        a1[y, k] = a1[y, k] + ry1[k]

    loop(0, wide, add_side)
    zstart(0)

    def small_wait(k):
        row = lax.rem(w + k, wide)
        for i, ref in enumerate((rsgz, rstz)):
            remote(ref.at[row], ref.at[row], ss.at[i, 3], sr.at[i, 3 + row], line_x).wait_recv()

    loop(1, wide, small_wait)
    sg_o[...] = lax.fori_loop(1, wide, lambda k, t: t + rsgz[k], rsgz[0])
    st_o[...] = lax.fori_loop(1, wide, lambda k, t: t + rstz[k], rstz[0])

    zwait(1)
    sum_line(wide, a2.at[w], rzs2, keep(fs, late))
    f_s2 = turn(8, fs.at[:, late], xs2, line_x)
    f_s2.start()

    in_send.wait_recv()

    def widen(r):
        rows_f[1, r, :] = back_in[r, :].astype(f32)

    rows_loop(256, 64, widen)
    in_last = pltpu.make_async_copy(rows_f.at[1], gin_o.at[1 - y], os.at[2])
    in_last.start()
    en_send.wait_recv()
    tmp_en[1] = back_en[1].astype(f32)
    en_last = pltpu.make_async_copy(tmp_en.at[1], gen_o.at[1 - y], os.at[3])
    en_last.start()

    f_mine = pl.ds(pl.multiple_of(d * 384, 128), 384)
    f_other = pl.ds(pl.multiple_of(384 - d * 384, 128), 384)
    put[3].wait_recv()
    put[4].wait_recv()
    ff_o[:, f_mine] = e1[...].astype(f32)
    ff_o[:, f_other] = x1[...].astype(f32)
    ff_o[:, pl.ds(D, D)] = e2[...].astype(f32) + x2[...].astype(f32)
    f_c1.wait_recv()
    f_c2.wait_recv()
    cr_o[:, mine] = fc[:, mine].astype(f32)
    cr_o[:, other] = xc1[...].astype(f32)
    cr_o[:, late] = fc[:, late].astype(f32) + xc2[...].astype(f32)
    zwait(0)
    sum_line(wide, a1.at[y, w], rzs1, keep(fs, mine))
    f_s1 = turn(9, fs.at[:, mine], xs1, line_x)
    f_s1.start()
    out_got.wait_recv()
    f_s2.wait_recv()
    se_o[:, mine] = fs[:, mine].astype(f32)
    se_o[:, late] = fs[:, late].astype(f32) + xs2[...].astype(f32)
    f_s1.wait_recv()
    se_o[:, other] = xs1[...].astype(f32)

    for copy in (in_local, en_local, in_last, en_last, loads[4]):
        copy.wait()
    for copy in (*cross, in_send, en_send, *put, y1, f_c1, f_c2, f_s1, f_s2):
        copy.wait_send()

    def finish(k):
        for path in range(4):
            zcopy(path, k).wait_send()
        for copy in small_line(k):
            copy.wait_send()

    loop(1, wide, finish)


def reduce_all(wide, se, c1, c2, e1, e2, outp, gxo, gxp, geo, gep, xf, d1, gain, gfeed, gcross, tg):
    rl = D // wide
    se = se.reshape(2, wide, rl, D)
    sem = pltpu.SemaphoreType.DMA
    V = pl.BlockSpec(memory_space=pltpu.VMEM)
    v = lambda *shape: pltpu.VMEM(shape, bf16)
    return pl.pallas_call(
        partial(reduce_kernel, wide),
        in_specs=[ANY, ANY, V, V, V, ANY, V, ANY, ANY, ANY, V, V, V, V, V, V],
        out_specs=[ANY, ANY, ANY, V, V, V, V, V],
        out_shape=[
            out((2, 256, D), bf16),
            out((2, 256, D), f32),
            out((2, 128, D), f32),
            out((8, D), f32),
            out((32, 128), f32),
            out((rl, 2 * D), f32),
            out((rl, D), f32),
            out((rl, D), f32),
        ],
        scratch_shapes=[
            v(2, wide, rl, 256),
            v(wide, rl, 256),
            v(2, wide, rl, 256),
            v(wide, rl, 256),
            v(wide, rl, 256),
            v(wide, rl, 256),
            v(wide, rl, 256),
            v(wide, rl, 256),
            v(wide, rl, 256),
            v(wide, rl, 256),
            v(wide, rl, 256),
            v(rl, D),
            v(rl, D),
            v(rl, 256),
            v(rl, 256),
            v(rl, 256),
            v(rl, 256),
            v(rl, 384),
            v(rl, D),
            v(2, 256, D),
            v(2, 128, D),
            v(256, D),
            pltpu.VMEM((2, 128, D), f32),
            v(256, D),
            v(2, 128, D),
            pltpu.VMEM((2, 256, D), f32),
            pltpu.VMEM((8, D), f32),
            pltpu.VMEM((32, 128), f32),
            pltpu.VMEM((3, 8, D), f32),
            pltpu.VMEM((3, 32, 128), f32),
            pltpu.VMEM((wide, 8, D), f32),
            pltpu.VMEM((wide, 32, 128), f32),
            sem((5,)),
            sem((5,)),
            sem((5,)),
            sem((10,)),
            sem((10,)),
            sem((4, wide)),
            sem((4, wide)),
            sem((2, 3 + wide)),
            sem((2, 3 + wide)),
            sem((4,)),
        ],
        compiler_params=pltpu.CompilerParams(
            collective_id=1, has_side_effects=True, vmem_limit_bytes=VMEM_LIMIT
        ),
        name="reduce_all",
    )(se, c1, c2, e1, e2, outp, gxo, gxp, geo, gep, xf, d1, gain, gfeed, gcross, tg)


def on_device(
    wide, hidden_in, encoder_out, cotangent, piece_starts, valid_lengths, bucket_table,
    gain_self, gain_cross, gain_feed, relative_bias, *mats
):
    me = lax.axis_index("narrow")
    micro = me // 2
    sq, sk, sv, so, cq, ck, cv, co, gate, up, down = mats
    ps = jnp.concatenate((sq, so, sk, sv), axis=1)
    pc = jnp.concatenate((cq, co, ck, cv), axis=1)
    pf = jnp.concatenate((gate, up, down), axis=1)
    tab = jnp.pad(relative_bias.T, ((0, 29), (0, 96)))
    xf, ef, cf, tabs, ws, wc, wf = gather(
        wide, hidden_in[:, 0], encoder_out[:, 0], cotangent[:, 0], tab, ps, pc, pf
    )
    ws, wc, wf = (g.reshape(4, D, g.shape[-1]) for g in (ws, wc, wf))
    xs, es, cs = xf.reshape(LEN, D), ef.reshape(ENC, D), cf.reshape(512, D)
    table = tabs[:, :3, :32].reshape(12, 32)
    one_hot = (bucket_table[:, None] == jnp.arange(BUCKETS)[None, :]).astype(f32)
    off = lax.dot_general(table, one_hot, (((1,), (1,)), ((), ())), precision=precise)
    off = jnp.pad(off, ((0, 0), (0, 1))).reshape(4, 3, 2048)
    info = jnp.stack([piece_starts[micro, 0], valid_lengths[micro, 0]])
    gains = [g.reshape(1, D) for g in (gain_self, gain_cross, gain_feed)]

    q, kv, at, p, h1 = self_forward(info, xs, ws, off, gains[0])
    cq, ckv, cat, cp, h2 = cross_forward(h1, es, wc, gains[1])
    gff, outp, d2, gg_feed = feed(h2, cs, wf, gains[2])
    gcr, d1, gg_cross, geo, gep, o1, o2 = cross_backward(wide, h1, es, d2, wc, gains[1], cq, ckv, cat, cp, gff)
    gse, gxo, gxp, dl, c1, c2, e1, e2 = self_backward(wide, xs, d1, ws, gains[0], q, kv, at, p, gcr, o1, o2)

    dl = jnp.where(me % 2 == 1, dl, dl.reshape(2, 2, 3, 2048)[:, ::-1].reshape(4, 3, 2048))
    doff = dl.reshape(12, 2048)[:, :2047]
    tg = lax.dot_general(one_hot, doff, (((0,), (1,)), ((), ())), precision=precise)
    tg = jnp.pad(tg, ((0, 0), (0, 116)))
    two = lambda a: a.reshape(2, -1, D)
    outs, gin, gen, sg, st, f, b, a = reduce_all(
        wide, gse, c1, c2, e1, e2, two(outp), two(gxo), two(gxp), two(geo), two(gep), xf, two(d1), gains[0], gg_feed, gg_cross, tg
    )
    tg = lax.dynamic_slice_in_dim(st, me * 3, 3, axis=1)
    return (
        outs[:, None], gin[:, None], gen[:, None],
        sg[0], sg[1], sg[2], tg,
        a[:, :192], a[:, 384:576], a[:, 576:], a[:, 192:384],
        b[:, :192], b[:, 384:576], b[:, 576:], b[:, 192:384],
        f[:, :512], f[:, 512:1024], f[:, 1024:],
    )


def solution(mesh):
    rows = P(None, ("dp", "wide"), "narrow", None)
    mat = P("wide", "narrow")
    return jax.shard_map(
        partial(on_device, mesh.shape["wide"]),
        mesh=mesh,
        in_specs=(rows, rows, rows, P(None, ("dp", "wide")), P(None, ("dp", "wide")), P(), P(), P(), P(), P(None, "narrow"))
        + (mat,) * 11,
        out_specs=(rows, rows, rows, P(), P(), P(), P(None, "narrow")) + (mat,) * 11,
        check_vma=False,
    )
```

```python
import math
from functools import partial

import jax
import jax.numpy as jnp
from jax import lax
from jax.experimental import pallas as pl
from jax.experimental.pallas import tpu as pltpu
from jax.sharding import PartitionSpec as P

D = 768
HD = 192
HEADS = 12
DHEAD = 64
FFB = 512
BUCKETS = 32
LEN = 1024
ENC = 512
PIC = 256
TILES = 11
SPAN = 1280
ROWS = 16

precise = lax.Precision.HIGHEST
epsilon = 1e-06
masked_value = -1e30
f32 = jnp.float32
bf16 = jnp.bfloat16
MESH = pl.DeviceIdType.MESH
ANY = pl.BlockSpec(memory_space=pl.ANY)
VMEM_LIMIT = 60 << 20


def nn(a, b):
    return lax.dot_general(a, b, (((1,), (0,)), ((), ())), preferred_element_type=f32)


def nt(a, b):
    return lax.dot_general(a, b, (((1,), (1,)), ((), ())), preferred_element_type=f32)


def tn(a, b):
    return lax.dot_general(a, b, (((0,), (0,)), ((), ())), preferred_element_type=f32)


def rows_loop(total, step, body, unroll=1):
    def run(i, carry):
        body(pl.ds(pl.multiple_of(i * step, step), step))
        return carry

    lax.fori_loop(0, total // step, run, 0, unroll=unroll)


def normed(x, gain):
    factor = lax.rsqrt(jnp.mean(x * x, axis=1, keepdims=True) + epsilon)
    return x * factor * gain


def norm_back(x, gain, upstream):
    factor = lax.rsqrt(jnp.mean(x * x, axis=1, keepdims=True) + epsilon)
    weighted = upstream * gain
    inner = jnp.sum(weighted * x, axis=1, keepdims=True)
    dx = weighted * factor - x * (factor * factor * factor * inner * (1.0 / D))
    return dx, jnp.sum(upstream * x * factor, axis=0, keepdims=True)


def own_blocks():
    me = lax.axis_index("narrow")
    return (me, 3 - me)


def block_rows(blk):
    return pl.ds(pl.multiple_of(blk * 256, 256), 256)


def softmax_rows(v):
    e = jnp.exp(v - jnp.max(v, axis=1, keepdims=True))
    return e * (1.0 / jnp.sum(e, axis=1, keepdims=True))


def place_here():
    d, w, n = lax.axis_index("dp"), lax.axis_index("wide"), lax.axis_index("narrow")
    return d, w, n, n + 1 - 2 * lax.rem(n, 2), lax.rem(n + 2, 4), 3 - n


def remote(src, dst, send, recv, dev):
    return pltpu.make_async_remote_copy(
        src_ref=src, dst_ref=dst, send_sem=send, recv_sem=recv, device_id=dev, device_id_type=MESH
    )


def greet(devs, wide=1):
    d, w, n = place_here()[:3]
    barrier = pltpu.get_barrier_semaphore()
    for dev in devs:
        pl.semaphore_signal(barrier, inc=1, device_id=dev, device_id_type=MESH)

    def line(k, carry):
        dev = (d, lax.rem(w + k, wide), n)
        pl.semaphore_signal(barrier, inc=1, device_id=dev, device_id_type=MESH)
        return carry

    lax.fori_loop(1, wide, line, 0)
    pl.semaphore_wait(barrier, wide - 1 + len(devs))


def loop(lo, hi, body):
    def run(k, carry):
        body(k)
        return carry

    lax.fori_loop(lo, hi, run, 0)


def add_into(dst, src):
    shape = dst.shape
    rl = shape[-2]
    step = 64 if rl % 64 == 0 else rl
    lead = shape[:-2]

    def one(*index):
        for j in range(rl // step):
            spot = index + (slice(j * step, (j + 1) * step), slice(None))
            dst[spot] = dst[spot] + src[spot]

    if len(lead) == 1:
        loop(0, lead[0], one)
    else:
        for i in range(lead[0]):
            loop(0, lead[1], partial(one, i))


def sum_line(wide, own, parts, store):
    w = lax.axis_index("wide")
    rl = own.shape[0]
    step = 64 if rl % 64 == 0 else rl
    for j in range(rl // step):
        r = slice(j * step, (j + 1) * step)

        def add(k, total, r=r):
            return total + parts[lax.rem(w + k, wide), r, :].astype(f32)

        store(r, lax.fori_loop(1, wide, add, own[r, :].astype(f32)))


def core_devs():
    d, w, n, pn, yn, dn = place_here()
    return (d, w, pn)


class CoreSum:
    def __init__(self, step, buf, landed, send, recv):
        self.step, self.buf, self.landed, self.send, self.recv = step, buf, landed, send, recv
        self.side = step // 2

    def copy(self):
        return remote(
            self.buf.at[0], self.landed.at[self.side], self.send.at[0], self.recv.at[self.side], core_devs()
        )

    def finish(self, result):
        @pl.when(lax.rem(self.step, 2) == 0)
        def _():
            self.copy().start()

        @pl.when(lax.rem(self.step, 2) == 1)
        def _():
            self.copy().wait_recv()

            def add(r):
                result[0, r, :] = self.buf[1, r, :] + self.landed[self.side, r, :]

            rows_loop(D, 64, add)
            self.copy().wait_send()


def whole(shape):
    zero = (0,) * len(shape)
    return pl.BlockSpec(shape, lambda n: zero)


def slab(shape):
    zero = (0,) * len(shape)
    return pl.BlockSpec((1,) + shape, lambda n: (n,) + zero)


def pair_slab(shape):
    zero = (0,) * len(shape)
    return pl.BlockSpec((1,) + shape, lambda n: (n // 2,) + zero)


def params(collective_id=None):
    if collective_id is None:
        return pltpu.CompilerParams(dimension_semantics=("arbitrary",), vmem_limit_bytes=VMEM_LIMIT)
    return pltpu.CompilerParams(
        dimension_semantics=("arbitrary",),
        vmem_limit_bytes=VMEM_LIMIT,
        collective_id=collective_id,
        has_side_effects=True,
    )


def out(shape, dtype):
    return jax.ShapeDtypeStruct(shape, dtype)


SMEM = pl.BlockSpec(memory_space=pltpu.SMEM)


def cost(gflop):
    return pl.CostEstimate(flops=int(gflop * 1e9), bytes_accessed=20 << 20, transcendentals=0)


GELU_A = 0.7978845608028654
GELU_B = 0.044715


FORWARD_VMEM = 58 << 20
ORDER_ATT = (1, 0, 3, 2)
ORDER_FEED = (1, 0, 2, 3)


def pick(order, k):
    index = order[3]
    for i in (2, 1, 0):
        index = jnp.where(k == i, order[i], index)
    return index


def forward_kernel(
    wide, ps_s, vl_s, hid, enc, cot, tab, hot, ps, pc, pf, gain_s, gain_c, gain_f,
    xf, gs, gc, gf, gff, ef, q1, kv1, at1, p1, q2, kv2, at2, p2, h1, out_o, d2_o, gg_o,
    wbuf, stage, xv, ev, tabs, off, nf, mask, tb, s, h2, nc, nct, cv, ct, gu, da, act, dgu, acc, buf, landed,
    ls, ins, inr, ws, vs, zs, zr, ys, yr, xs, xr, cs, cr, fsend, frecv, fout,
):
    step = pl.program_id(0)
    d, w, n, pn, yn, dn = place_here()
    y = n // 2
    blks = (n, dn)
    rl = ps.shape[0]
    groups = ((ps, gs, 0, 768, True), (pc, gc, 0, 768, True), (pf, gf, 0, 1024, True), (pf, gf, 1024, 512, False))
    keep, give = (1, 3), (0, 2)
    diag, pair, line_x, line_y = (d, w, dn), (d, w, pn), (1 - d, w, n), (d, w, yn)

    def cols(g, which):
        start, width, split = groups[g][2:]
        if which == 2 or not split:
            return pl.ds(start, width)
        half = width // 2
        pos = d if which == 0 else 1 - d
        return pl.ds(pl.multiple_of(start + pos * half, 128), half)

    def own(g, which):
        return groups[g][0].at[:, cols(g, which)]

    def spot(g, slot, row, which):
        return groups[g][1].at[slot, row, :, cols(g, which)]

    def zcopy(g, k):
        dev = (d, lax.rem(w + k, wide), n)
        if g == 4:
            ref = spot(3, 3, w, 0)
            return remote(ref, ref, zs.at[4, k], zr.at[4, w], dev)
        return remote(own(g, 0), spot(g, 1, w, 0), zs.at[g, k], zr.at[g, w], dev)

    def zgot(g, row):
        ref = spot(3, 3, row, 0) if g == 4 else spot(g, 1, row, 0)
        return remote(ref, ref, zs.at[g, 0], zr.at[g, row], line_x)

    def ycopy(g, row, src=None):
        ref = spot(g, 1, row, 0)
        return remote(ref if src is None else src, spot(g, 3, row, 0), ys.at[g, row], yr.at[g, row], line_y)

    def ygot(g, row):
        return remote(spot(g, 3, row, 0), spot(g, 3, row, 0), ys.at[g, row], yr.at[g, row], line_y)

    def xcopy(g, side, row):
        ref = spot(g, keep[side], row, 0)
        return remote(ref, ref, xs.at[g, side, row], xr.at[g, side, row], line_x)

    def xgot(g, side, row):
        ref = spot(g, keep[side], row, 1)
        return remote(ref, ref, xs.at[g, side, row], xr.at[g, side, row], line_x)

    def ccopy(g, side, row, src=None):
        ref = spot(g, keep[side], row, 2)
        return remote(
            ref if src is None else src, spot(g, give[side], row, 2), cs.at[g, side, row], cr.at[g, side, row], pair
        )

    def cgot(g, side, row):
        ref = spot(g, give[side], row, 2)
        return remote(ref, ref, cs.at[g, side, row], cr.at[g, side, row], pair)

    def around(first, body):
        loop(first, wide, lambda k: body(lax.rem(w + k, wide)))

    def zsend(g):
        loop(1, wide, lambda k: zcopy(g, k).start())

    def own_sends(g):
        ycopy(g, w, own(g, 0)).start()
        ccopy(g, 0, w, own(g, 2)).start()

    def zpass(g, then):
        def one(row):
            zgot(g, row).wait_recv()
            for nxt in then:
                nxt(row).start()

        around(1, one)

    def ypass(g):
        def one(row):
            ygot(g, row).wait_recv()
            xcopy(g, 1, row).start()

        around(0, one)

    def xsend(g):
        around(1, lambda row: xcopy(g, 0, row).start())

    def xstep(g, side):
        def one(k):
            row = lax.rem(w + k, wide)
            xgot(g, side, row).wait_recv()
            ccopy(g, side, row).start()

        loop(1 - side, wide, one)

    def cwait(g, side):
        loop(0, wide, lambda k: cgot(g, side, lax.rem(w + k, wide)).wait_recv())

    straight = rl % 16 == 0
    many = 16 // math.gcd(rl, 16)

    def slab_copies(ref, slot, b):
        width = ref.shape[-1]
        if straight:
            return [
                pltpu.make_async_copy(
                    ref.at[slot, k], wbuf.at[b, pl.ds(k * rl, rl), pl.ds(0, width)], ws.at[b, k]
                )
                for k in range(wide)
            ]
        return [pltpu.make_async_copy(ref.at[slot], stage.at[:, :, pl.ds(0, width)], ws.at[b, 0])]

    def fetch(ref, slot, b):
        for copy in slab_copies(ref, slot, b):
            copy.start()

    def fetched(ref, slot, b):
        for copy in slab_copies(ref, slot, b):
            copy.wait()
        if not straight:
            width = ref.shape[-1]
            for k in range(0, wide, many):
                part = jnp.concatenate([stage[k + i, :, 0:width].astype(f32) for i in range(many)], axis=0)
                wbuf[b, k * rl : (k + many) * rl, 0:width] = part.astype(bf16)

    local = [
        pltpu.make_async_copy(src, dst, ls.at[i])
        for i, (src, dst) in enumerate(
            (
                (ps, gs.at[1, w]),
                (pc, gc.at[1, w]),
                (pf, gf.at[1, w]),
                (hid.at[y], xv.at[n]),
                (enc.at[y], ev.at[n]),
                (cot.at[y], cv.at[0]),
            )
        )
    ]
    back = [pltpu.make_async_copy(xv, xf, vs.at[0]), pltpu.make_async_copy(ev, ef, vs.at[1])]
    early = [
        remote(tab, tabs.at[0], ins.at[3], inr.at[3], pair),
        remote(tab, tabs.at[3], ins.at[4], inr.at[4], line_y),
        remote(tab, tabs.at[2], ins.at[5], inr.at[5], diag),
        remote(hid.at[1 - y], xv.at[n], ins.at[0], inr.at[0], diag),
        remote(hid.at[y], xv.at[n], ins.at[6], inr.at[6], pair),
    ]
    middle = [
        remote(enc.at[1 - y], ev.at[n], ins.at[1], inr.at[1], diag),
        remote(enc.at[y], ev.at[n], ins.at[7], inr.at[7], pair),
        remote(cot.at[1 - y], cv.at[1], ins.at[2], inr.at[2], diag),
    ]
    later = [
        remote(xv.at[dn], xv.at[dn], ins.at[8], inr.at[8], pair),
        remote(ev.at[dn], ev.at[dn], ins.at[9], inr.at[9], pair),
    ]

    def arrived(i, ref):
        remote(ref, ref, ins.at[i], inr.at[i], pair).wait_recv()

    @pl.when(step == 0)
    def _():
        for copy in local:
            copy.start()
        greet((pair, line_y, diag, line_x), wide)
        for copy in early:
            copy.start()
        zsend(0)
        own_sends(0)
        tabs[1] = tab[...]
        arrived(6, xv.at[pn])
        arrived(0, xv.at[dn])
        later[0].start()
        arrived(8, xv.at[yn])
        local[3].wait()
        back[0].start()
        arrived(3, tabs.at[0])
        arrived(4, tabs.at[3])
        arrived(5, tabs.at[2])
        start, length = ps_s[y, 0], vl_s[y, 0]
        for i in range(2):

            def mask_rows(r, i=i):
                shape = (32, LEN)
                qi = blks[i] * 256 + r.start + lax.broadcasted_iota(jnp.int32, shape, 0)
                kj = lax.broadcasted_iota(jnp.int32, shape, 1)
                inside = (qi >= start) & (qi < start + PIC) & (kj >= start) & (kj < start + PIC)
                allowed = ((kj <= qi) | inside) & (kj < length)
                mask[pl.ds(i * 256 + r.start, 32), :] = jnp.where(allowed, 0.0, masked_value)

            rows_loop(256, 32, mask_rows)
        for i in range(4):

            def norm_rows(r, i=i):
                nf[pl.ds(i * 256 + r.start, 64), :] = normed(xv[i, r, :].astype(f32), gain_s[...]).astype(bf16)

            rows_loop(256, 64, norm_rows)
        for i in range(2):
            h1[i * 256 : (i + 1) * 256, :] = xv[blks[i]].astype(f32)
        zpass(0, (lambda row: ycopy(0, row), lambda row: xcopy(0, 0, row)))
        zsend(1)
        own_sends(1)
        middle[0].start()
        middle[1].start()
        xstep(0, 0)
        for i in range(3):
            local[i].wait()
        fetch(gs, 1, 0)

    @pl.when(step < 4)
    def _():
        b = lax.rem(step, 2)
        slot = pick(ORDER_ATT, step)
        fetched(gs, slot, b)
        off[...] = lax.dot_general(
            tabs[slot, 0:8, 0:BUCKETS], hot[...], (((1,), (0,)), ((), ())), precision=precise, preferred_element_type=f32
        )
        kv1[0] = nn(nf[...], wbuf[b, :, 384:768]).astype(bf16).T
        for i in range(2):
            q1[0, i * 256 : (i + 1) * 256, :] = nn(nf[block_rows(blks[i]), :], wbuf[b, :, 0:192]).astype(bf16)
        for h in range(3):
            for t in range(TILES):
                line = jnp.broadcast_to(off[h : h + 1, 128 * t : 128 * t + 256], (128, 256))
                tb[t] = pltpu.roll(line, 129, 1, stride=1, stride_axis=0)[:, :128]
            hs = slice(h * DHEAD, (h + 1) * DHEAD)
            vs_ = slice(HD + h * DHEAD, HD + (h + 1) * DHEAD)
            for i in range(2):
                s[...] = nn(q1[0, i * 256 : (i + 1) * 256, hs], kv1[0, hs, :])
                for r in range(2):
                    idx = [jnp.minimum(kb - 2 * blks[i] - r, 3) + 7 for kb in range(8)]

                    def soft_rows(rr, i=i, r=r, h=h, idx=idx):
                        bias = jnp.concatenate([tb[idx[kb], rr, :] for kb in range(8)], axis=1)
                        v = s[pl.ds(r * 128 + rr.start, ROWS), :] + bias
                        v = v + mask[pl.ds(i * 256 + r * 128 + rr.start, ROWS), :]
                        p1[0, h, pl.ds(i * 256 + r * 128 + rr.start, ROWS), :] = softmax_rows(v).astype(bf16)

                    rows_loop(128, ROWS, soft_rows, unroll=8)
                at1[0, i * 256 : (i + 1) * 256, hs] = nt(
                    p1[0, h, i * 256 : (i + 1) * 256, :], kv1[0, vs_, :]
                ).astype(bf16)
        h1[...] += nt(at1[0], wbuf[b, :, 192:384])

    @pl.when(step == 0)
    def _():
        cwait(0, 0)
        fetch(gs, 0, 1)
        ypass(0)
        zpass(1, (lambda row: ycopy(1, row),))
        zsend(2)
        own_sends(2)
        own_sends(3)

    @pl.when(step == 1)
    def _():
        xstep(0, 1)
        fetch(gs, 3, 0)
        xsend(1)
        middle[2].start()

    @pl.when(step == 2)
    def _():
        cwait(0, 1)
        fetch(gs, 2, 1)
        ypass(1)
        zpass(2, (lambda row: ycopy(2, row),))
        zsend(3)
        ygot(3, w).wait_recv()
        ccopy(3, 1, w).start()
        zsend(4)

    @pl.when(step == 3)
    def _():
        xstep(1, 0)
        fetch(gc, 1, 0)
        xsend(2)
        arrived(1, ev.at[dn])
        later[1].start()
        arrived(7, ev.at[pn])
        arrived(9, ev.at[yn])
        local[4].wait()
        back[1].start()

        def norm_rows(r):
            x = h1[r, :]
            nc[r, :] = normed(x, gain_c[...]).astype(bf16)
            h2[r, :] = x

        rows_loop(512, 64, norm_rows)

    @pl.when((step >= 4) & (step < 8))
    def _():
        b = lax.rem(step, 2)
        fetched(gc, pick(ORDER_ATT, step - 4), b)
        kv2[0] = nn(ev[...].reshape(ENC, D), wbuf[b, :, 384:768]).astype(bf16).T
        q2[0] = nn(nc[...], wbuf[b, :, 0:192]).astype(bf16)
        for h in range(3):
            hs = slice(h * DHEAD, (h + 1) * DHEAD)
            vs_ = slice(HD + h * DHEAD, HD + (h + 1) * DHEAD)
            gu[:, 0:ENC] = nn(q2[0, :, hs], kv2[0, hs, :])

            def soft_rows(r, h=h):
                p2[0, h, r, :] = softmax_rows(gu[r, 0:ENC]).astype(bf16)

            rows_loop(512, 16, soft_rows, unroll=32)
            at2[0, :, hs] = nt(p2[0, h], kv2[0, vs_, :]).astype(bf16)
        h2[...] += nt(at2[0], wbuf[b, :, 192:384])

    @pl.when(step == 4)
    def _():
        cwait(1, 0)
        fetch(gc, 0, 1)

    @pl.when(step == 5)
    def _():
        xstep(1, 1)
        fetch(gc, 3, 0)
        ypass(2)

    @pl.when(step == 6)
    def _():
        cwait(1, 1)
        fetch(gc, 2, 1)

    @pl.when(step == 7)
    def _():
        xstep(2, 0)
        zpass(3, (lambda row: ccopy(3, 0, row),))
        fetch(gf, 1, 0)
        arrived(2, cv.at[1])
        local[5].wait()

        def norm_rows(r):
            x = h2[r, :]
            nc[r, :] = normed(x, gain_f[...]).astype(bf16)
            acc[r, :] = x
            d2_o[r, :] = jnp.zeros((64, D), f32)

        rows_loop(512, 64, norm_rows)
        nct[...] = nc[...].T
        ct[...] = cv[...].reshape(512, D).T

    def give_copy(side):
        return remote(buf.at[0], landed.at[side], fsend.at[side], frecv.at[side], pair)

    def put_out(side):
        return pltpu.make_async_copy(buf.at[1], gff.at[side], fout.at[side])

    def add_side(side):
        give_copy(side).wait_recv()

        def add(r):
            buf[1, r, :] = buf[1, r, :] + landed[side, r, :]

        rows_loop(D, 64, add)
        put_out(side).start()

    @pl.when(step >= 8)
    def _():
        b = lax.rem(step, 2)
        fetched(gf, pick(ORDER_FEED, step - 8), b)
        gu[...] = nn(nc[...], wbuf[b, :, : 2 * FFB])
        da[...] = nn(cv[...].reshape(512, D), wbuf[b, :, 2 * FFB :])

        def gelu_rows(r):
            gate = gu[r, :FFB]
            up = gu[r, FFB:]
            d_act = da[r, :]
            sq = gate * gate
            th = jnp.tanh(GELU_A * gate * (1.0 + GELU_B * sq))
            half = 0.5 + 0.5 * th
            gelu = gate * half
            slope = half + 0.5 * GELU_A * gate * (1.0 - th * th) * (1.0 + 3.0 * GELU_B * sq)
            act[r, :] = (gelu * up).astype(bf16)
            dgu[r, :FFB] = (d_act * up * slope).astype(bf16)
            dgu[r, FFB:] = (d_act * gelu).astype(bf16)

        rows_loop(512, 16, gelu_rows, unroll=32)
        acc[...] += nt(act[...], wbuf[b, :, 2 * FFB :])
        d2_o[...] += nt(dgu[...], wbuf[b, :, : 2 * FFB])

        @pl.when(step == 10)
        def _():
            give_copy(0).wait_send()

        @pl.when(step == 11)
        def _():
            put_out(0).wait()

        place = jnp.where((step == 8) | (step == 11), 1, 0)
        buf[place, :, : 2 * FFB] = nn(nct[...], dgu[...]).astype(bf16)
        buf[place, :, 2 * FFB :] = nn(ct[...], act[...]).astype(bf16)

    @pl.when(step == 8)
    def _():
        cwait(2, 0)
        cwait(3, 0)
        fetch(gf, 0, 1)

    @pl.when(step == 9)
    def _():
        give_copy(0).start()
        zpass(4, (lambda row: ccopy(3, 1, row),))
        xstep(2, 1)
        cwait(2, 1)
        cwait(3, 1)
        fetch(gf, 2, 0)

    @pl.when(step == 10)
    def _():
        give_copy(1).start()
        fetch(gf, 3, 1)
        add_side(0)

    @pl.when(step == 11)
    def _():
        add_side(1)
        gg_o[...] = jnp.zeros((1, D), f32)

        for i in range(2):

            def back_rows(r, i=i):
                rows = pl.ds(i * 256 + r.start, 64)
                dx, gg = norm_back(h2[rows, :], gain_f[...], d2_o[rows, :])
                d2_o[rows, :] = cv[i, r, :].astype(f32) + dx
                gg_o[...] += gg
                out_o[rows, :] = acc[rows, :].astype(bf16)

            rows_loop(256, 64, back_rows, unroll=2)
        for copy in back:
            copy.wait()
        put_out(1).wait()
        give_copy(1).wait_send()
        for copy in early + middle + later:
            copy.wait_send()

        def finish(row):
            for g in range(4):
                for side in range(2):
                    ccopy(g, side, row).wait_send()
            for g in range(3):
                ycopy(g, row).wait_send()
                xcopy(g, 1, row).wait_send()

        around(0, finish)
        ycopy(3, w).wait_send()

        def finish_line(k):
            row = lax.rem(w + k, wide)
            for g in range(5):
                zcopy(g, k).wait_send()
            for g in range(3):
                xcopy(g, 0, row).wait_send()

        loop(1, wide, finish_line)


def forward(wide, ps_s, vl_s, hid, enc, cot, tab, hot, ps, pc, pf, gain_s, gain_c, gain_f):
    rl = ps.shape[0]
    sem = pltpu.SemaphoreType.DMA
    V = pl.BlockSpec(memory_space=pltpu.VMEM)

    def turn(first, shape):
        zero = (0,) * len(shape)
        return pl.BlockSpec(
            (1,) + shape, lambda n: (pick(ORDER_ATT, jnp.clip(n - first, 0, 3)),) + zero
        )

    v = lambda *shape: pltpu.VMEM(shape, bf16)
    vf = lambda *shape: pltpu.VMEM(shape, f32)
    return pl.pallas_call(
        partial(forward_kernel, wide),
        grid=(12,),
        in_specs=[SMEM, SMEM, ANY, ANY, ANY, V, V, V, V, V, V, V, V],
        out_specs=[ANY] * 6
        + [turn(0, (512, HD)), turn(0, (2 * HD, LEN)), turn(0, (512, HD)), turn(0, (3, 512, LEN))]
        + [turn(4, (512, HD)), turn(4, (2 * HD, ENC)), turn(4, (512, HD)), turn(4, (3, 512, ENC))]
        + [V, V, V, V],
        out_shape=[
            out((4, 256, D), bf16),
            out((4, wide, rl, D), bf16),
            out((4, wide, rl, D), bf16),
            out((4, wide, rl, 2 * D), bf16),
            out((2, D, 3 * FFB), bf16),
            out((4, 128, D), bf16),
            out((4, 512, HD), bf16),
            out((4, 2 * HD, LEN), bf16),
            out((4, 512, HD), bf16),
            out((4, 3, 512, LEN), bf16),
            out((4, 512, HD), bf16),
            out((4, 2 * HD, ENC), bf16),
            out((4, 512, HD), bf16),
            out((4, 3, 512, ENC), bf16),
            out((512, D), f32),
            out((512, D), bf16),
            out((512, D), f32),
            out((1, D), f32),
        ],
        scratch_shapes=[
            v(2, D, 3 * FFB),
            v(wide, rl, 3 * FFB) if rl % 16 else v(16, 128),
            v(4, 256, D),
            v(4, 128, D),
            vf(4, 32, 128),
            vf(8, 2048),
            v(LEN, D),
            vf(512, LEN),
            vf(TILES, 128, 128),
            vf(256, LEN),
            vf(512, D),
            v(512, D),
            v(D, 512),
            v(2, 256, D),
            v(D, 512),
            vf(512, 2 * FFB),
            vf(512, FFB),
            v(512, FFB),
            v(512, 2 * FFB),
            vf(512, D),
            v(2, D, 3 * FFB),
            v(2, D, 3 * FFB),
            sem((6,)),
            sem((10,)),
            sem((10,)),
            sem((2, wide)),
            sem((2,)),
            sem((5, wide)),
            sem((5, wide)),
            sem((4, wide)),
            sem((4, wide)),
            sem((4, 2, wide)),
            sem((4, 2, wide)),
            sem((4, 2, wide)),
            sem((4, 2, wide)),
            sem((2,)),
            sem((2,)),
            sem((2,)),
        ],
        compiler_params=pltpu.CompilerParams(
            dimension_semantics=("arbitrary",), vmem_limit_bytes=FORWARD_VMEM, collective_id=0, has_side_effects=True
        ),
        cost_estimate=cost(60),
        name="forward",
    )(ps_s, vl_s, hid, enc, cot, tab, hot, ps, pc, pf, gain_s, gain_c, gain_f)


def cross_backward_kernel(
    h1, ef, d2, w, gain, q, kv, at, p, gff,
    gw_o, d1_o, gg_o, ge_o, gep_o, o1, o2,
    d2b, d2t, nct, eft, get, do, dp, ds, dq, dkv, buf, landed, rx, ry, send, recv, load, fs, fr,
):
    n = pl.program_id(0)
    slot = lax.rem(n, 2)
    core = CoreSum(n, buf, landed, send, recv)
    d, wi, me, pn, yn, dn = place_here()
    y = me // 2
    mine = pl.ds(pl.multiple_of(d * 384, 128), 384)
    other = pl.ds(pl.multiple_of(384 - d * 384, 128), 384)
    late = pl.ds(D, D)
    loads = [
        pltpu.make_async_copy(gff.at[:, :, :, mine], o1, load.at[0]),
        pltpu.make_async_copy(gff.at[0, :, :, late], o2, load.at[1]),
    ]
    sends = [
        remote(gff.at[:, :, :, other], rx, fs.at[0], fr.at[0], (1 - d, wi, me)),
        remote(gff.at[1, :, :, late], ry, fs.at[1], fr.at[1], (d, wi, yn)),
    ]

    @pl.when(n == 0)
    def _():
        def norm_rows(r):
            d2b[r, :] = d2[r, :].astype(bf16)
            d1_o[r, :] = jnp.zeros((64, D), f32)
            dp[r, :] = normed(h1[r, :], gain[...])

        for copy in loads:
            copy.start()
        greet(((d, wi, pn), (d, wi, yn), (1 - d, wi, me)))
        for copy in sends:
            copy.start()
        rows_loop(512, 64, norm_rows)
        nct[...] = dp[...].astype(bf16).T
        d2t[...] = d2b[...].T
        eft[...] = ef[...].T
        get[...] = jnp.zeros((D, ENC), f32)

    do[...] = nn(d2b[...], w[0, :, 192:384]).astype(bf16)
    for h in range(3):
        hs = slice(h * DHEAD, (h + 1) * DHEAD)
        vs = slice(HD + h * DHEAD, HD + (h + 1) * DHEAD)
        dp[:, :ENC] = nn(do[:, hs], kv[0, vs, :])

        def grad_rows(r, h=h, hs=hs):
            delta = jnp.sum(do[r, hs].astype(f32) * at[0, r, hs].astype(f32), axis=1, keepdims=True)
            ds[r, :] = (p[0, h, r, :].astype(f32) * (dp[r, :ENC] - delta)).astype(bf16)

        rows_loop(512, 16, grad_rows, unroll=32)
        dq[:, hs] = nt(ds[...], kv[0, hs, :]).astype(bf16)
        dkv[hs, :] = tn(q[0, :, hs], ds[...]).astype(bf16)
        dkv[vs, :] = tn(do[:, hs], p[0, h]).astype(bf16)
    d1_o[...] += nt(dq[...], w[0, :, 0:192])
    get[...] += nn(w[0, :, 384:768], dkv[...])
    buf[slot, :, 0:384] = jnp.concatenate([nn(nct[...], dq[...]), nn(d2t[...], at[0])], axis=1).astype(bf16)
    buf[slot, :, 384:768] = nt(eft[...], dkv[...]).astype(bf16)
    core.finish(gw_o)

    @pl.when(n == 3)
    def _():
        gg_o[...] = jnp.zeros((1, D), f32)

        def back_rows(r):
            dx, gg = norm_back(h1[r, :], gain[...], d1_o[r, :])
            d1_o[r, :] = d2[r, :] + dx
            gg_o[...] += gg

        rows_loop(512, 64, back_rows)
        for i in range(2):
            half = slice(i * 128, (i + 1) * 128)
            cols = lambda blk: pl.ds(pl.multiple_of(blk * 128, 128), 128)
            ge_o[half, :] = get[:, cols((me, 3 - me)[i])].T
            gep_o[half, :] = get[:, cols((pn, 3 - pn)[i])].T.astype(bf16)
        for copy in loads:
            copy.wait()
        for copy in sends:
            copy.wait()
        add_into(o1, rx)
        add_into(o2, ry)


def cross_backward(wide, h1, ef, d2, w, gain, q, kv, at, p, gff):
    rl = D // wide
    return pl.pallas_call(
        cross_backward_kernel,
        grid=(4,),
        in_specs=[
            whole((512, D)),
            whole((ENC, D)),
            whole((512, D)),
            slab((D, D)),
            whole((1, D)),
            slab((512, HD)),
            slab((2 * HD, ENC)),
            slab((512, HD)),
            slab((3, 512, ENC)),
            ANY,
        ],
        out_specs=[
            pair_slab((D, D)),
            whole((512, D)),
            whole((1, D)),
            whole((256, D)),
            whole((256, D)),
            whole((2, wide, rl, 384)),
            whole((wide, rl, D)),
        ],
        out_shape=[
            out((2, D, D), bf16),
            out((512, D), f32),
            out((1, D), f32),
            out((256, D), f32),
            out((256, D), bf16),
            out((2, wide, rl, 384), bf16),
            out((wide, rl, D), bf16),
        ],
        scratch_shapes=[
            pltpu.VMEM((512, D), bf16),
            pltpu.VMEM((D, 512), bf16),
            pltpu.VMEM((D, 512), bf16),
            pltpu.VMEM((D, ENC), bf16),
            pltpu.VMEM((D, ENC), f32),
            pltpu.VMEM((512, HD), bf16),
            pltpu.VMEM((512, D), f32),
            pltpu.VMEM((512, ENC), bf16),
            pltpu.VMEM((512, HD), bf16),
            pltpu.VMEM((2 * HD, ENC), bf16),
            pltpu.VMEM((2, D, D), bf16),
            pltpu.VMEM((2, D, D), bf16),
            pltpu.VMEM((2, wide, rl, 384), bf16),
            pltpu.VMEM((wide, rl, D), bf16),
            pltpu.SemaphoreType.DMA((1,)),
            pltpu.SemaphoreType.DMA((2,)),
            pltpu.SemaphoreType.DMA((2,)),
            pltpu.SemaphoreType.DMA((2,)),
            pltpu.SemaphoreType.DMA((2,)),
        ],
        compiler_params=params(3),
        cost_estimate=cost(14),
        name="cross_backward",
    )(h1, ef, d2, w, gain, q, kv, at, p, gff.reshape(2, wide, rl, 3 * FFB))


def self_backward_kernel(
    wide, xf, d1, w, gain, q, kv, at, p, gcr, o1, o2,
    gw_o, g_o, gp_o, dl_o, c1, c2, e1, e2,
    d1b, d1t, nft, nqt, gt, gq, do, dp, ds, dq, dkv, buf, landed, s1, f2, rx, ry, ry1, rz1, rz2,
    send, recv, load, fs, fr, zs, zr,
):
    n = pl.program_id(0)
    blks = own_blocks()
    slot = lax.rem(n, 2)
    core = CoreSum(n, buf, landed, send, recv)
    d, wi, me, pn, yn, dn = place_here()
    y = me // 2
    mine = pl.ds(pl.multiple_of(d * 256, 128), 256)
    other = pl.ds(pl.multiple_of(256 - d * 256, 128), 256)
    late = pl.ds(512, 256)
    loads = [
        pltpu.make_async_copy(gcr.at[:, :, :, mine], c1, load.at[0]),
        pltpu.make_async_copy(gcr.at[0, :, :, late], c2, load.at[1]),
        pltpu.make_async_copy(o1.at[0], s1, load.at[2]),
        pltpu.make_async_copy(o2.at[wi], f2, load.at[3]),
    ]
    sends = [
        remote(o1.at[1], ry1, fs.at[0], fr.at[0], (d, wi, yn)),
        remote(gcr.at[:, :, :, other], rx, fs.at[1], fr.at[1], (1 - d, wi, me)),
        remote(gcr.at[1, :, :, late], ry, fs.at[2], fr.at[2], (d, wi, yn)),
    ]

    def zcopy(path, k):
        row = lax.rem(wi + k, wide)
        src, dst = ((s1, rz1), (o2, rz2))[path]
        return remote(src.at[row], dst.at[wi], zs.at[path, k], zr.at[path, wi], (d, row, me))

    def zgot(path, k):
        row = lax.rem(wi + k, wide)
        ref = (rz1, rz2)[path].at[row]
        return remote(ref, ref, zs.at[path, k], zr.at[path, row], (d, row, me))

    @pl.when(n == 0)
    def _():
        def cast_rows(r):
            d1b[r, :] = d1[r, :].astype(bf16)
            gq[r, :] = jnp.zeros((64, D), f32)

        for copy in loads:
            copy.start()
        greet(((d, wi, pn), (d, wi, yn), (1 - d, wi, me)), wide)
        for copy in sends:
            copy.start()
        loop(1, wide, lambda k: zcopy(1, k).start())
        rows_loop(512, 64, cast_rows)
        d1t[...] = d1b[...].T
        for i in range(4):
            part = normed(xf[i * 256 : (i + 1) * 256, :].astype(f32), gain[...]).astype(bf16)
            nft[:, i * 256 : (i + 1) * 256] = part.T
        for i in range(2):
            part = normed(xf[block_rows(blks[i]), :].astype(f32), gain[...]).astype(bf16)
            nqt[:, i * 256 : (i + 1) * 256] = part.T
        gt[...] = jnp.zeros((D, LEN), f32)

    @pl.when(n == 2)
    def _():
        loads[2].wait()
        sends[0].wait_recv()
        add_into(s1, ry1)
        loop(1, wide, lambda k: zcopy(0, k).start())

    dl_o[0] = jnp.zeros((3, 2048), f32)
    do[...] = nn(d1b[...], w[0, :, 192:384]).astype(bf16)
    for h in range(3):
        hs = slice(h * DHEAD, (h + 1) * DHEAD)
        vs = slice(HD + h * DHEAD, HD + (h + 1) * DHEAD)
        dk = jnp.zeros((DHEAD, LEN), f32)
        dv = jnp.zeros((DHEAD, LEN), f32)
        for i in range(2):
            half = slice(i * 256, (i + 1) * 256)
            dp[...] = nn(do[half, hs], kv[0, vs, :])

            def grad_rows(rr, i=i, h=h, hs=hs):
                rows = pl.ds(i * 256 + rr.start, ROWS)
                delta = jnp.sum(do[rows, hs].astype(f32) * at[0, rows, hs].astype(f32), axis=1, keepdims=True)
                ds[rr, :] = (p[0, h, rows, :].astype(f32) * (dp[rr, :] - delta)).astype(bf16)

            rows_loop(256, ROWS, grad_rows, unroll=16)
            upper, lower = ds[:128, :].astype(f32), ds[128:, :].astype(f32)
            part = jnp.concatenate(
                [
                    upper[:, :896] + lower[:, 128:],
                    upper[:, 896:],
                    jnp.zeros((128, 128), f32),
                    lower[:, :128],
                ],
                axis=1,
            )
            height = 128
            while height > 1:
                height //= 2
                part = part[:height] + pltpu.roll(part[height:], SPAN - height, 1)
            where = pl.ds(pl.multiple_of(768 - 256 * blks[i], 128), SPAN)
            dl_o[0, h : h + 1, where] += pltpu.roll(part, 255, 1)
            dq[half, hs] = nt(ds[...], kv[0, hs, :]).astype(bf16)
            dk = dk + tn(q[0, half, hs], ds[...])
            dv = dv + tn(do[half, hs], p[0, h, half, :])
        dkv[hs, :] = dk.astype(bf16)
        dkv[vs, :] = dv.astype(bf16)
    gq[...] += nt(dq[...], w[0, :, 0:192])
    gt[...] += nn(w[0, :, 384:768], dkv[...])
    buf[slot, :, 0:384] = jnp.concatenate([nn(nqt[...], dq[...]), nn(d1t[...], at[0])], axis=1).astype(bf16)
    buf[slot, :, 384:768] = nt(nft[...], dkv[...]).astype(bf16)
    core.finish(gw_o)

    @pl.when(n == 3)
    def _():
        for i in range(2):
            half = slice(i * 256, (i + 1) * 256)
            g_o[half, :] = gq[half, :] + gt[:, block_rows(blks[i])].T
            gp_o[half, :] = gt[:, block_rows((pn, 3 - pn)[i])].T.astype(bf16)
        loads[0].wait()
        sends[1].wait_recv()
        add_into(c1, rx)
        loads[1].wait()
        sends[2].wait_recv()
        add_into(c2, ry)
        loads[3].wait()
        for path in (1, 0):
            loop(1, wide, lambda k, path=path: zgot(path, k).wait_recv())

        def put(ref):
            def store(r, total):
                ref[r, :] = total.astype(bf16)

            return store

        sum_line(wide, s1.at[wi], rz1, put(e1))
        sum_line(wide, f2, rz2, put(e2))
        for copy in sends:
            copy.wait_send()
        for path in (0, 1):
            loop(1, wide, lambda k, path=path: zcopy(path, k).wait_send())


def self_backward(wide, xf, d1, w, gain, q, kv, at, p, gcr, o1, o2):
    rl = D // wide
    return pl.pallas_call(
        partial(self_backward_kernel, wide),
        grid=(4,),
        in_specs=[
            whole((LEN, D)),
            whole((512, D)),
            slab((D, D)),
            whole((1, D)),
            slab((512, HD)),
            slab((2 * HD, LEN)),
            slab((512, HD)),
            slab((3, 512, LEN)),
            ANY,
            ANY,
            ANY,
        ],
        out_specs=[
            pair_slab((D, D)),
            whole((512, D)),
            whole((512, D)),
            slab((3, 2048)),
            whole((2, wide, rl, 256)),
            whole((wide, rl, 256)),
            whole((rl, 384)),
            whole((rl, D)),
        ],
        out_shape=[
            out((2, D, D), bf16),
            out((512, D), f32),
            out((512, D), bf16),
            out((4, 3, 2048), f32),
            out((2, wide, rl, 256), bf16),
            out((wide, rl, 256), bf16),
            out((rl, 384), bf16),
            out((rl, D), bf16),
        ],
        scratch_shapes=[
            pltpu.VMEM((512, D), bf16),
            pltpu.VMEM((D, 512), bf16),
            pltpu.VMEM((D, LEN), bf16),
            pltpu.VMEM((D, 512), bf16),
            pltpu.VMEM((D, LEN), f32),
            pltpu.VMEM((512, D), f32),
            pltpu.VMEM((512, HD), bf16),
            pltpu.VMEM((256, LEN), f32),
            pltpu.VMEM((256, LEN), bf16),
            pltpu.VMEM((512, HD), bf16),
            pltpu.VMEM((2 * HD, LEN), bf16),
            pltpu.VMEM((2, D, D), bf16),
            pltpu.VMEM((2, D, D), bf16),
            pltpu.VMEM((wide, rl, 384), bf16),
            pltpu.VMEM((rl, D), bf16),
            pltpu.VMEM((2, wide, rl, 256), bf16),
            pltpu.VMEM((wide, rl, 256), bf16),
            pltpu.VMEM((wide, rl, 384), bf16),
            pltpu.VMEM((wide, rl, 384), bf16),
            pltpu.VMEM((wide, rl, D), bf16),
            pltpu.SemaphoreType.DMA((1,)),
            pltpu.SemaphoreType.DMA((2,)),
            pltpu.SemaphoreType.DMA((4,)),
            pltpu.SemaphoreType.DMA((3,)),
            pltpu.SemaphoreType.DMA((3,)),
            pltpu.SemaphoreType.DMA((2, wide)),
            pltpu.SemaphoreType.DMA((2, wide)),
        ],
        compiler_params=params(4),
        cost_estimate=cost(25),
        name="self_backward",
    )(xf, d1, w, gain, q, kv, at, p, gcr.reshape(2, wide, rl, D), o1, o2)


def reduce_kernel(
    wide, se, c1, c2, e1, e2, outp, gxo, gxp, geo, gep, xf, d1, gain, gfeed, gcross, tg,
    out_o, gin_o, gen_o, sg_o, st_o, ff_o, cr_o, se_o,
    a1, a2, rx, ry, ry1, cy1, b1, rzs1, rzs2, rzc1, rzc2, fs, fc, xs1, xs2, xc1, xc2, x1, x2,
    rgx, rge, tmp_in, tmp_en, back_in, back_en, rows_f, sg, st, rsg, rst, rsgz, rstz,
    load, ms, mr, ts, tr, zs, zr, ss, sr, os,
):
    d, w, n, pn, yn, dn = place_here()
    y = n // 2
    pair, line_y, diag, line_x = (d, w, pn), (d, w, yn), (d, w, dn), (1 - d, w, n)
    mine = pl.ds(pl.multiple_of(d * 256, 128), 256)
    other = pl.ds(pl.multiple_of(256 - d * 256, 128), 256)
    late = pl.ds(512, 256)
    loads = [
        pltpu.make_async_copy(se.at[:, :, :, mine], a1, load.at[0]),
        pltpu.make_async_copy(se.at[0, :, :, late], a2, load.at[1]),
        pltpu.make_async_copy(c1.at[0], b1, load.at[2]),
        pltpu.make_async_copy(geo, tmp_en, load.at[3]),
        pltpu.make_async_copy(outp.at[0], out_o.at[y], load.at[4]),
    ]
    for copy in loads:
        copy.start()
    greet((pair, line_y, diag, line_x), wide)
    turn = lambda i, src, dst, dev: remote(src, dst, ts.at[i], tr.at[i], dev)
    put = [
        turn(0, se.at[:, :, :, other], rx, line_x),
        turn(1, c1.at[1], cy1, line_y),
        turn(2, se.at[1, :, :, late], ry, line_y),
        turn(3, e1, x1, line_x),
        turn(4, e2, x2, line_x),
    ]
    cross = [
        remote(gxp, rgx, ms.at[0], mr.at[0], pair),
        remote(gep, rge, ms.at[1], mr.at[1], pair),
        remote(outp.at[1], out_o.at[y], ms.at[2], mr.at[2], diag),
    ]
    out_got = remote(out_o.at[1 - y], out_o.at[1 - y], ms.at[2], mr.at[2], diag)
    z_refs = ((a1, rzs1), (a2, rzs2), (b1, rzc1), (c2, rzc2))

    def zcopy(path, k):
        row = lax.rem(w + k, wide)
        src, dst = z_refs[path]
        src = src.at[0, row] if path == 0 else src.at[row]
        return remote(src, dst.at[w], zs.at[path, k], zr.at[path, w], (d, row, n))

    def zgot(path, k):
        row = lax.rem(w + k, wide)
        ref = z_refs[path][1].at[row]
        return remote(ref, ref, zs.at[path, k], zr.at[path, row], (d, row, n))

    def zstart(path):
        loop(1, wide, lambda k: zcopy(path, k).start())

    def zwait(path):
        loop(1, wide, lambda k: zgot(path, k).wait_recv())

    cross[0].start()
    cross[1].start()
    put[0].start()
    put[1].start()
    put[2].start()
    zstart(3)
    cross[2].start()
    put[3].start()
    put[4].start()

    sg[...] = jnp.zeros((8, D), f32)
    sg[1:2, :] = gcross[...]
    sg[2:3, :] = gfeed[...]
    st[...] = tg[...]
    cross[0].wait_recv()
    own = (n, dn)
    for i in (1, 0):

        def back(r, i=i):
            x = xf[own[i], r, :].astype(f32)
            dx, gg = norm_back(x, gain[...], gxo[i, r, :] + rgx[i, r, :].astype(f32))
            total = d1[i, r, :] + dx
            sg[0:1, :] += gg
            if i == 0:
                rows_f[0, r, :] = total
            else:
                tmp_in[r, :] = total.astype(bf16)

        rows_loop(256, 32, back, unroll=2)
        if i == 1:
            in_send = remote(tmp_in, back_in, ms.at[3], mr.at[3], diag)
            in_send.start()
    in_local = pltpu.make_async_copy(rows_f.at[0], gin_o.at[y], os.at[0])
    in_local.start()
    cross[1].wait_recv()
    loads[3].wait()
    back_en[0] = (tmp_en[1] + rge[1].astype(f32)).astype(bf16)
    en_send = remote(back_en.at[0], back_en.at[1], ms.at[4], mr.at[4], diag)
    en_send.start()
    tmp_en[0] = tmp_en[0] + rge[0].astype(f32)
    en_local = pltpu.make_async_copy(tmp_en.at[0], gen_o.at[y], os.at[1])
    en_local.start()

    def small(j, dev):
        return (
            remote(sg, rsg.at[j], ss.at[0, j], sr.at[0, j], dev),
            remote(st, rst.at[j], ss.at[1, j], sr.at[1, j], dev),
        )

    def small_add(j, dev):
        for copy in small(j, dev):
            copy.wait()
        sg[...] += rsg[j]
        st[...] += rst[j]

    def small_line(k):
        dev = (d, lax.rem(w + k, wide), n)
        return (
            remote(sg, rsgz.at[w], ss.at[0, 3 + k], sr.at[0, 3 + w], dev),
            remote(st, rstz.at[w], ss.at[1, 3 + k], sr.at[1, 3 + w], dev),
        )

    def start_all(copies):
        for copy in copies:
            copy.start()

    start_all(small(0, pair))
    small_add(0, pair)
    start_all(small(1, line_y))

    loads[2].wait()
    put[1].wait_recv()
    add_into(b1, cy1)
    zstart(2)
    small_add(1, line_y)
    start_all(small(2, line_x))
    loads[1].wait()
    put[2].wait_recv()
    add_into(a2, ry)
    zstart(1)
    small_add(2, line_x)
    loop(1, wide, lambda k: start_all(small_line(k)))
    rsgz[w] = sg[...]
    rstz[w] = st[...]
    loads[0].wait()
    put[0].wait_recv()
    add_into(a1, rx)
    y1 = turn(5, a1.at[1], ry1, line_y)
    y1.start()

    def keep(ref, cols):
        def store(r, total):
            ref[r, cols] = total.astype(bf16)

        return store

    everything = slice(None)
    zwait(3)
    sum_line(wide, c2.at[w], rzc2, keep(fc, late))
    f_c2 = turn(6, fc.at[:, late], xc2, line_x)
    f_c2.start()
    zwait(2)
    sum_line(wide, b1.at[w], rzc1, keep(fc, mine))
    f_c1 = turn(7, fc.at[:, mine], xc1, line_x)
    f_c1.start()
    y1.wait_recv()
    rl = e1.shape[0]

    def add_side(k):
        a1[0, k] = a1[0, k] + ry1[k]

    loop(0, wide, add_side)
    zstart(0)

    def small_wait(k):
        row = lax.rem(w + k, wide)
        for i, ref in enumerate((rsgz, rstz)):
            remote(ref.at[row], ref.at[row], ss.at[i, 3], sr.at[i, 3 + row], line_x).wait_recv()

    loop(1, wide, small_wait)
    sg_o[...] = lax.fori_loop(1, wide, lambda k, t: t + rsgz[k], rsgz[0])
    st_o[...] = lax.fori_loop(1, wide, lambda k, t: t + rstz[k], rstz[0])

    zwait(1)
    sum_line(wide, a2.at[w], rzs2, keep(fs, late))
    f_s2 = turn(8, fs.at[:, late], xs2, line_x)
    f_s2.start()

    in_send.wait_recv()

    def widen(r):
        rows_f[1, r, :] = back_in[r, :].astype(f32)

    rows_loop(256, 64, widen)
    in_last = pltpu.make_async_copy(rows_f.at[1], gin_o.at[1 - y], os.at[2])
    in_last.start()
    en_send.wait_recv()
    tmp_en[1] = back_en[1].astype(f32)
    en_last = pltpu.make_async_copy(tmp_en.at[1], gen_o.at[1 - y], os.at[3])
    en_last.start()

    f_mine = pl.ds(pl.multiple_of(d * 384, 128), 384)
    f_other = pl.ds(pl.multiple_of(384 - d * 384, 128), 384)
    put[3].wait_recv()
    put[4].wait_recv()
    ff_o[:, f_mine] = e1[...].astype(f32)
    ff_o[:, f_other] = x1[...].astype(f32)
    ff_o[:, pl.ds(D, D)] = e2[...].astype(f32) + x2[...].astype(f32)
    f_c1.wait_recv()
    f_c2.wait_recv()
    cr_o[:, mine] = fc[:, mine].astype(f32)
    cr_o[:, other] = xc1[...].astype(f32)
    cr_o[:, late] = fc[:, late].astype(f32) + xc2[...].astype(f32)
    zwait(0)
    sum_line(wide, a1.at[0, w], rzs1, keep(fs, mine))
    f_s1 = turn(9, fs.at[:, mine], xs1, line_x)
    f_s1.start()
    out_got.wait_recv()
    f_s2.wait_recv()
    se_o[:, mine] = fs[:, mine].astype(f32)
    se_o[:, late] = fs[:, late].astype(f32) + xs2[...].astype(f32)
    f_s1.wait_recv()
    se_o[:, other] = xs1[...].astype(f32)

    for copy in (in_local, en_local, in_last, en_last, loads[4]):
        copy.wait()
    for copy in (*cross, in_send, en_send, *put, y1, f_c1, f_c2, f_s1, f_s2):
        copy.wait_send()

    def finish(k):
        for path in range(4):
            zcopy(path, k).wait_send()
        for copy in small_line(k):
            copy.wait_send()

    loop(1, wide, finish)


def reduce_all(wide, se, c1, c2, e1, e2, outp, gxo, gxp, geo, gep, xf, d1, gain, gfeed, gcross, tg):
    rl = D // wide
    se = se.reshape(2, wide, rl, D)
    sem = pltpu.SemaphoreType.DMA
    V = pl.BlockSpec(memory_space=pltpu.VMEM)
    v = lambda *shape: pltpu.VMEM(shape, bf16)
    return pl.pallas_call(
        partial(reduce_kernel, wide),
        in_specs=[ANY, ANY, V, V, V, V, V, ANY, ANY, ANY, V, V, V, V, V, V],
        out_specs=[ANY, ANY, ANY, V, V, V, V, V],
        out_shape=[
            out((2, 256, D), bf16),
            out((2, 256, D), f32),
            out((2, 128, D), f32),
            out((8, D), f32),
            out((32, 128), f32),
            out((rl, 2 * D), f32),
            out((rl, D), f32),
            out((rl, D), f32),
        ],
        scratch_shapes=[
            v(2, wide, rl, 256),
            v(wide, rl, 256),
            v(2, wide, rl, 256),
            v(wide, rl, 256),
            v(wide, rl, 256),
            v(wide, rl, 256),
            v(wide, rl, 256),
            v(wide, rl, 256),
            v(wide, rl, 256),
            v(wide, rl, 256),
            v(wide, rl, 256),
            v(rl, D),
            v(rl, D),
            v(rl, 256),
            v(rl, 256),
            v(rl, 256),
            v(rl, 256),
            v(rl, 384),
            v(rl, D),
            v(2, 256, D),
            v(2, 128, D),
            v(256, D),
            pltpu.VMEM((2, 128, D), f32),
            v(256, D),
            v(2, 128, D),
            pltpu.VMEM((2, 256, D), f32),
            pltpu.VMEM((8, D), f32),
            pltpu.VMEM((32, 128), f32),
            pltpu.VMEM((3, 8, D), f32),
            pltpu.VMEM((3, 32, 128), f32),
            pltpu.VMEM((wide, 8, D), f32),
            pltpu.VMEM((wide, 32, 128), f32),
            sem((5,)),
            sem((5,)),
            sem((5,)),
            sem((10,)),
            sem((10,)),
            sem((4, wide)),
            sem((4, wide)),
            sem((2, 3 + wide)),
            sem((2, 3 + wide)),
            sem((4,)),
        ],
        compiler_params=pltpu.CompilerParams(
            collective_id=1, has_side_effects=True, vmem_limit_bytes=VMEM_LIMIT
        ),
        name="reduce_all",
    )(se, c1, c2, e1, e2, outp, gxo, gxp, geo, gep, xf, d1, gain, gfeed, gcross, tg)


def on_device(
    wide, hidden_in, encoder_out, cotangent, piece_starts, valid_lengths, bucket_table,
    gain_self, gain_cross, gain_feed, relative_bias, *mats
):
    me = lax.axis_index("narrow")
    sq, sk, sv, so, cq, ck, cv, co, gate, up, down = mats
    ps = jnp.concatenate((sq, so, sk, sv), axis=1)
    pc = jnp.concatenate((cq, co, ck, cv), axis=1)
    pf = jnp.concatenate((gate, up, down), axis=1)
    tab = jnp.pad(relative_bias.T, ((0, 29), (0, 96)))
    padded = jnp.pad(bucket_table, (0, 1), constant_values=-1)
    hot = (padded[None, :] == jnp.arange(BUCKETS)[:, None]).astype(f32)
    gains = [g.reshape(1, D) for g in (gain_self, gain_cross, gain_feed)]
    (
        xf, ws, wc, _, gff, ef, q, kv, at, p, cqh, ckv, cat, cp, h1, outp, d2, gg_feed,
    ) = forward(
        wide, piece_starts, valid_lengths, hidden_in[:, 0], encoder_out[:, 0], cotangent[:, 0], tab, hot, ps, pc, pf, *gains
    )
    ws, wc = (g.reshape(4, D, D) for g in (ws, wc))
    xs, es = xf.reshape(LEN, D), ef.reshape(ENC, D)
    gcr, d1, gg_cross, geo, gep, o1, o2 = cross_backward(wide, h1, es, d2, wc, gains[1], cqh, ckv, cat, cp, gff)
    gse, gxo, gxp, dl, c1, c2, e1, e2 = self_backward(wide, xs, d1, ws, gains[0], q, kv, at, p, gcr, o1, o2)
    tg = lax.dot_general(hot, dl.reshape(12, 2048), (((1,), (1,)), ((), ())), precision=precise)
    order = jnp.arange(12) // 3 ^ me ^ 1
    tg = tg.reshape(BUCKETS, 4, 3)
    tg = sum(jnp.where(order == k, jnp.tile(tg[:, k], (1, 4)), 0.0) for k in range(4))
    tg = jnp.pad(tg, ((0, 0), (0, 116)))
    two = lambda a: a.reshape(2, -1, D)
    outs, gin, gen, sg, st, f, b, a = reduce_all(
        wide, gse, c1, c2, e1, e2, two(outp), two(gxo), two(gxp), two(geo), two(gep), xf, two(d1), gains[0], gg_feed, gg_cross, tg
    )
    tg = lax.dynamic_slice_in_dim(st, me * 3, 3, axis=1)
    return (
        outs[:, None], gin[:, None], gen[:, None],
        sg[0], sg[1], sg[2], tg,
        a[:, :192], a[:, 384:576], a[:, 576:], a[:, 192:384],
        b[:, :192], b[:, 384:576], b[:, 576:], b[:, 192:384],
        f[:, :512], f[:, 512:1024], f[:, 1024:],
    )


def solution(mesh):
    rows = P(None, ("dp", "wide"), "narrow", None)
    mat = P("wide", "narrow")
    return jax.shard_map(
        partial(on_device, mesh.shape["wide"]),
        mesh=mesh,
        in_specs=(rows, rows, rows, P(None, ("dp", "wide")), P(None, ("dp", "wide")), P(), P(), P(), P(), P(None, "narrow"))
        + (mat,) * 11,
        out_specs=(rows, rows, rows, P(), P(), P(), P(None, "narrow")) + (mat,) * 11,
        check_vma=False,
    )
```

```python
import math
from functools import partial

import jax
import jax.numpy as jnp
from jax import lax
from jax.experimental import pallas as pl
from jax.experimental.pallas import tpu as pltpu
from jax.sharding import PartitionSpec as P

D = 768
HD = 192
HEADS = 12
DHEAD = 64
FFB = 512
BUCKETS = 32
LEN = 1024
ENC = 512
PIC = 256
TILES = 11
SPAN = 1280
ROWS = 16

precise = lax.Precision.HIGHEST
epsilon = 1e-06
masked_value = -1e30
f32 = jnp.float32
bf16 = jnp.bfloat16
MESH = pl.DeviceIdType.MESH
ANY = pl.BlockSpec(memory_space=pl.ANY)
VMEM_LIMIT = 60 << 20


def nn(a, b):
    return lax.dot_general(a, b, (((1,), (0,)), ((), ())), preferred_element_type=f32)


def nt(a, b):
    return lax.dot_general(a, b, (((1,), (1,)), ((), ())), preferred_element_type=f32)


def tn(a, b):
    return lax.dot_general(a, b, (((0,), (0,)), ((), ())), preferred_element_type=f32)


def rows_loop(total, step, body, unroll=1):
    def run(i, carry):
        body(pl.ds(pl.multiple_of(i * step, step), step))
        return carry

    lax.fori_loop(0, total // step, run, 0, unroll=unroll)


def normed(x, gain):
    factor = lax.rsqrt(jnp.mean(x * x, axis=1, keepdims=True) + epsilon)
    return x * factor * gain


def norm_back(x, gain, upstream):
    factor = lax.rsqrt(jnp.mean(x * x, axis=1, keepdims=True) + epsilon)
    weighted = upstream * gain
    inner = jnp.sum(weighted * x, axis=1, keepdims=True)
    dx = weighted * factor - x * (factor * factor * factor * inner * (1.0 / D))
    return dx, jnp.sum(upstream * x * factor, axis=0, keepdims=True)


def own_blocks():
    me = lax.axis_index("narrow")
    return (me, 3 - me)


def block_rows(blk):
    return pl.ds(pl.multiple_of(blk * 256, 256), 256)


def softmax_rows(v):
    e = jnp.exp(v - jnp.max(v, axis=1, keepdims=True))
    return e * (1.0 / jnp.sum(e, axis=1, keepdims=True))


def place_here():
    d, w, n = lax.axis_index("dp"), lax.axis_index("wide"), lax.axis_index("narrow")
    return d, w, n, n + 1 - 2 * lax.rem(n, 2), lax.rem(n + 2, 4), 3 - n


def remote(src, dst, send, recv, dev):
    return pltpu.make_async_remote_copy(
        src_ref=src, dst_ref=dst, send_sem=send, recv_sem=recv, device_id=dev, device_id_type=MESH
    )


def greet(devs, wide=1):
    d, w, n = place_here()[:3]
    barrier = pltpu.get_barrier_semaphore()
    for dev in devs:
        pl.semaphore_signal(barrier, inc=1, device_id=dev, device_id_type=MESH)

    def line(k, carry):
        dev = (d, lax.rem(w + k, wide), n)
        pl.semaphore_signal(barrier, inc=1, device_id=dev, device_id_type=MESH)
        return carry

    lax.fori_loop(1, wide, line, 0)
    pl.semaphore_wait(barrier, wide - 1 + len(devs))


def loop(lo, hi, body):
    def run(k, carry):
        body(k)
        return carry

    lax.fori_loop(lo, hi, run, 0)


def add_into(dst, src):
    shape = dst.shape
    rl = shape[-2]
    step = 64 if rl % 64 == 0 else rl
    lead = shape[:-2]

    def one(*index):
        for j in range(rl // step):
            spot = index + (slice(j * step, (j + 1) * step), slice(None))
            dst[spot] = dst[spot] + src[spot]

    if len(lead) == 1:
        loop(0, lead[0], one)
    else:
        for i in range(lead[0]):
            loop(0, lead[1], partial(one, i))


def sum_line(wide, own, parts, store):
    w = lax.axis_index("wide")
    rl = own.shape[0]
    step = 64 if rl % 64 == 0 else rl
    for j in range(rl // step):
        r = slice(j * step, (j + 1) * step)

        def add(k, total, r=r):
            return total + parts[lax.rem(w + k, wide), r, :].astype(f32)

        store(r, lax.fori_loop(1, wide, add, own[r, :].astype(f32)))


def core_devs():
    d, w, n, pn, yn, dn = place_here()
    return (d, w, pn)


class CoreSum:
    def __init__(self, step, buf, landed, send, recv):
        self.step, self.buf, self.landed, self.send, self.recv = step, buf, landed, send, recv
        self.side = step // 2

    def copy(self):
        return remote(
            self.buf.at[0], self.landed.at[self.side], self.send.at[0], self.recv.at[self.side], core_devs()
        )

    def finish(self, result):
        @pl.when(lax.rem(self.step, 2) == 0)
        def _():
            self.copy().start()

        @pl.when(lax.rem(self.step, 2) == 1)
        def _():
            self.copy().wait_recv()

            def add(r):
                result[0, r, :] = self.buf[1, r, :] + self.landed[self.side, r, :]

            rows_loop(D, 64, add)
            self.copy().wait_send()


def whole(shape):
    zero = (0,) * len(shape)
    return pl.BlockSpec(shape, lambda n: zero)


def slab(shape):
    zero = (0,) * len(shape)
    return pl.BlockSpec((1,) + shape, lambda n: (n,) + zero)


def pair_slab(shape):
    zero = (0,) * len(shape)
    return pl.BlockSpec((1,) + shape, lambda n: (n // 2,) + zero)


def params(collective_id=None):
    if collective_id is None:
        return pltpu.CompilerParams(dimension_semantics=("arbitrary",), vmem_limit_bytes=VMEM_LIMIT)
    return pltpu.CompilerParams(
        dimension_semantics=("arbitrary",),
        vmem_limit_bytes=VMEM_LIMIT,
        collective_id=collective_id,
        has_side_effects=True,
    )


def out(shape, dtype):
    return jax.ShapeDtypeStruct(shape, dtype)


SMEM = pl.BlockSpec(memory_space=pltpu.SMEM)


def cost(gflop):
    return pl.CostEstimate(flops=int(gflop * 1e9), bytes_accessed=20 << 20, transcendentals=0)


GELU_A = 0.7978845608028654
GELU_B = 0.044715


FORWARD_VMEM = 58 << 20
ORDER_ATT = (1, 0, 3, 2)
ORDER_FEED = (1, 0, 2, 3)


def pick(order, k):
    index = order[3]
    for i in (2, 1, 0):
        index = jnp.where(k == i, order[i], index)
    return index


def forward_kernel(
    wide, ps_s, vl_s, hid, enc, cot, tab, hot, ps, pc, pf, gain_s, gain_c, gain_f,
    xf, gs, gc, gf, gff, ef, q1, kv1, at1, p1, q2, kv2, at2, p2, h1, out_o, d2_o, gg_o,
    wbuf, stage, xv, ev, tabs, off, nf, mask, tb, s, h2, nc, nct, cv, ct, gu, da, act, dgu, acc, buf, landed,
    ls, ins, inr, ws, vs, zs, zr, ys, yr, xs, xr, cs, cr, fsend, frecv, fout,
):
    step = pl.program_id(0)
    d, w, n, pn, yn, dn = place_here()
    y = n // 2
    blks = (n, dn)
    rl = ps.shape[0]
    groups = ((ps, gs, 0, 768, True), (pc, gc, 0, 768, True), (pf, gf, 0, 1024, True), (pf, gf, 1024, 512, False))
    keep, give = (1, 3), (0, 2)
    diag, pair, line_x, line_y = (d, w, dn), (d, w, pn), (1 - d, w, n), (d, w, yn)

    def cols(g, which):
        start, width, split = groups[g][2:]
        if which == 2 or not split:
            return pl.ds(start, width)
        half = width // 2
        pos = d if which == 0 else 1 - d
        return pl.ds(pl.multiple_of(start + pos * half, 128), half)

    def own(g, which):
        return groups[g][0].at[:, cols(g, which)]

    def spot(g, slot, row, which):
        return groups[g][1].at[slot, row, :, cols(g, which)]

    def zcopy(g, k):
        dev = (d, lax.rem(w + k, wide), n)
        if g == 4:
            ref = spot(3, 3, w, 0)
            return remote(ref, ref, zs.at[4, k], zr.at[4, w], dev)
        return remote(own(g, 0), spot(g, 1, w, 0), zs.at[g, k], zr.at[g, w], dev)

    def zgot(g, row):
        ref = spot(3, 3, row, 0) if g == 4 else spot(g, 1, row, 0)
        return remote(ref, ref, zs.at[g, 0], zr.at[g, row], line_x)

    def ycopy(g, row, src=None):
        ref = spot(g, 1, row, 0)
        return remote(ref if src is None else src, spot(g, 3, row, 0), ys.at[g, row], yr.at[g, row], line_y)

    def ygot(g, row):
        return remote(spot(g, 3, row, 0), spot(g, 3, row, 0), ys.at[g, row], yr.at[g, row], line_y)

    def xcopy(g, side, row):
        ref = spot(g, keep[side], row, 0)
        return remote(ref, ref, xs.at[g, side, row], xr.at[g, side, row], line_x)

    def xgot(g, side, row):
        ref = spot(g, keep[side], row, 1)
        return remote(ref, ref, xs.at[g, side, row], xr.at[g, side, row], line_x)

    def ccopy(g, side, row, src=None):
        ref = spot(g, keep[side], row, 2)
        return remote(
            ref if src is None else src, spot(g, give[side], row, 2), cs.at[g, side, row], cr.at[g, side, row], pair
        )

    def cgot(g, side, row):
        ref = spot(g, give[side], row, 2)
        return remote(ref, ref, cs.at[g, side, row], cr.at[g, side, row], pair)

    def around(first, body):
        loop(first, wide, lambda k: body(lax.rem(w + k, wide)))

    def zsend(g):
        loop(1, wide, lambda k: zcopy(g, k).start())

    def own_sends(g):
        ycopy(g, w, own(g, 0)).start()
        ccopy(g, 0, w, own(g, 2)).start()

    def zpass(g, then):
        def one(row):
            zgot(g, row).wait_recv()
            for nxt in then:
                nxt(row).start()

        around(1, one)

    def ypass(g):
        def one(row):
            ygot(g, row).wait_recv()
            xcopy(g, 1, row).start()

        around(0, one)

    def xsend(g):
        around(1, lambda row: xcopy(g, 0, row).start())

    def xstep(g, side):
        def one(k):
            row = lax.rem(w + k, wide)
            xgot(g, side, row).wait_recv()
            ccopy(g, side, row).start()

        loop(1 - side, wide, one)

    def cwait(g, side):
        loop(0, wide, lambda k: cgot(g, side, lax.rem(w + k, wide)).wait_recv())

    straight = rl % 16 == 0
    many = 16 // math.gcd(rl, 16)

    def slab_copies(ref, slot, b):
        width = ref.shape[-1]
        if straight:
            return [
                pltpu.make_async_copy(
                    ref.at[slot, k], wbuf.at[b, pl.ds(k * rl, rl), pl.ds(0, width)], ws.at[b, k]
                )
                for k in range(wide)
            ]
        return [pltpu.make_async_copy(ref.at[slot], stage.at[:, :, pl.ds(0, width)], ws.at[b, 0])]

    def fetch(ref, slot, b):
        for copy in slab_copies(ref, slot, b):
            copy.start()

    def fetched(ref, slot, b):
        for copy in slab_copies(ref, slot, b):
            copy.wait()
        if not straight:
            width = ref.shape[-1]
            for k in range(0, wide, many):
                part = jnp.concatenate([stage[k + i, :, 0:width].astype(f32) for i in range(many)], axis=0)
                wbuf[b, k * rl : (k + many) * rl, 0:width] = part.astype(bf16)

    local = [
        pltpu.make_async_copy(src, dst, ls.at[i])
        for i, (src, dst) in enumerate(
            (
                (ps, gs.at[1, w]),
                (pc, gc.at[1, w]),
                (pf, gf.at[1, w]),
                (hid.at[y], xv.at[n]),
                (enc.at[y], ev.at[n]),
                (cot.at[y], cv.at[0]),
            )
        )
    ]
    back = [pltpu.make_async_copy(xv, xf, vs.at[0]), pltpu.make_async_copy(ev, ef, vs.at[1])]
    early = [
        remote(tab, tabs.at[0], ins.at[3], inr.at[3], pair),
        remote(tab, tabs.at[3], ins.at[4], inr.at[4], line_y),
        remote(tab, tabs.at[2], ins.at[5], inr.at[5], diag),
        remote(hid.at[1 - y], xv.at[n], ins.at[0], inr.at[0], diag),
        remote(hid.at[y], xv.at[n], ins.at[6], inr.at[6], pair),
    ]
    middle = [
        remote(enc.at[1 - y], ev.at[n], ins.at[1], inr.at[1], diag),
        remote(enc.at[y], ev.at[n], ins.at[7], inr.at[7], pair),
        remote(cot.at[1 - y], cv.at[1], ins.at[2], inr.at[2], diag),
    ]
    later = [
        remote(xv.at[dn], xv.at[dn], ins.at[8], inr.at[8], pair),
        remote(ev.at[dn], ev.at[dn], ins.at[9], inr.at[9], pair),
    ]

    def arrived(i, ref):
        remote(ref, ref, ins.at[i], inr.at[i], pair).wait_recv()

    @pl.when(step == 0)
    def _():
        for copy in local:
            copy.start()
        greet((pair, line_y, diag, line_x), wide)
        for copy in early:
            copy.start()
        zsend(0)
        own_sends(0)
        tabs[1] = tab[...]
        start, length = ps_s[y, 0], vl_s[y, 0]
        for i in range(2):

            def mask_rows(r, i=i):
                shape = (32, LEN)
                qi = blks[i] * 256 + r.start + lax.broadcasted_iota(jnp.int32, shape, 0)
                kj = lax.broadcasted_iota(jnp.int32, shape, 1)
                inside = (qi >= start) & (qi < start + PIC) & (kj >= start) & (kj < start + PIC)
                allowed = ((kj <= qi) | inside) & (kj < length)
                mask[pl.ds(i * 256 + r.start, 32), :] = jnp.where(allowed, 0.0, masked_value)

            rows_loop(256, 32, mask_rows, unroll=2)
        arrived(6, xv.at[pn])
        arrived(0, xv.at[dn])
        later[0].start()
        zpass(0, (lambda row: ycopy(0, row), lambda row: xcopy(0, 0, row)))
        zsend(1)
        arrived(8, xv.at[yn])
        local[3].wait()
        back[0].start()
        arrived(3, tabs.at[0])
        arrived(4, tabs.at[3])
        arrived(5, tabs.at[2])
        for i in range(4):

            def norm_rows(r, i=i):
                nf[pl.ds(i * 256 + r.start, 64), :] = normed(xv[i, r, :].astype(f32), gain_s[...]).astype(bf16)

            rows_loop(256, 64, norm_rows, unroll=4)
        for i in range(2):
            h1[i * 256 : (i + 1) * 256, :] = xv[blks[i]].astype(f32)
        xstep(0, 0)
        ypass(0)
        own_sends(1)
        middle[0].start()
        middle[1].start()
        for i in range(3):
            local[i].wait()
        fetch(gs, 1, 0)

    @pl.when(step < 4)
    def _():
        b = lax.rem(step, 2)
        slot = pick(ORDER_ATT, step)
        fetched(gs, slot, b)
        off[...] = lax.dot_general(
            tabs[slot, 0:8, 0:BUCKETS], hot[...], (((1,), (0,)), ((), ())), precision=precise, preferred_element_type=f32
        )
        kv1[0] = nn(nf[...], wbuf[b, :, 384:768]).astype(bf16).T
        for i in range(2):
            q1[0, i * 256 : (i + 1) * 256, :] = nn(nf[block_rows(blks[i]), :], wbuf[b, :, 0:192]).astype(bf16)
        for h in range(3):
            for t in range(TILES):
                line = jnp.broadcast_to(off[h : h + 1, 128 * t : 128 * t + 256], (128, 256))
                tb[t] = pltpu.roll(line, 129, 1, stride=1, stride_axis=0)[:, :128]
            hs = slice(h * DHEAD, (h + 1) * DHEAD)
            vs_ = slice(HD + h * DHEAD, HD + (h + 1) * DHEAD)
            for i in range(2):
                s[...] = nn(q1[0, i * 256 : (i + 1) * 256, hs], kv1[0, hs, :])
                for r in range(2):
                    idx = [jnp.minimum(kb - 2 * blks[i] - r, 3) + 7 for kb in range(8)]

                    def soft_rows(rr, i=i, r=r, h=h, idx=idx):
                        bias = jnp.concatenate([tb[idx[kb], rr, :] for kb in range(8)], axis=1)
                        v = s[pl.ds(r * 128 + rr.start, ROWS), :] + bias
                        v = v + mask[pl.ds(i * 256 + r * 128 + rr.start, ROWS), :]
                        p1[0, h, pl.ds(i * 256 + r * 128 + rr.start, ROWS), :] = softmax_rows(v).astype(bf16)

                    rows_loop(128, ROWS, soft_rows, unroll=8)
                at1[0, i * 256 : (i + 1) * 256, hs] = nt(
                    p1[0, h, i * 256 : (i + 1) * 256, :], kv1[0, vs_, :]
                ).astype(bf16)
        h1[...] += nt(at1[0], wbuf[b, :, 192:384])

    @pl.when(step == 0)
    def _():
        cwait(0, 0)
        fetch(gs, 0, 1)
        zpass(1, (lambda row: ycopy(1, row),))
        zsend(2)
        own_sends(2)
        own_sends(3)

    @pl.when(step == 1)
    def _():
        xstep(0, 1)
        fetch(gs, 3, 0)
        xsend(1)
        middle[2].start()

    @pl.when(step == 2)
    def _():
        cwait(0, 1)
        fetch(gs, 2, 1)
        ypass(1)
        zpass(2, (lambda row: ycopy(2, row),))
        zsend(3)
        ygot(3, w).wait_recv()
        ccopy(3, 1, w).start()
        zsend(4)

    @pl.when(step == 3)
    def _():
        xstep(1, 0)
        fetch(gc, 1, 0)
        xsend(2)
        arrived(1, ev.at[dn])
        later[1].start()
        arrived(7, ev.at[pn])
        arrived(9, ev.at[yn])
        local[4].wait()
        back[1].start()

        def norm_rows(r):
            x = h1[r, :]
            nc[r, :] = normed(x, gain_c[...]).astype(bf16)
            h2[r, :] = x

        rows_loop(512, 64, norm_rows, unroll=4)

    @pl.when((step >= 4) & (step < 8))
    def _():
        b = lax.rem(step, 2)
        fetched(gc, pick(ORDER_ATT, step - 4), b)
        kv2[0] = nn(ev[...].reshape(ENC, D), wbuf[b, :, 384:768]).astype(bf16).T
        q2[0] = nn(nc[...], wbuf[b, :, 0:192]).astype(bf16)
        for h in range(3):
            hs = slice(h * DHEAD, (h + 1) * DHEAD)
            vs_ = slice(HD + h * DHEAD, HD + (h + 1) * DHEAD)
            gu[:, 0:ENC] = nn(q2[0, :, hs], kv2[0, hs, :])

            def soft_rows(r, h=h):
                p2[0, h, r, :] = softmax_rows(gu[r, 0:ENC]).astype(bf16)

            rows_loop(512, 16, soft_rows, unroll=32)
            at2[0, :, hs] = nt(p2[0, h], kv2[0, vs_, :]).astype(bf16)
        h2[...] += nt(at2[0], wbuf[b, :, 192:384])

    @pl.when(step == 4)
    def _():
        cwait(1, 0)
        fetch(gc, 0, 1)

    @pl.when(step == 5)
    def _():
        xstep(1, 1)
        fetch(gc, 3, 0)
        ypass(2)

    @pl.when(step == 6)
    def _():
        cwait(1, 1)
        fetch(gc, 2, 1)

    @pl.when(step == 7)
    def _():
        xstep(2, 0)
        zpass(3, (lambda row: ccopy(3, 0, row),))
        fetch(gf, 1, 0)
        arrived(2, cv.at[1])
        local[5].wait()

        def norm_rows(r):
            x = h2[r, :]
            nc[r, :] = normed(x, gain_f[...]).astype(bf16)
            acc[r, :] = x
            d2_o[r, :] = jnp.zeros((64, D), f32)

        rows_loop(512, 64, norm_rows, unroll=4)
        nct[...] = nc[...].T
        ct[...] = cv[...].reshape(512, D).T

    def give_copy(side):
        return remote(buf.at[0], landed.at[side], fsend.at[side], frecv.at[side], pair)

    def put_out(side):
        return pltpu.make_async_copy(buf.at[1], gff.at[side], fout.at[side])

    def add_side(side):
        give_copy(side).wait_recv()

        def add(r):
            buf[1, r, :] = buf[1, r, :] + landed[side, r, :]

        rows_loop(D, 64, add)
        put_out(side).start()

    @pl.when(step >= 8)
    def _():
        b = lax.rem(step, 2)
        fetched(gf, pick(ORDER_FEED, step - 8), b)
        gu[...] = nn(nc[...], wbuf[b, :, : 2 * FFB])
        da[...] = nn(cv[...].reshape(512, D), wbuf[b, :, 2 * FFB :])

        def gelu_rows(r):
            gate = gu[r, :FFB]
            up = gu[r, FFB:]
            d_act = da[r, :]
            sq = gate * gate
            th = jnp.tanh(GELU_A * gate * (1.0 + GELU_B * sq))
            half = 0.5 + 0.5 * th
            gelu = gate * half
            slope = half + 0.5 * GELU_A * gate * (1.0 - th * th) * (1.0 + 3.0 * GELU_B * sq)
            act[r, :] = (gelu * up).astype(bf16)
            dgu[r, :FFB] = (d_act * up * slope).astype(bf16)
            dgu[r, FFB:] = (d_act * gelu).astype(bf16)

        rows_loop(512, 16, gelu_rows, unroll=32)
        acc[...] += nt(act[...], wbuf[b, :, 2 * FFB :])
        d2_o[...] += nt(dgu[...], wbuf[b, :, : 2 * FFB])

        @pl.when(step == 10)
        def _():
            give_copy(0).wait_send()

        @pl.when(step == 11)
        def _():
            put_out(0).wait()

        place = jnp.where((step == 8) | (step == 11), 1, 0)
        buf[place, :, : 2 * FFB] = nn(nct[...], dgu[...]).astype(bf16)
        buf[place, :, 2 * FFB :] = nn(ct[...], act[...]).astype(bf16)

    @pl.when(step == 8)
    def _():
        cwait(2, 0)
        cwait(3, 0)
        fetch(gf, 0, 1)

    @pl.when(step == 9)
    def _():
        give_copy(0).start()
        zpass(4, (lambda row: ccopy(3, 1, row),))
        xstep(2, 1)
        cwait(2, 1)
        cwait(3, 1)
        fetch(gf, 2, 0)

    @pl.when(step == 10)
    def _():
        give_copy(1).start()
        fetch(gf, 3, 1)
        add_side(0)

    @pl.when(step == 11)
    def _():
        add_side(1)
        gg_o[...] = jnp.zeros((1, D), f32)

        for i in range(2):

            def back_rows(r, i=i):
                rows = pl.ds(i * 256 + r.start, 64)
                dx, gg = norm_back(h2[rows, :], gain_f[...], d2_o[rows, :])
                d2_o[rows, :] = cv[i, r, :].astype(f32) + dx
                gg_o[...] += gg
                out_o[rows, :] = acc[rows, :].astype(bf16)

            rows_loop(256, 64, back_rows, unroll=2)
        for copy in back:
            copy.wait()
        put_out(1).wait()
        give_copy(1).wait_send()
        for copy in early + middle + later:
            copy.wait_send()

        def finish(row):
            for g in range(4):
                for side in range(2):
                    ccopy(g, side, row).wait_send()
            for g in range(3):
                ycopy(g, row).wait_send()
                xcopy(g, 1, row).wait_send()

        around(0, finish)
        ycopy(3, w).wait_send()

        def finish_line(k):
            row = lax.rem(w + k, wide)
            for g in range(5):
                zcopy(g, k).wait_send()
            for g in range(3):
                xcopy(g, 0, row).wait_send()

        loop(1, wide, finish_line)


def forward(wide, ps_s, vl_s, hid, enc, cot, tab, hot, ps, pc, pf, gain_s, gain_c, gain_f):
    rl = ps.shape[0]
    sem = pltpu.SemaphoreType.DMA
    V = pl.BlockSpec(memory_space=pltpu.VMEM)

    def turn(first, shape):
        zero = (0,) * len(shape)
        return pl.BlockSpec(
            (1,) + shape, lambda n: (pick(ORDER_ATT, jnp.clip(n - first, 0, 3)),) + zero
        )

    v = lambda *shape: pltpu.VMEM(shape, bf16)
    vf = lambda *shape: pltpu.VMEM(shape, f32)
    return pl.pallas_call(
        partial(forward_kernel, wide),
        grid=(12,),
        in_specs=[SMEM, SMEM, ANY, ANY, ANY, V, V, V, V, V, V, V, V],
        out_specs=[ANY] * 6
        + [turn(0, (512, HD)), turn(0, (2 * HD, LEN)), turn(0, (512, HD)), turn(0, (3, 512, LEN))]
        + [turn(4, (512, HD)), turn(4, (2 * HD, ENC)), turn(4, (512, HD)), turn(4, (3, 512, ENC))]
        + [V, V, V, V],
        out_shape=[
            out((4, 256, D), bf16),
            out((4, wide, rl, D), bf16),
            out((4, wide, rl, D), bf16),
            out((4, wide, rl, 2 * D), bf16),
            out((2, D, 3 * FFB), bf16),
            out((4, 128, D), bf16),
            out((4, 512, HD), bf16),
            out((4, 2 * HD, LEN), bf16),
            out((4, 512, HD), bf16),
            out((4, 3, 512, LEN), bf16),
            out((4, 512, HD), bf16),
            out((4, 2 * HD, ENC), bf16),
            out((4, 512, HD), bf16),
            out((4, 3, 512, ENC), bf16),
            out((512, D), f32),
            out((512, D), bf16),
            out((512, D), f32),
            out((1, D), f32),
        ],
        scratch_shapes=[
            v(2, D, 3 * FFB),
            v(wide, rl, 3 * FFB) if rl % 16 else v(16, 128),
            v(4, 256, D),
            v(4, 128, D),
            vf(4, 32, 128),
            vf(8, 2048),
            v(LEN, D),
            vf(512, LEN),
            vf(TILES, 128, 128),
            vf(256, LEN),
            vf(512, D),
            v(512, D),
            v(D, 512),
            v(2, 256, D),
            v(D, 512),
            vf(512, 2 * FFB),
            vf(512, FFB),
            v(512, FFB),
            v(512, 2 * FFB),
            vf(512, D),
            v(2, D, 3 * FFB),
            v(2, D, 3 * FFB),
            sem((6,)),
            sem((10,)),
            sem((10,)),
            sem((2, wide)),
            sem((2,)),
            sem((5, wide)),
            sem((5, wide)),
            sem((4, wide)),
            sem((4, wide)),
            sem((4, 2, wide)),
            sem((4, 2, wide)),
            sem((4, 2, wide)),
            sem((4, 2, wide)),
            sem((2,)),
            sem((2,)),
            sem((2,)),
        ],
        compiler_params=pltpu.CompilerParams(
            dimension_semantics=("arbitrary",), vmem_limit_bytes=FORWARD_VMEM, collective_id=0, has_side_effects=True
        ),
        cost_estimate=cost(60),
        name="forward",
    )(ps_s, vl_s, hid, enc, cot, tab, hot, ps, pc, pf, gain_s, gain_c, gain_f)


def cross_backward_kernel(
    h1, ef, d2, w, gain, q, kv, at, p, gff,
    gw_o, d1_o, gg_o, ge_o, gep_o, o1, o2,
    d2b, d2t, nct, eft, get, do, dp, ds, dq, dkv, buf, landed, rx, ry, send, recv, load, fs, fr,
):
    n = pl.program_id(0)
    slot = lax.rem(n, 2)
    core = CoreSum(n, buf, landed, send, recv)
    d, wi, me, pn, yn, dn = place_here()
    y = me // 2
    mine = pl.ds(pl.multiple_of(d * 384, 128), 384)
    other = pl.ds(pl.multiple_of(384 - d * 384, 128), 384)
    late = pl.ds(D, D)
    loads = [
        pltpu.make_async_copy(gff.at[:, :, :, mine], o1, load.at[0]),
        pltpu.make_async_copy(gff.at[0, :, :, late], o2, load.at[1]),
    ]
    sends = [
        remote(gff.at[:, :, :, other], rx, fs.at[0], fr.at[0], (1 - d, wi, me)),
        remote(gff.at[1, :, :, late], ry, fs.at[1], fr.at[1], (d, wi, yn)),
    ]

    @pl.when(n == 0)
    def _():
        def norm_rows(r):
            d2b[r, :] = d2[r, :].astype(bf16)
            d1_o[r, :] = jnp.zeros((64, D), f32)
            dp[r, :] = normed(h1[r, :], gain[...])

        for copy in loads:
            copy.start()
        greet(((d, wi, pn), (d, wi, yn), (1 - d, wi, me)))
        for copy in sends:
            copy.start()
        rows_loop(512, 64, norm_rows, unroll=4)
        nct[...] = dp[...].astype(bf16).T
        d2t[...] = d2b[...].T
        eft[...] = ef[...].T
        get[...] = jnp.zeros((D, ENC), f32)

    do[...] = nn(d2b[...], w[0, :, 192:384]).astype(bf16)
    for h in range(3):
        hs = slice(h * DHEAD, (h + 1) * DHEAD)
        vs = slice(HD + h * DHEAD, HD + (h + 1) * DHEAD)
        dp[:, :ENC] = nn(do[:, hs], kv[0, vs, :])

        def grad_rows(r, h=h, hs=hs):
            delta = jnp.sum(do[r, hs].astype(f32) * at[0, r, hs].astype(f32), axis=1, keepdims=True)
            ds[r, :] = (p[0, h, r, :].astype(f32) * (dp[r, :ENC] - delta)).astype(bf16)

        rows_loop(512, 16, grad_rows, unroll=32)
        dq[:, hs] = nt(ds[...], kv[0, hs, :]).astype(bf16)
        dkv[hs, :] = tn(q[0, :, hs], ds[...]).astype(bf16)
        dkv[vs, :] = tn(do[:, hs], p[0, h]).astype(bf16)
    d1_o[...] += nt(dq[...], w[0, :, 0:192])
    get[...] += nn(w[0, :, 384:768], dkv[...])
    buf[slot, :, 0:384] = jnp.concatenate([nn(nct[...], dq[...]), nn(d2t[...], at[0])], axis=1).astype(bf16)
    buf[slot, :, 384:768] = nt(eft[...], dkv[...]).astype(bf16)
    core.finish(gw_o)

    @pl.when(n == 3)
    def _():
        gg_o[...] = jnp.zeros((1, D), f32)

        def back_rows(r):
            dx, gg = norm_back(h1[r, :], gain[...], d1_o[r, :])
            d1_o[r, :] = d2[r, :] + dx
            gg_o[...] += gg

        rows_loop(512, 64, back_rows, unroll=2)
        for i in range(2):
            half = slice(i * 128, (i + 1) * 128)
            cols = lambda blk: pl.ds(pl.multiple_of(blk * 128, 128), 128)
            ge_o[half, :] = get[:, cols((me, 3 - me)[i])].T
            gep_o[half, :] = get[:, cols((pn, 3 - pn)[i])].T.astype(bf16)
        for copy in loads:
            copy.wait()
        for copy in sends:
            copy.wait()
        add_into(o1, rx)
        add_into(o2, ry)


def cross_backward(wide, h1, ef, d2, w, gain, q, kv, at, p, gff):
    rl = D // wide
    return pl.pallas_call(
        cross_backward_kernel,
        grid=(4,),
        in_specs=[
            whole((512, D)),
            whole((ENC, D)),
            whole((512, D)),
            slab((D, D)),
            whole((1, D)),
            slab((512, HD)),
            slab((2 * HD, ENC)),
            slab((512, HD)),
            slab((3, 512, ENC)),
            ANY,
        ],
        out_specs=[
            pair_slab((D, D)),
            whole((512, D)),
            whole((1, D)),
            whole((256, D)),
            whole((256, D)),
            whole((2, wide, rl, 384)),
            whole((wide, rl, D)),
        ],
        out_shape=[
            out((2, D, D), bf16),
            out((512, D), f32),
            out((1, D), f32),
            out((256, D), f32),
            out((256, D), bf16),
            out((2, wide, rl, 384), bf16),
            out((wide, rl, D), bf16),
        ],
        scratch_shapes=[
            pltpu.VMEM((512, D), bf16),
            pltpu.VMEM((D, 512), bf16),
            pltpu.VMEM((D, 512), bf16),
            pltpu.VMEM((D, ENC), bf16),
            pltpu.VMEM((D, ENC), f32),
            pltpu.VMEM((512, HD), bf16),
            pltpu.VMEM((512, D), f32),
            pltpu.VMEM((512, ENC), bf16),
            pltpu.VMEM((512, HD), bf16),
            pltpu.VMEM((2 * HD, ENC), bf16),
            pltpu.VMEM((2, D, D), bf16),
            pltpu.VMEM((2, D, D), bf16),
            pltpu.VMEM((2, wide, rl, 384), bf16),
            pltpu.VMEM((wide, rl, D), bf16),
            pltpu.SemaphoreType.DMA((1,)),
            pltpu.SemaphoreType.DMA((2,)),
            pltpu.SemaphoreType.DMA((2,)),
            pltpu.SemaphoreType.DMA((2,)),
            pltpu.SemaphoreType.DMA((2,)),
        ],
        compiler_params=params(3),
        cost_estimate=cost(14),
        name="cross_backward",
    )(h1, ef, d2, w, gain, q, kv, at, p, gff.reshape(2, wide, rl, 3 * FFB))


def self_backward_kernel(
    wide, xf, d1, w, gain, q, kv, at, p, gcr, o1, o2, outp,
    gw_o, g_o, gp_o, dl_o, b1, c2, e1, e2, out_o,
    c1, cy1, d1b, d1t, nft, nqt, gt, gq, do, dp, ds, dq, dkv, buf, landed, s1, f2, rx, ry, ry1, rz1, rz2,
    send, recv, load, fs, fr, zs, zr,
):
    n = pl.program_id(0)
    blks = own_blocks()
    slot = lax.rem(n, 2)
    core = CoreSum(n, buf, landed, send, recv)
    d, wi, me, pn, yn, dn = place_here()
    y = me // 2
    mine = pl.ds(pl.multiple_of(d * 256, 128), 256)
    other = pl.ds(pl.multiple_of(256 - d * 256, 128), 256)
    late = pl.ds(512, 256)
    loads = [
        pltpu.make_async_copy(gcr.at[:, :, :, mine], c1, load.at[0]),
        pltpu.make_async_copy(gcr.at[0, :, :, late], c2, load.at[1]),
        pltpu.make_async_copy(o1.at[0], s1, load.at[2]),
        pltpu.make_async_copy(o2.at[wi], f2, load.at[3]),
        pltpu.make_async_copy(outp.at[0], out_o.at[y], load.at[4]),
    ]
    sends = [
        remote(o1.at[1], ry1, fs.at[0], fr.at[0], (d, wi, yn)),
        remote(gcr.at[:, :, :, other], rx, fs.at[1], fr.at[1], (1 - d, wi, me)),
        remote(gcr.at[1, :, :, late], ry, fs.at[2], fr.at[2], (d, wi, yn)),
        remote(outp.at[1], out_o.at[y], fs.at[3], fr.at[3], (d, wi, dn)),
    ]
    out_got = remote(out_o.at[1 - y], out_o.at[1 - y], fs.at[3], fr.at[3], (d, wi, dn))
    y_cross = remote(c1.at[1], cy1, fs.at[4], fr.at[4], (d, wi, yn))

    def zcopy(path, k):
        row = lax.rem(wi + k, wide)
        src, dst = ((s1, rz1), (o2, rz2))[path]
        return remote(src.at[row], dst.at[wi], zs.at[path, k], zr.at[path, wi], (d, row, me))

    def zgot(path, k):
        row = lax.rem(wi + k, wide)
        ref = (rz1, rz2)[path].at[row]
        return remote(ref, ref, zs.at[path, k], zr.at[path, row], (d, row, me))

    @pl.when(n == 0)
    def _():
        def cast_rows(r):
            d1b[r, :] = d1[r, :].astype(bf16)
            gq[r, :] = jnp.zeros((64, D), f32)

        for copy in loads:
            copy.start()
        greet(((d, wi, pn), (d, wi, yn), (1 - d, wi, me), (d, wi, dn)), wide)
        for copy in sends[:3]:
            copy.start()
        loop(1, wide, lambda k: zcopy(1, k).start())
        rows_loop(512, 64, cast_rows)
        d1t[...] = d1b[...].T
        for i in range(4):
            part = normed(xf[i * 256 : (i + 1) * 256, :].astype(f32), gain[...]).astype(bf16)
            nft[:, i * 256 : (i + 1) * 256] = part.T
        for i in range(2):
            part = normed(xf[block_rows(blks[i]), :].astype(f32), gain[...]).astype(bf16)
            nqt[:, i * 256 : (i + 1) * 256] = part.T
        gt[...] = jnp.zeros((D, LEN), f32)

    @pl.when(n == 2)
    def _():
        loads[2].wait()
        sends[0].wait_recv()
        add_into(s1, ry1)
        loop(1, wide, lambda k: zcopy(0, k).start())
        sends[3].start()

    @pl.when(n == 3)
    def _():
        loads[0].wait()
        sends[1].wait_recv()
        add_into(c1, rx)
        y_cross.start()

    dl_o[0] = jnp.zeros((3, 2048), f32)
    do[...] = nn(d1b[...], w[0, :, 192:384]).astype(bf16)
    for h in range(3):
        hs = slice(h * DHEAD, (h + 1) * DHEAD)
        vs = slice(HD + h * DHEAD, HD + (h + 1) * DHEAD)
        dk = jnp.zeros((DHEAD, LEN), f32)
        dv = jnp.zeros((DHEAD, LEN), f32)
        for i in range(2):
            half = slice(i * 256, (i + 1) * 256)
            dp[...] = nn(do[half, hs], kv[0, vs, :])

            def grad_rows(rr, i=i, h=h, hs=hs):
                rows = pl.ds(i * 256 + rr.start, ROWS)
                delta = jnp.sum(do[rows, hs].astype(f32) * at[0, rows, hs].astype(f32), axis=1, keepdims=True)
                ds[rr, :] = (p[0, h, rows, :].astype(f32) * (dp[rr, :] - delta)).astype(bf16)

            rows_loop(256, ROWS, grad_rows, unroll=16)
            upper, lower = ds[:128, :].astype(f32), ds[128:, :].astype(f32)
            part = jnp.concatenate(
                [
                    upper[:, :896] + lower[:, 128:],
                    upper[:, 896:],
                    jnp.zeros((128, 128), f32),
                    lower[:, :128],
                ],
                axis=1,
            )
            height = 128
            while height > 1:
                height //= 2
                part = part[:height] + pltpu.roll(part[height:], SPAN - height, 1)
            where = pl.ds(pl.multiple_of(768 - 256 * blks[i], 128), SPAN)
            dl_o[0, h : h + 1, where] += pltpu.roll(part, 255, 1)
            dq[half, hs] = nt(ds[...], kv[0, hs, :]).astype(bf16)
            dk = dk + tn(q[0, half, hs], ds[...])
            dv = dv + tn(do[half, hs], p[0, h, half, :])
        dkv[hs, :] = dk.astype(bf16)
        dkv[vs, :] = dv.astype(bf16)
    gq[...] += nt(dq[...], w[0, :, 0:192])
    gt[...] += nn(w[0, :, 384:768], dkv[...])
    buf[slot, :, 0:384] = jnp.concatenate([nn(nqt[...], dq[...]), nn(d1t[...], at[0])], axis=1).astype(bf16)
    buf[slot, :, 384:768] = nt(nft[...], dkv[...]).astype(bf16)
    core.finish(gw_o)

    @pl.when(n == 3)
    def _():
        for i in range(2):
            half = slice(i * 256, (i + 1) * 256)
            g_o[half, :] = gq[half, :] + gt[:, block_rows(blks[i])].T
            gp_o[half, :] = gt[:, block_rows((pn, 3 - pn)[i])].T.astype(bf16)
        loads[1].wait()
        sends[2].wait_recv()
        add_into(c2, ry)
        loads[3].wait()
        for path in (1, 0):
            loop(1, wide, lambda k, path=path: zgot(path, k).wait_recv())

        def put(ref):
            def store(r, total):
                ref[r, :] = total.astype(bf16)

            return store

        sum_line(wide, s1.at[wi], rz1, put(e1))
        sum_line(wide, f2, rz2, put(e2))
        y_cross.wait_recv()

        def add_cross(k):
            b1[k] = c1[0, k] + cy1[k]

        loop(0, wide, add_cross)
        out_got.wait_recv()
        loads[4].wait()
        for copy in (*sends, y_cross):
            copy.wait_send()
        for path in (0, 1):
            loop(1, wide, lambda k, path=path: zcopy(path, k).wait_send())


def self_backward(wide, xf, d1, w, gain, q, kv, at, p, gcr, o1, o2, outp):
    rl = D // wide
    return pl.pallas_call(
        partial(self_backward_kernel, wide),
        grid=(4,),
        in_specs=[
            whole((LEN, D)),
            whole((512, D)),
            slab((D, D)),
            whole((1, D)),
            slab((512, HD)),
            slab((2 * HD, LEN)),
            slab((512, HD)),
            slab((3, 512, LEN)),
            ANY,
            ANY,
            ANY,
            pl.BlockSpec(memory_space=pltpu.VMEM),
        ],
        out_specs=[
            pair_slab((D, D)),
            whole((512, D)),
            whole((512, D)),
            slab((3, 2048)),
            whole((wide, rl, 256)),
            whole((wide, rl, 256)),
            whole((rl, 384)),
            whole((rl, D)),
            ANY,
        ],
        out_shape=[
            out((2, D, D), bf16),
            out((512, D), f32),
            out((512, D), bf16),
            out((4, 3, 2048), f32),
            out((wide, rl, 256), bf16),
            out((wide, rl, 256), bf16),
            out((rl, 384), bf16),
            out((rl, D), bf16),
            out((2, 256, D), bf16),
        ],
        scratch_shapes=[
            pltpu.VMEM((2, wide, rl, 256), bf16),
            pltpu.VMEM((wide, rl, 256), bf16),
            pltpu.VMEM((512, D), bf16),
            pltpu.VMEM((D, 512), bf16),
            pltpu.VMEM((D, LEN), bf16),
            pltpu.VMEM((D, 512), bf16),
            pltpu.VMEM((D, LEN), f32),
            pltpu.VMEM((512, D), f32),
            pltpu.VMEM((512, HD), bf16),
            pltpu.VMEM((256, LEN), f32),
            pltpu.VMEM((256, LEN), bf16),
            pltpu.VMEM((512, HD), bf16),
            pltpu.VMEM((2 * HD, LEN), bf16),
            pltpu.VMEM((2, D, D), bf16),
            pltpu.VMEM((2, D, D), bf16),
            pltpu.VMEM((wide, rl, 384), bf16),
            pltpu.VMEM((rl, D), bf16),
            pltpu.VMEM((2, wide, rl, 256), bf16),
            pltpu.VMEM((wide, rl, 256), bf16),
            pltpu.VMEM((wide, rl, 384), bf16),
            pltpu.VMEM((wide, rl, 384), bf16),
            pltpu.VMEM((wide, rl, D), bf16),
            pltpu.SemaphoreType.DMA((1,)),
            pltpu.SemaphoreType.DMA((2,)),
            pltpu.SemaphoreType.DMA((5,)),
            pltpu.SemaphoreType.DMA((5,)),
            pltpu.SemaphoreType.DMA((5,)),
            pltpu.SemaphoreType.DMA((2, wide)),
            pltpu.SemaphoreType.DMA((2, wide)),
        ],
        compiler_params=params(4),
        cost_estimate=cost(25),
        name="self_backward",
    )(xf, d1, w, gain, q, kv, at, p, gcr.reshape(2, wide, rl, D), o1, o2, outp)


def reduce_kernel(
    wide, se, b1, c2, e1, e2, gxo, gxp, geo, gep, xf, d1, gain, gfeed, gcross, tg,
    gin_o, gen_o, sg_o, st_o, ff_o, cr_o, se_o,
    a1, a2, rx, ry, ry1, rzs1, rzs2, rzc1, rzc2, fs, fc, xs1, xs2, xc1, xc2, x1, x2,
    rgx, rge, tmp_in, tmp_en, back_in, back_en, rows_f, sg, st, rsg, rst, rsgz, rstz,
    load, ms, mr, ts, tr, zs, zr, ss, sr, os,
):
    d, w, n, pn, yn, dn = place_here()
    y = n // 2
    pair, line_y, diag, line_x = (d, w, pn), (d, w, yn), (d, w, dn), (1 - d, w, n)
    mine = pl.ds(pl.multiple_of(d * 256, 128), 256)
    other = pl.ds(pl.multiple_of(256 - d * 256, 128), 256)
    late = pl.ds(512, 256)
    loads = [
        pltpu.make_async_copy(se.at[:, :, :, mine], a1, load.at[0]),
        pltpu.make_async_copy(se.at[0, :, :, late], a2, load.at[1]),
        pltpu.make_async_copy(geo, tmp_en, load.at[2]),
    ]
    for copy in loads:
        copy.start()
    greet((pair, line_y, diag, line_x), wide)
    turn = lambda i, src, dst, dev: remote(src, dst, ts.at[i], tr.at[i], dev)
    put = [
        turn(0, se.at[:, :, :, other], rx, line_x),
        turn(2, se.at[1, :, :, late], ry, line_y),
        turn(3, e1, x1, line_x),
        turn(4, e2, x2, line_x),
    ]
    cross = [
        remote(gxp, rgx, ms.at[0], mr.at[0], pair),
        remote(gep, rge, ms.at[1], mr.at[1], pair),
    ]
    z_refs = ((a1, rzs1), (a2, rzs2), (b1, rzc1), (c2, rzc2))

    def zcopy(path, k):
        row = lax.rem(w + k, wide)
        src, dst = z_refs[path]
        src = src.at[0, row] if path == 0 else src.at[row]
        return remote(src, dst.at[w], zs.at[path, k], zr.at[path, w], (d, row, n))

    def zgot(path, k):
        row = lax.rem(w + k, wide)
        ref = z_refs[path][1].at[row]
        return remote(ref, ref, zs.at[path, k], zr.at[path, row], (d, row, n))

    def zstart(path):
        loop(1, wide, lambda k: zcopy(path, k).start())

    def zwait(path):
        loop(1, wide, lambda k: zgot(path, k).wait_recv())

    cross[0].start()
    cross[1].start()
    put[0].start()
    put[1].start()
    zstart(3)
    zstart(2)
    put[2].start()
    put[3].start()

    sg[...] = jnp.zeros((8, D), f32)
    sg[1:2, :] = gcross[...]
    sg[2:3, :] = gfeed[...]
    st[...] = tg[...]
    cross[0].wait_recv()
    own = (n, dn)
    for i in (1, 0):

        def back(r, i=i):
            x = xf[own[i], r, :].astype(f32)
            dx, gg = norm_back(x, gain[...], gxo[i, r, :] + rgx[i, r, :].astype(f32))
            total = d1[i, r, :] + dx
            sg[0:1, :] += gg
            if i == 0:
                rows_f[0, r, :] = total
            else:
                tmp_in[r, :] = total.astype(bf16)

        rows_loop(256, 32, back, unroll=2)
        if i == 1:
            in_send = remote(tmp_in, back_in, ms.at[3], mr.at[3], diag)
            in_send.start()
    in_local = pltpu.make_async_copy(rows_f.at[0], gin_o.at[y], os.at[0])
    in_local.start()
    cross[1].wait_recv()
    loads[2].wait()
    back_en[0] = (tmp_en[1] + rge[1].astype(f32)).astype(bf16)
    en_send = remote(back_en.at[0], back_en.at[1], ms.at[4], mr.at[4], diag)
    en_send.start()
    tmp_en[0] = tmp_en[0] + rge[0].astype(f32)
    en_local = pltpu.make_async_copy(tmp_en.at[0], gen_o.at[y], os.at[1])
    en_local.start()

    def small(j, dev):
        return (
            remote(sg, rsg.at[j], ss.at[0, j], sr.at[0, j], dev),
            remote(st, rst.at[j], ss.at[1, j], sr.at[1, j], dev),
        )

    def small_add(j, dev):
        for copy in small(j, dev):
            copy.wait()
        sg[...] += rsg[j]
        st[...] += rst[j]

    def small_line(k):
        dev = (d, lax.rem(w + k, wide), n)
        return (
            remote(sg, rsgz.at[w], ss.at[0, 3 + k], sr.at[0, 3 + w], dev),
            remote(st, rstz.at[w], ss.at[1, 3 + k], sr.at[1, 3 + w], dev),
        )

    def start_all(copies):
        for copy in copies:
            copy.start()

    start_all(small(0, pair))
    small_add(0, pair)
    start_all(small(1, line_y))

    small_add(1, line_y)
    start_all(small(2, line_x))
    loads[1].wait()
    put[1].wait_recv()
    add_into(a2, ry)
    zstart(1)
    small_add(2, line_x)
    loop(1, wide, lambda k: start_all(small_line(k)))
    rsgz[w] = sg[...]
    rstz[w] = st[...]
    loads[0].wait()
    put[0].wait_recv()
    add_into(a1, rx)
    y1 = turn(5, a1.at[1], ry1, line_y)
    y1.start()

    def keep(ref, cols):
        def store(r, total):
            ref[r, cols] = total.astype(bf16)

        return store

    everything = slice(None)
    zwait(3)
    sum_line(wide, c2.at[w], rzc2, keep(fc, late))
    f_c2 = turn(6, fc.at[:, late], xc2, line_x)
    f_c2.start()
    zwait(2)
    sum_line(wide, b1.at[w], rzc1, keep(fc, mine))
    f_c1 = turn(7, fc.at[:, mine], xc1, line_x)
    f_c1.start()
    y1.wait_recv()
    rl = e1.shape[0]

    def add_side(k):
        a1[0, k] = a1[0, k] + ry1[k]

    loop(0, wide, add_side)
    zstart(0)

    def small_wait(k):
        row = lax.rem(w + k, wide)
        for i, ref in enumerate((rsgz, rstz)):
            remote(ref.at[row], ref.at[row], ss.at[i, 3], sr.at[i, 3 + row], line_x).wait_recv()

    loop(1, wide, small_wait)
    sg_o[...] = lax.fori_loop(1, wide, lambda k, t: t + rsgz[k], rsgz[0])
    st_o[...] = lax.fori_loop(1, wide, lambda k, t: t + rstz[k], rstz[0])

    zwait(1)
    sum_line(wide, a2.at[w], rzs2, keep(fs, late))
    f_s2 = turn(8, fs.at[:, late], xs2, line_x)
    f_s2.start()

    in_send.wait_recv()

    def widen(r):
        rows_f[1, r, :] = back_in[r, :].astype(f32)

    rows_loop(256, 64, widen)
    in_last = pltpu.make_async_copy(rows_f.at[1], gin_o.at[1 - y], os.at[2])
    in_last.start()
    en_send.wait_recv()
    tmp_en[1] = back_en[1].astype(f32)
    en_last = pltpu.make_async_copy(tmp_en.at[1], gen_o.at[1 - y], os.at[3])
    en_last.start()

    f_mine = pl.ds(pl.multiple_of(d * 384, 128), 384)
    f_other = pl.ds(pl.multiple_of(384 - d * 384, 128), 384)
    put[2].wait_recv()
    put[3].wait_recv()
    ff_o[:, f_mine] = e1[...].astype(f32)
    ff_o[:, f_other] = x1[...].astype(f32)
    ff_o[:, pl.ds(D, D)] = e2[...].astype(f32) + x2[...].astype(f32)
    f_c1.wait_recv()
    f_c2.wait_recv()
    cr_o[:, mine] = fc[:, mine].astype(f32)
    cr_o[:, other] = xc1[...].astype(f32)
    cr_o[:, late] = fc[:, late].astype(f32) + xc2[...].astype(f32)
    zwait(0)
    sum_line(wide, a1.at[0, w], rzs1, keep(fs, mine))
    f_s1 = turn(9, fs.at[:, mine], xs1, line_x)
    f_s1.start()
    f_s2.wait_recv()
    se_o[:, mine] = fs[:, mine].astype(f32)
    se_o[:, late] = fs[:, late].astype(f32) + xs2[...].astype(f32)
    f_s1.wait_recv()
    se_o[:, other] = xs1[...].astype(f32)

    for copy in (in_local, en_local, in_last, en_last):
        copy.wait()
    for copy in (*cross, in_send, en_send, *put, y1, f_c1, f_c2, f_s1, f_s2):
        copy.wait_send()

    def finish(k):
        for path in range(4):
            zcopy(path, k).wait_send()
        for copy in small_line(k):
            copy.wait_send()

    loop(1, wide, finish)


def reduce_all(wide, se, b1, c2, e1, e2, gxo, gxp, geo, gep, xf, d1, gain, gfeed, gcross, tg):
    rl = D // wide
    se = se.reshape(2, wide, rl, D)
    sem = pltpu.SemaphoreType.DMA
    V = pl.BlockSpec(memory_space=pltpu.VMEM)
    v = lambda *shape: pltpu.VMEM(shape, bf16)
    return pl.pallas_call(
        partial(reduce_kernel, wide),
        in_specs=[ANY, V, V, V, V, V, ANY, ANY, ANY, V, V, V, V, V, V],
        out_specs=[ANY, ANY, V, V, V, V, V],
        out_shape=[
            out((2, 256, D), f32),
            out((2, 128, D), f32),
            out((8, D), f32),
            out((32, 128), f32),
            out((rl, 2 * D), f32),
            out((rl, D), f32),
            out((rl, D), f32),
        ],
        scratch_shapes=[
            v(2, wide, rl, 256),
            v(wide, rl, 256),
            v(2, wide, rl, 256),
            v(wide, rl, 256),
            v(wide, rl, 256),
            v(wide, rl, 256),
            v(wide, rl, 256),
            v(wide, rl, 256),
            v(wide, rl, 256),
            v(rl, D),
            v(rl, D),
            v(rl, 256),
            v(rl, 256),
            v(rl, 256),
            v(rl, 256),
            v(rl, 384),
            v(rl, D),
            v(2, 256, D),
            v(2, 128, D),
            v(256, D),
            pltpu.VMEM((2, 128, D), f32),
            v(256, D),
            v(2, 128, D),
            pltpu.VMEM((2, 256, D), f32),
            pltpu.VMEM((8, D), f32),
            pltpu.VMEM((32, 128), f32),
            pltpu.VMEM((3, 8, D), f32),
            pltpu.VMEM((3, 32, 128), f32),
            pltpu.VMEM((wide, 8, D), f32),
            pltpu.VMEM((wide, 32, 128), f32),
            sem((5,)),
            sem((5,)),
            sem((5,)),
            sem((10,)),
            sem((10,)),
            sem((4, wide)),
            sem((4, wide)),
            sem((2, 3 + wide)),
            sem((2, 3 + wide)),
            sem((4,)),
        ],
        compiler_params=pltpu.CompilerParams(
            collective_id=1, has_side_effects=True, vmem_limit_bytes=VMEM_LIMIT
        ),
        name="reduce_all",
    )(se, b1, c2, e1, e2, gxo, gxp, geo, gep, xf, d1, gain, gfeed, gcross, tg)


def on_device(
    wide, hidden_in, encoder_out, cotangent, piece_starts, valid_lengths, bucket_table,
    gain_self, gain_cross, gain_feed, relative_bias, *mats
):
    me = lax.axis_index("narrow")
    sq, sk, sv, so, cq, ck, cv, co, gate, up, down = mats
    ps = jnp.concatenate((sq, so, sk, sv), axis=1)
    pc = jnp.concatenate((cq, co, ck, cv), axis=1)
    pf = jnp.concatenate((gate, up, down), axis=1)
    tab = jnp.pad(relative_bias.T, ((0, 29), (0, 96)))
    padded = jnp.pad(bucket_table, (0, 1), constant_values=-1)
    hot = (padded[None, :] == jnp.arange(BUCKETS)[:, None]).astype(f32)
    gains = [g.reshape(1, D) for g in (gain_self, gain_cross, gain_feed)]
    (
        xf, ws, wc, _, gff, ef, q, kv, at, p, cqh, ckv, cat, cp, h1, outp, d2, gg_feed,
    ) = forward(
        wide, piece_starts, valid_lengths, hidden_in[:, 0], encoder_out[:, 0], cotangent[:, 0], tab, hot, ps, pc, pf, *gains
    )
    ws, wc = (g.reshape(4, D, D) for g in (ws, wc))
    xs, es = xf.reshape(LEN, D), ef.reshape(ENC, D)
    gcr, d1, gg_cross, geo, gep, o1, o2 = cross_backward(wide, h1, es, d2, wc, gains[1], cqh, ckv, cat, cp, gff)
    gse, gxo, gxp, dl, b1, c2, e1, e2, outs = self_backward(
        wide, xs, d1, ws, gains[0], q, kv, at, p, gcr, o1, o2, outp.reshape(2, 256, D)
    )
    tg = lax.dot_general(hot, dl.reshape(12, 2048), (((1,), (1,)), ((), ())), precision=precise)
    order = jnp.arange(12) // 3 ^ me ^ 1
    tg = tg.reshape(BUCKETS, 4, 3)
    tg = sum(jnp.where(order == k, jnp.tile(tg[:, k], (1, 4)), 0.0) for k in range(4))
    tg = jnp.pad(tg, ((0, 0), (0, 116)))
    two = lambda a: a.reshape(2, -1, D)
    gin, gen, sg, st, f, b, a = reduce_all(
        wide, gse, b1, c2, e1, e2, two(gxo), two(gxp), two(geo), two(gep), xf, two(d1), gains[0], gg_feed, gg_cross, tg
    )
    tg = lax.dynamic_slice_in_dim(st, me * 3, 3, axis=1)
    return (
        outs[:, None], gin[:, None], gen[:, None],
        sg[0], sg[1], sg[2], tg,
        a[:, :192], a[:, 384:576], a[:, 576:], a[:, 192:384],
        b[:, :192], b[:, 384:576], b[:, 576:], b[:, 192:384],
        f[:, :512], f[:, 512:1024], f[:, 1024:],
    )


def solution(mesh):
    rows = P(None, ("dp", "wide"), "narrow", None)
    mat = P("wide", "narrow")
    return jax.shard_map(
        partial(on_device, mesh.shape["wide"]),
        mesh=mesh,
        in_specs=(rows, rows, rows, P(None, ("dp", "wide")), P(None, ("dp", "wide")), P(), P(), P(), P(), P(None, "narrow"))
        + (mat,) * 11,
        out_specs=(rows, rows, rows, P(), P(), P(), P(None, "narrow")) + (mat,) * 11,
        check_vma=False,
    )
```

```python
import math
from functools import partial

import jax
import jax.numpy as jnp
from jax import lax
from jax.experimental import pallas as pl
from jax.experimental.pallas import tpu as pltpu
from jax.sharding import PartitionSpec as P

D = 768
HD = 192
HEADS = 12
DHEAD = 64
FFB = 512
BUCKETS = 32
LEN = 1024
ENC = 512
PIC = 256
TILES = 11
SPAN = 1280
ROWS = 16

precise = lax.Precision.HIGHEST
epsilon = 1e-06
masked_value = -1e30
f32 = jnp.float32
bf16 = jnp.bfloat16
MESH = pl.DeviceIdType.MESH
ANY = pl.BlockSpec(memory_space=pl.ANY)
VMEM_LIMIT = 60 << 20


def nn(a, b):
    return lax.dot_general(a, b, (((1,), (0,)), ((), ())), preferred_element_type=f32)


def nt(a, b):
    return lax.dot_general(a, b, (((1,), (1,)), ((), ())), preferred_element_type=f32)


def tn(a, b):
    return lax.dot_general(a, b, (((0,), (0,)), ((), ())), preferred_element_type=f32)


def rows_loop(total, step, body, unroll=1):
    def run(i, carry):
        body(pl.ds(pl.multiple_of(i * step, step), step))
        return carry

    lax.fori_loop(0, total // step, run, 0, unroll=unroll)


def normed(x, gain):
    factor = lax.rsqrt(jnp.mean(x * x, axis=1, keepdims=True) + epsilon)
    return x * factor * gain


def norm_back(x, gain, upstream):
    factor = lax.rsqrt(jnp.mean(x * x, axis=1, keepdims=True) + epsilon)
    weighted = upstream * gain
    inner = jnp.sum(weighted * x, axis=1, keepdims=True)
    dx = weighted * factor - x * (factor * factor * factor * inner * (1.0 / D))
    return dx, jnp.sum(upstream * x * factor, axis=0, keepdims=True)


def own_blocks():
    me = lax.axis_index("narrow")
    return (me, 3 - me)


def block_rows(blk):
    return pl.ds(pl.multiple_of(blk * 256, 256), 256)


def softmax_rows(v):
    e = jnp.exp(v - jnp.max(v, axis=1, keepdims=True))
    return e * (1.0 / jnp.sum(e, axis=1, keepdims=True))


def place_here():
    d, w, n = lax.axis_index("dp"), lax.axis_index("wide"), lax.axis_index("narrow")
    return d, w, n, n + 1 - 2 * lax.rem(n, 2), lax.rem(n + 2, 4), 3 - n


def remote(src, dst, send, recv, dev):
    return pltpu.make_async_remote_copy(
        src_ref=src, dst_ref=dst, send_sem=send, recv_sem=recv, device_id=dev, device_id_type=MESH
    )


def greet(devs, wide=1):
    d, w, n = place_here()[:3]
    barrier = pltpu.get_barrier_semaphore()
    for dev in devs:
        pl.semaphore_signal(barrier, inc=1, device_id=dev, device_id_type=MESH)

    def line(k, carry):
        dev = (d, lax.rem(w + k, wide), n)
        pl.semaphore_signal(barrier, inc=1, device_id=dev, device_id_type=MESH)
        return carry

    lax.fori_loop(1, wide, line, 0)
    pl.semaphore_wait(barrier, wide - 1 + len(devs))


def loop(lo, hi, body):
    def run(k, carry):
        body(k)
        return carry

    lax.fori_loop(lo, hi, run, 0)


def add_into(dst, src):
    shape = dst.shape
    rl = shape[-2]
    step = 64 if rl % 64 == 0 else rl
    lead = shape[:-2]

    def one(*index):
        for j in range(rl // step):
            spot = index + (slice(j * step, (j + 1) * step), slice(None))
            dst[spot] = dst[spot] + src[spot]

    if len(lead) == 1:
        loop(0, lead[0], one)
    else:
        for i in range(lead[0]):
            loop(0, lead[1], partial(one, i))


def sum_line(wide, own, parts, store):
    w = lax.axis_index("wide")
    rl = own.shape[0]
    step = 64 if rl % 64 == 0 else rl
    for j in range(rl // step):
        r = slice(j * step, (j + 1) * step)

        def add(k, total, r=r):
            return total + parts[lax.rem(w + k, wide), r, :].astype(f32)

        store(r, lax.fori_loop(1, wide, add, own[r, :].astype(f32)))


def core_devs():
    d, w, n, pn, yn, dn = place_here()
    return (d, w, pn)


class CoreSum:
    def __init__(self, step, buf, landed, send, recv):
        self.step, self.buf, self.landed, self.send, self.recv = step, buf, landed, send, recv
        self.side = step // 2

    def copy(self):
        return remote(
            self.buf.at[0], self.landed.at[self.side], self.send.at[0], self.recv.at[self.side], core_devs()
        )

    def finish(self, result):
        @pl.when(lax.rem(self.step, 2) == 0)
        def _():
            self.copy().start()

        @pl.when(lax.rem(self.step, 2) == 1)
        def _():
            self.copy().wait_recv()

            def add(r):
                result[0, r, :] = self.buf[1, r, :] + self.landed[self.side, r, :]

            rows_loop(D, 64, add)
            self.copy().wait_send()


def whole(shape):
    zero = (0,) * len(shape)
    return pl.BlockSpec(shape, lambda n: zero)


def slab(shape):
    zero = (0,) * len(shape)
    return pl.BlockSpec((1,) + shape, lambda n: (n,) + zero)


def pair_slab(shape):
    zero = (0,) * len(shape)
    return pl.BlockSpec((1,) + shape, lambda n: (n // 2,) + zero)


def params(collective_id=None):
    if collective_id is None:
        return pltpu.CompilerParams(dimension_semantics=("arbitrary",), vmem_limit_bytes=VMEM_LIMIT)
    return pltpu.CompilerParams(
        dimension_semantics=("arbitrary",),
        vmem_limit_bytes=VMEM_LIMIT,
        collective_id=collective_id,
        has_side_effects=True,
    )


def out(shape, dtype):
    return jax.ShapeDtypeStruct(shape, dtype)


SMEM = pl.BlockSpec(memory_space=pltpu.SMEM)


def cost(gflop):
    return pl.CostEstimate(flops=int(gflop * 1e9), bytes_accessed=20 << 20, transcendentals=0)


GELU_A = 0.7978845608028654
GELU_B = 0.044715


FORWARD_VMEM = 58 << 20
ORDER_ATT = (1, 0, 3, 2)
ORDER_FEED = (1, 0, 2, 3)


def pick(order, k):
    index = order[3]
    for i in (2, 1, 0):
        index = jnp.where(k == i, order[i], index)
    return index


def forward_kernel(
    wide, ps_s, vl_s, hid, enc, cot, tab, hot, ps, pc, pf, gain_s, gain_c, gain_f,
    xf, gs, gc, gf, gff, ef, q1, kv1, at1, p1, q2, kv2, at2, p2, h1, out_o, d2_o, gg_o,
    wbuf, stage, xv, ev, tabs, off, nf, mask, tb, s, h2, nc, nct, cv, ct, gu, da, act, dgu, acc, buf, landed,
    ls, ins, inr, ws, vs, zs, zr, ys, yr, xs, xr, cs, cr, fsend, frecv, fout,
):
    step = pl.program_id(0)
    d, w, n, pn, yn, dn = place_here()
    y = n // 2
    blks = (n, dn)
    rl = ps.shape[0]
    groups = ((ps, gs, 0, 768, True), (pc, gc, 0, 768, True), (pf, gf, 0, 1024, True), (pf, gf, 1024, 512, False))
    keep, give = (1, 3), (0, 2)
    diag, pair, line_x, line_y = (d, w, dn), (d, w, pn), (1 - d, w, n), (d, w, yn)

    def cols(g, which):
        start, width, split = groups[g][2:]
        if which == 2 or not split:
            return pl.ds(start, width)
        half = width // 2
        pos = d if which == 0 else 1 - d
        return pl.ds(pl.multiple_of(start + pos * half, 128), half)

    def own(g, which):
        return groups[g][0].at[:, cols(g, which)]

    def spot(g, slot, row, which):
        return groups[g][1].at[slot, row, :, cols(g, which)]

    def zcopy(g, k):
        dev = (d, lax.rem(w + k, wide), n)
        if g == 4:
            ref = spot(3, 3, w, 0)
            return remote(ref, ref, zs.at[4, k], zr.at[4, w], dev)
        return remote(own(g, 0), spot(g, 1, w, 0), zs.at[g, k], zr.at[g, w], dev)

    def zgot(g, row):
        ref = spot(3, 3, row, 0) if g == 4 else spot(g, 1, row, 0)
        return remote(ref, ref, zs.at[g, 0], zr.at[g, row], line_x)

    def ycopy(g, row, src=None):
        ref = spot(g, 1, row, 0)
        return remote(ref if src is None else src, spot(g, 3, row, 0), ys.at[g, row], yr.at[g, row], line_y)

    def ygot(g, row):
        return remote(spot(g, 3, row, 0), spot(g, 3, row, 0), ys.at[g, row], yr.at[g, row], line_y)

    def xcopy(g, side, row):
        ref = spot(g, keep[side], row, 0)
        return remote(ref, ref, xs.at[g, side, row], xr.at[g, side, row], line_x)

    def xgot(g, side, row):
        ref = spot(g, keep[side], row, 1)
        return remote(ref, ref, xs.at[g, side, row], xr.at[g, side, row], line_x)

    def ccopy(g, side, row, src=None):
        ref = spot(g, keep[side], row, 2)
        return remote(
            ref if src is None else src, spot(g, give[side], row, 2), cs.at[g, side, row], cr.at[g, side, row], pair
        )

    def cgot(g, side, row):
        ref = spot(g, give[side], row, 2)
        return remote(ref, ref, cs.at[g, side, row], cr.at[g, side, row], pair)

    def around(first, body):
        loop(first, wide, lambda k: body(lax.rem(w + k, wide)))

    def zsend(g):
        loop(1, wide, lambda k: zcopy(g, k).start())

    def own_sends(g):
        ycopy(g, w, own(g, 0)).start()
        ccopy(g, 0, w, own(g, 2)).start()

    def zpass(g, then):
        def one(row):
            zgot(g, row).wait_recv()
            for nxt in then:
                nxt(row).start()

        around(1, one)

    def ypass(g):
        def one(row):
            ygot(g, row).wait_recv()
            xcopy(g, 1, row).start()

        around(0, one)

    def xsend(g):
        around(1, lambda row: xcopy(g, 0, row).start())

    def xstep(g, side):
        def one(k):
            row = lax.rem(w + k, wide)
            xgot(g, side, row).wait_recv()
            ccopy(g, side, row).start()

        loop(1 - side, wide, one)

    def cwait(g, side):
        loop(0, wide, lambda k: cgot(g, side, lax.rem(w + k, wide)).wait_recv())

    straight = rl % 16 == 0
    many = 16 // math.gcd(rl, 16)

    def slab_copies(ref, slot, b):
        width = ref.shape[-1]
        if straight:
            return [
                pltpu.make_async_copy(
                    ref.at[slot, k], wbuf.at[b, pl.ds(k * rl, rl), pl.ds(0, width)], ws.at[b, k]
                )
                for k in range(wide)
            ]
        return [pltpu.make_async_copy(ref.at[slot], stage.at[:, :, pl.ds(0, width)], ws.at[b, 0])]

    def fetch(ref, slot, b):
        for copy in slab_copies(ref, slot, b):
            copy.start()

    def fetched(ref, slot, b):
        for copy in slab_copies(ref, slot, b):
            copy.wait()
        if not straight:
            width = ref.shape[-1]
            for k in range(0, wide, many):
                part = jnp.concatenate([stage[k + i, :, 0:width].astype(f32) for i in range(many)], axis=0)
                wbuf[b, k * rl : (k + many) * rl, 0:width] = part.astype(bf16)

    local = [
        pltpu.make_async_copy(src, dst, ls.at[i])
        for i, (src, dst) in enumerate(
            (
                (ps, gs.at[1, w]),
                (pc, gc.at[1, w]),
                (pf, gf.at[1, w]),
                (hid.at[y], xv.at[n]),
                (enc.at[y], ev.at[n]),
                (cot.at[y], cv.at[0]),
            )
        )
    ]
    back = [pltpu.make_async_copy(xv, xf, vs.at[0]), pltpu.make_async_copy(ev, ef, vs.at[1])]
    early = [
        remote(tab, tabs.at[0], ins.at[3], inr.at[3], pair),
        remote(tab, tabs.at[3], ins.at[4], inr.at[4], line_y),
        remote(tab, tabs.at[2], ins.at[5], inr.at[5], diag),
        remote(hid.at[1 - y], xv.at[n], ins.at[0], inr.at[0], diag),
        remote(hid.at[y], xv.at[n], ins.at[6], inr.at[6], pair),
    ]
    middle = [
        remote(enc.at[1 - y], ev.at[n], ins.at[1], inr.at[1], diag),
        remote(enc.at[y], ev.at[n], ins.at[7], inr.at[7], pair),
        remote(cot.at[1 - y], cv.at[1], ins.at[2], inr.at[2], diag),
    ]
    later = [
        remote(xv.at[dn], xv.at[dn], ins.at[8], inr.at[8], pair),
        remote(ev.at[dn], ev.at[dn], ins.at[9], inr.at[9], pair),
    ]

    def arrived(i, ref):
        remote(ref, ref, ins.at[i], inr.at[i], pair).wait_recv()

    @pl.when(step == 0)
    def _():
        for copy in local:
            copy.start()
        greet((pair, line_y, diag, line_x), wide)
        for copy in early:
            copy.start()
        zsend(0)
        own_sends(0)
        tabs[1] = tab[...]
        start, length = ps_s[y, 0], vl_s[y, 0]
        for i in range(2):

            def mask_rows(r, i=i):
                shape = (32, LEN)
                qi = blks[i] * 256 + r.start + lax.broadcasted_iota(jnp.int32, shape, 0)
                kj = lax.broadcasted_iota(jnp.int32, shape, 1)
                inside = (qi >= start) & (qi < start + PIC) & (kj >= start) & (kj < start + PIC)
                allowed = ((kj <= qi) | inside) & (kj < length)
                mask[pl.ds(i * 256 + r.start, 32), :] = jnp.where(allowed, 0.0, masked_value)

            rows_loop(256, 32, mask_rows, unroll=2)
        arrived(6, xv.at[pn])
        arrived(0, xv.at[dn])
        later[0].start()
        zpass(0, (lambda row: ycopy(0, row), lambda row: xcopy(0, 0, row)))
        zsend(1)
        arrived(8, xv.at[yn])
        local[3].wait()
        back[0].start()
        arrived(3, tabs.at[0])
        arrived(4, tabs.at[3])
        arrived(5, tabs.at[2])
        for i in range(4):

            def norm_rows(r, i=i):
                nf[pl.ds(i * 256 + r.start, 64), :] = normed(xv[i, r, :].astype(f32), gain_s[...]).astype(bf16)

            rows_loop(256, 64, norm_rows, unroll=4)
        for i in range(2):
            h1[i * 256 : (i + 1) * 256, :] = xv[blks[i]].astype(f32)
        xstep(0, 0)
        ypass(0)
        own_sends(1)
        middle[0].start()
        middle[1].start()
        for i in range(3):
            local[i].wait()
        fetch(gs, 1, 0)

    @pl.when(step < 4)
    def _():
        b = lax.rem(step, 2)
        slot = pick(ORDER_ATT, step)
        fetched(gs, slot, b)
        off[...] = lax.dot_general(
            tabs[slot, 0:8, 0:BUCKETS], hot[...], (((1,), (0,)), ((), ())), precision=precise, preferred_element_type=f32
        )
        kv1[0] = nn(nf[...], wbuf[b, :, 384:768]).astype(bf16).T
        for i in range(2):
            q1[0, i * 256 : (i + 1) * 256, :] = nn(nf[block_rows(blks[i]), :], wbuf[b, :, 0:192]).astype(bf16)
        for h in range(3):
            for t in range(TILES):
                line = jnp.broadcast_to(off[h : h + 1, 128 * t : 128 * t + 256], (128, 256))
                tb[t] = pltpu.roll(line, 129, 1, stride=1, stride_axis=0)[:, :128]
            hs = slice(h * DHEAD, (h + 1) * DHEAD)
            vs_ = slice(HD + h * DHEAD, HD + (h + 1) * DHEAD)
            for i in range(2):
                s[...] = nn(q1[0, i * 256 : (i + 1) * 256, hs], kv1[0, hs, :])
                for r in range(2):
                    idx = [jnp.minimum(kb - 2 * blks[i] - r, 3) + 7 for kb in range(8)]

                    def soft_rows(rr, i=i, r=r, h=h, idx=idx):
                        bias = jnp.concatenate([tb[idx[kb], rr, :] for kb in range(8)], axis=1)
                        v = s[pl.ds(r * 128 + rr.start, ROWS), :] + bias
                        v = v + mask[pl.ds(i * 256 + r * 128 + rr.start, ROWS), :]
                        p1[0, h, pl.ds(i * 256 + r * 128 + rr.start, ROWS), :] = softmax_rows(v).astype(bf16)

                    rows_loop(128, ROWS, soft_rows, unroll=8)
                at1[0, i * 256 : (i + 1) * 256, hs] = nt(
                    p1[0, h, i * 256 : (i + 1) * 256, :], kv1[0, vs_, :]
                ).astype(bf16)
        h1[...] += nt(at1[0], wbuf[b, :, 192:384])

    @pl.when(step == 0)
    def _():
        cwait(0, 0)
        fetch(gs, 0, 1)
        zpass(1, (lambda row: ycopy(1, row),))
        zsend(2)
        own_sends(2)
        own_sends(3)

    @pl.when(step == 1)
    def _():
        xstep(0, 1)
        fetch(gs, 3, 0)
        xsend(1)
        middle[2].start()

    @pl.when(step == 2)
    def _():
        cwait(0, 1)
        fetch(gs, 2, 1)
        ypass(1)
        zpass(2, (lambda row: ycopy(2, row),))
        zsend(3)
        ygot(3, w).wait_recv()
        ccopy(3, 1, w).start()
        zsend(4)

    @pl.when(step == 3)
    def _():
        xstep(1, 0)
        fetch(gc, 1, 0)
        xsend(2)
        arrived(1, ev.at[dn])
        later[1].start()
        arrived(7, ev.at[pn])
        arrived(9, ev.at[yn])
        local[4].wait()
        back[1].start()

        def norm_rows(r):
            x = h1[r, :]
            nc[r, :] = normed(x, gain_c[...]).astype(bf16)
            h2[r, :] = x

        rows_loop(512, 64, norm_rows, unroll=4)

    @pl.when((step >= 4) & (step < 8))
    def _():
        b = lax.rem(step, 2)
        fetched(gc, pick(ORDER_ATT, step - 4), b)
        kv2[0] = nn(ev[...].reshape(ENC, D), wbuf[b, :, 384:768]).astype(bf16).T
        q2[0] = nn(nc[...], wbuf[b, :, 0:192]).astype(bf16)
        for h in range(3):
            hs = slice(h * DHEAD, (h + 1) * DHEAD)
            vs_ = slice(HD + h * DHEAD, HD + (h + 1) * DHEAD)
            gu[:, 0:ENC] = nn(q2[0, :, hs], kv2[0, hs, :])

            def soft_rows(r, h=h):
                p2[0, h, r, :] = softmax_rows(gu[r, 0:ENC]).astype(bf16)

            rows_loop(512, 16, soft_rows, unroll=32)
            at2[0, :, hs] = nt(p2[0, h], kv2[0, vs_, :]).astype(bf16)
        h2[...] += nt(at2[0], wbuf[b, :, 192:384])

    @pl.when(step == 4)
    def _():
        cwait(1, 0)
        fetch(gc, 0, 1)

    @pl.when(step == 5)
    def _():
        xstep(1, 1)
        fetch(gc, 3, 0)
        ypass(2)

    @pl.when(step == 6)
    def _():
        cwait(1, 1)
        fetch(gc, 2, 1)

    @pl.when(step == 7)
    def _():
        xstep(2, 0)
        zpass(3, (lambda row: ccopy(3, 0, row),))
        fetch(gf, 1, 0)
        arrived(2, cv.at[1])
        local[5].wait()

        def norm_rows(r):
            x = h2[r, :]
            nc[r, :] = normed(x, gain_f[...]).astype(bf16)
            acc[r, :] = x
            d2_o[r, :] = jnp.zeros((64, D), f32)

        rows_loop(512, 64, norm_rows, unroll=4)
        nct[...] = nc[...].T
        ct[...] = cv[...].reshape(512, D).T

    def give_copy(side):
        return remote(buf.at[0], landed.at[side], fsend.at[side], frecv.at[side], pair)

    def put_out(side):
        return pltpu.make_async_copy(buf.at[1], gff.at[side], fout.at[side])

    def add_side(side):
        give_copy(side).wait_recv()

        def add(r):
            buf[1, r, :] = buf[1, r, :] + landed[side, r, :]

        rows_loop(D, 64, add)
        put_out(side).start()

    @pl.when(step >= 8)
    def _():
        b = lax.rem(step, 2)
        fetched(gf, pick(ORDER_FEED, step - 8), b)
        gu[...] = nn(nc[...], wbuf[b, :, : 2 * FFB])
        da[...] = nn(cv[...].reshape(512, D), wbuf[b, :, 2 * FFB :])

        def gelu_rows(r):
            gate = gu[r, :FFB]
            up = gu[r, FFB:]
            d_act = da[r, :]
            sq = gate * gate
            th = jnp.tanh(GELU_A * gate * (1.0 + GELU_B * sq))
            half = 0.5 + 0.5 * th
            gelu = gate * half
            slope = half + 0.5 * GELU_A * gate * (1.0 - th * th) * (1.0 + 3.0 * GELU_B * sq)
            act[r, :] = (gelu * up).astype(bf16)
            dgu[r, :FFB] = (d_act * up * slope).astype(bf16)
            dgu[r, FFB:] = (d_act * gelu).astype(bf16)

        rows_loop(512, 16, gelu_rows, unroll=32)
        acc[...] += nt(act[...], wbuf[b, :, 2 * FFB :])
        d2_o[...] += nt(dgu[...], wbuf[b, :, : 2 * FFB])

        @pl.when(step == 10)
        def _():
            give_copy(0).wait_send()

        @pl.when(step == 11)
        def _():
            put_out(0).wait()

        place = jnp.where((step == 8) | (step == 11), 1, 0)
        buf[place, :, : 2 * FFB] = nn(nct[...], dgu[...]).astype(bf16)
        buf[place, :, 2 * FFB :] = nn(ct[...], act[...]).astype(bf16)

    @pl.when(step == 8)
    def _():
        cwait(2, 0)
        cwait(3, 0)
        fetch(gf, 0, 1)

    @pl.when(step == 9)
    def _():
        give_copy(0).start()
        zpass(4, (lambda row: ccopy(3, 1, row),))
        xstep(2, 1)
        cwait(2, 1)
        cwait(3, 1)
        fetch(gf, 2, 0)

    @pl.when(step == 10)
    def _():
        give_copy(1).start()
        fetch(gf, 3, 1)
        add_side(0)

    @pl.when(step == 11)
    def _():
        add_side(1)
        gg_o[...] = jnp.zeros((1, D), f32)

        for i in range(2):

            def back_rows(r, i=i):
                rows = pl.ds(i * 256 + r.start, 64)
                dx, gg = norm_back(h2[rows, :], gain_f[...], d2_o[rows, :])
                d2_o[rows, :] = cv[i, r, :].astype(f32) + dx
                gg_o[...] += gg
                out_o[rows, :] = acc[rows, :].astype(bf16)

            rows_loop(256, 64, back_rows, unroll=2)
        for copy in back:
            copy.wait()
        put_out(1).wait()
        give_copy(1).wait_send()
        for copy in early + middle + later:
            copy.wait_send()

        def finish(row):
            for g in range(4):
                for side in range(2):
                    ccopy(g, side, row).wait_send()
            for g in range(3):
                ycopy(g, row).wait_send()
                xcopy(g, 1, row).wait_send()

        around(0, finish)
        ycopy(3, w).wait_send()

        def finish_line(k):
            row = lax.rem(w + k, wide)
            for g in range(5):
                zcopy(g, k).wait_send()
            for g in range(3):
                xcopy(g, 0, row).wait_send()

        loop(1, wide, finish_line)


def forward(wide, ps_s, vl_s, hid, enc, cot, tab, hot, ps, pc, pf, gain_s, gain_c, gain_f):
    rl = ps.shape[0]
    sem = pltpu.SemaphoreType.DMA
    V = pl.BlockSpec(memory_space=pltpu.VMEM)

    def turn(first, shape):
        zero = (0,) * len(shape)
        return pl.BlockSpec(
            (1,) + shape, lambda n: (pick(ORDER_ATT, jnp.clip(n - first, 0, 3)),) + zero
        )

    v = lambda *shape: pltpu.VMEM(shape, bf16)
    vf = lambda *shape: pltpu.VMEM(shape, f32)
    return pl.pallas_call(
        partial(forward_kernel, wide),
        grid=(12,),
        in_specs=[SMEM, SMEM, ANY, ANY, ANY, V, V, V, V, V, V, V, V],
        out_specs=[ANY] * 6
        + [turn(0, (512, HD)), turn(0, (2 * HD, LEN)), turn(0, (512, HD)), turn(0, (3, 512, LEN))]
        + [turn(4, (512, HD)), turn(4, (2 * HD, ENC)), turn(4, (512, HD)), turn(4, (3, 512, ENC))]
        + [V, V, V, V],
        out_shape=[
            out((4, 256, D), bf16),
            out((4, wide, rl, D), bf16),
            out((4, wide, rl, D), bf16),
            out((4, wide, rl, 2 * D), bf16),
            out((2, D, 3 * FFB), bf16),
            out((4, 128, D), bf16),
            out((4, 512, HD), bf16),
            out((4, 2 * HD, LEN), bf16),
            out((4, 512, HD), bf16),
            out((4, 3, 512, LEN), bf16),
            out((4, 512, HD), bf16),
            out((4, 2 * HD, ENC), bf16),
            out((4, 512, HD), bf16),
            out((4, 3, 512, ENC), bf16),
            out((512, D), f32),
            out((512, D), bf16),
            out((512, D), f32),
            out((1, D), f32),
        ],
        scratch_shapes=[
            v(2, D, 3 * FFB),
            v(wide, rl, 3 * FFB) if rl % 16 else v(16, 128),
            v(4, 256, D),
            v(4, 128, D),
            vf(4, 32, 128),
            vf(8, 2048),
            v(LEN, D),
            vf(512, LEN),
            vf(TILES, 128, 128),
            vf(256, LEN),
            vf(512, D),
            v(512, D),
            v(D, 512),
            v(2, 256, D),
            v(D, 512),
            vf(512, 2 * FFB),
            vf(512, FFB),
            v(512, FFB),
            v(512, 2 * FFB),
            vf(512, D),
            v(2, D, 3 * FFB),
            v(2, D, 3 * FFB),
            sem((6,)),
            sem((10,)),
            sem((10,)),
            sem((2, wide)),
            sem((2,)),
            sem((5, wide)),
            sem((5, wide)),
            sem((4, wide)),
            sem((4, wide)),
            sem((4, 2, wide)),
            sem((4, 2, wide)),
            sem((4, 2, wide)),
            sem((4, 2, wide)),
            sem((2,)),
            sem((2,)),
            sem((2,)),
        ],
        compiler_params=pltpu.CompilerParams(
            dimension_semantics=("arbitrary",), vmem_limit_bytes=FORWARD_VMEM, collective_id=0, has_side_effects=True
        ),
        cost_estimate=cost(60),
        name="forward",
    )(ps_s, vl_s, hid, enc, cot, tab, hot, ps, pc, pf, gain_s, gain_c, gain_f)


def cross_backward_kernel(
    wide, h1, ef, d2, w, gain, q, kv, at, p, gff,
    gw_o, d1_o, gg_o, ge_o, gep_o, o1, o2, o3,
    d2b, d2t, nct, eft, get, do, dp, ds, dq, dkv, buf, landed, rx, ry, rz, send, recv, load, fs, fr, zs, zr,
):
    n = pl.program_id(0)
    slot = lax.rem(n, 2)
    core = CoreSum(n, buf, landed, send, recv)
    d, wi, me, pn, yn, dn = place_here()
    y = me // 2
    mine = pl.ds(pl.multiple_of(d * 256, 128), 256)
    other = pl.ds(pl.multiple_of(256 - d * 256, 128), 256)
    late = pl.ds(512, 640)
    third = pl.ds(1152, 384)
    loads = [
        pltpu.make_async_copy(gff.at[:, :, :, mine], o1, load.at[0]),
        pltpu.make_async_copy(gff.at[0, :, :, late], o2, load.at[1]),
        pltpu.make_async_copy(gff.at[:, wi, :, third], o3, load.at[2]),
    ]

    def zcopy(k):
        row = lax.rem(wi + k, wide)
        return remote(gff.at[:, row, :, third], rz.at[wi], zs.at[k], zr.at[wi], (d, row, me))

    def zgot(k):
        row = lax.rem(wi + k, wide)
        return remote(rz.at[row], rz.at[row], zs.at[k], zr.at[row], (d, row, me))

    sends = [
        remote(gff.at[:, :, :, other], rx, fs.at[0], fr.at[0], (1 - d, wi, me)),
        remote(gff.at[1, :, :, late], ry, fs.at[1], fr.at[1], (d, wi, yn)),
    ]

    @pl.when(n == 0)
    def _():
        def norm_rows(r):
            d2b[r, :] = d2[r, :].astype(bf16)
            d1_o[r, :] = jnp.zeros((64, D), f32)
            dp[r, :] = normed(h1[r, :], gain[...])

        for copy in loads:
            copy.start()
        greet(((d, wi, pn), (d, wi, yn), (1 - d, wi, me)), wide)
        for copy in sends:
            copy.start()
        loop(1, wide, lambda k: zcopy(k).start())
        rows_loop(512, 64, norm_rows, unroll=4)
        nct[...] = dp[...].astype(bf16).T
        d2t[...] = d2b[...].T
        eft[...] = ef[...].T
        get[...] = jnp.zeros((D, ENC), f32)

    do[...] = nn(d2b[...], w[0, :, 192:384]).astype(bf16)
    for h in range(3):
        hs = slice(h * DHEAD, (h + 1) * DHEAD)
        vs = slice(HD + h * DHEAD, HD + (h + 1) * DHEAD)
        dp[:, :ENC] = nn(do[:, hs], kv[0, vs, :])

        def grad_rows(r, h=h, hs=hs):
            delta = jnp.sum(do[r, hs].astype(f32) * at[0, r, hs].astype(f32), axis=1, keepdims=True)
            ds[r, :] = (p[0, h, r, :].astype(f32) * (dp[r, :ENC] - delta)).astype(bf16)

        rows_loop(512, 16, grad_rows, unroll=32)
        dq[:, hs] = nt(ds[...], kv[0, hs, :]).astype(bf16)
        dkv[hs, :] = tn(q[0, :, hs], ds[...]).astype(bf16)
        dkv[vs, :] = tn(do[:, hs], p[0, h]).astype(bf16)
    d1_o[...] += nt(dq[...], w[0, :, 0:192])
    get[...] += nn(w[0, :, 384:768], dkv[...])
    buf[slot, :, 0:384] = jnp.concatenate([nn(nct[...], dq[...]), nn(d2t[...], at[0])], axis=1).astype(bf16)
    buf[slot, :, 384:768] = nt(eft[...], dkv[...]).astype(bf16)
    core.finish(gw_o)

    @pl.when(n == 3)
    def _():
        gg_o[...] = jnp.zeros((1, D), f32)

        def back_rows(r):
            dx, gg = norm_back(h1[r, :], gain[...], d1_o[r, :])
            d1_o[r, :] = d2[r, :] + dx
            gg_o[...] += gg

        rows_loop(512, 64, back_rows, unroll=2)
        for i in range(2):
            half = slice(i * 128, (i + 1) * 128)
            cols = lambda blk: pl.ds(pl.multiple_of(blk * 128, 128), 128)
            ge_o[half, :] = get[:, cols((me, 3 - me)[i])].T
            gep_o[half, :] = get[:, cols((pn, 3 - pn)[i])].T.astype(bf16)
        for copy in loads:
            copy.wait()
        for copy in sends:
            copy.wait()
        add_into(o1, rx)
        add_into(o2, ry)
        loop(1, wide, lambda k: zgot(k).wait_recv())
        rl = o3.shape[1]
        part = 64 if rl % 64 == 0 else rl
        for i in range(2):
            for j in range(rl // part):
                r = slice(j * part, (j + 1) * part)

                def add(k, total, i=i, r=r):
                    return total + rz[lax.rem(wi + k, wide), i, r, :].astype(f32)

                o3[i, r, :] = lax.fori_loop(1, wide, add, o3[i, r, :].astype(f32)).astype(bf16)
        loop(1, wide, lambda k: zcopy(k).wait_send())


def cross_backward(wide, h1, ef, d2, w, gain, q, kv, at, p, gff):
    rl = D // wide
    return pl.pallas_call(
        partial(cross_backward_kernel, wide),
        grid=(4,),
        in_specs=[
            whole((512, D)),
            whole((ENC, D)),
            whole((512, D)),
            slab((D, D)),
            whole((1, D)),
            slab((512, HD)),
            slab((2 * HD, ENC)),
            slab((512, HD)),
            slab((3, 512, ENC)),
            ANY,
        ],
        out_specs=[
            pair_slab((D, D)),
            whole((512, D)),
            whole((1, D)),
            whole((256, D)),
            whole((256, D)),
            whole((2, wide, rl, 256)),
            whole((wide, rl, 640)),
            whole((2, rl, 384)),
        ],
        out_shape=[
            out((2, D, D), bf16),
            out((512, D), f32),
            out((1, D), f32),
            out((256, D), f32),
            out((256, D), bf16),
            out((2, wide, rl, 256), bf16),
            out((wide, rl, 640), bf16),
            out((2, rl, 384), bf16),
        ],
        scratch_shapes=[
            pltpu.VMEM((512, D), bf16),
            pltpu.VMEM((D, 512), bf16),
            pltpu.VMEM((D, 512), bf16),
            pltpu.VMEM((D, ENC), bf16),
            pltpu.VMEM((D, ENC), f32),
            pltpu.VMEM((512, HD), bf16),
            pltpu.VMEM((512, D), f32),
            pltpu.VMEM((512, ENC), bf16),
            pltpu.VMEM((512, HD), bf16),
            pltpu.VMEM((2 * HD, ENC), bf16),
            pltpu.VMEM((2, D, D), bf16),
            pltpu.VMEM((2, D, D), bf16),
            pltpu.VMEM((2, wide, rl, 256), bf16),
            pltpu.VMEM((wide, rl, 640), bf16),
            pltpu.VMEM((wide, 2, rl, 384), bf16),
            pltpu.SemaphoreType.DMA((1,)),
            pltpu.SemaphoreType.DMA((2,)),
            pltpu.SemaphoreType.DMA((3,)),
            pltpu.SemaphoreType.DMA((2,)),
            pltpu.SemaphoreType.DMA((2,)),
            pltpu.SemaphoreType.DMA((wide,)),
            pltpu.SemaphoreType.DMA((wide,)),
        ],
        compiler_params=params(3),
        cost_estimate=cost(14),
        name="cross_backward",
    )(h1, ef, d2, w, gain, q, kv, at, p, gff.reshape(2, wide, rl, 3 * FFB))


def self_backward_kernel(
    wide, xf, d1, w, gain, q, kv, at, p, gcr, o1, o2, o3, outp,
    gw_o, g_o, gp_o, dl_o, b1, c2, e1, e2, out_o,
    c1, cy1, d1b, d1t, nft, nqt, gt, gq, do, dp, ds, dq, dkv, buf, landed, s1, f2, s3, rx, ry, ry1, ry3, rz1, rz2,
    send, recv, load, fs, fr, zs, zr,
):
    n = pl.program_id(0)
    blks = own_blocks()
    slot = lax.rem(n, 2)
    core = CoreSum(n, buf, landed, send, recv)
    d, wi, me, pn, yn, dn = place_here()
    y = me // 2
    mine = pl.ds(pl.multiple_of(d * 256, 128), 256)
    other = pl.ds(pl.multiple_of(256 - d * 256, 128), 256)
    late = pl.ds(512, 256)
    loads = [
        pltpu.make_async_copy(gcr.at[:, :, :, mine], c1, load.at[0]),
        pltpu.make_async_copy(gcr.at[0, :, :, late], c2, load.at[1]),
        pltpu.make_async_copy(o1.at[0], s1, load.at[2]),
        pltpu.make_async_copy(o2.at[wi], f2, load.at[3]),
        pltpu.make_async_copy(outp.at[0], out_o.at[y], load.at[4]),
        pltpu.make_async_copy(o3.at[0], s3, load.at[5]),
    ]
    sends = [
        remote(o1.at[1], ry1, fs.at[0], fr.at[0], (d, wi, yn)),
        remote(gcr.at[:, :, :, other], rx, fs.at[1], fr.at[1], (1 - d, wi, me)),
        remote(gcr.at[1, :, :, late], ry, fs.at[2], fr.at[2], (d, wi, yn)),
        remote(outp.at[1], out_o.at[y], fs.at[3], fr.at[3], (d, wi, dn)),
    ]
    out_got = remote(out_o.at[1 - y], out_o.at[1 - y], fs.at[3], fr.at[3], (d, wi, dn))
    y_cross = remote(c1.at[1], cy1, fs.at[4], fr.at[4], (d, wi, yn))
    y_third = remote(o3.at[1], ry3, fs.at[5], fr.at[5], (d, wi, yn))

    def zcopy(path, k):
        row = lax.rem(wi + k, wide)
        src, dst = ((s1, rz1), (o2, rz2))[path]
        return remote(src.at[row], dst.at[wi], zs.at[path, k], zr.at[path, wi], (d, row, me))

    def zgot(path, k):
        row = lax.rem(wi + k, wide)
        ref = (rz1, rz2)[path].at[row]
        return remote(ref, ref, zs.at[path, k], zr.at[path, row], (d, row, me))

    @pl.when(n == 0)
    def _():
        def cast_rows(r):
            d1b[r, :] = d1[r, :].astype(bf16)
            gq[r, :] = jnp.zeros((64, D), f32)

        for copy in loads:
            copy.start()
        greet(((d, wi, pn), (d, wi, yn), (1 - d, wi, me), (d, wi, dn)), wide)
        for copy in sends[:3]:
            copy.start()
        loop(1, wide, lambda k: zcopy(1, k).start())
        rows_loop(512, 64, cast_rows)
        d1t[...] = d1b[...].T
        for i in range(4):
            part = normed(xf[i * 256 : (i + 1) * 256, :].astype(f32), gain[...]).astype(bf16)
            nft[:, i * 256 : (i + 1) * 256] = part.T
        for i in range(2):
            part = normed(xf[block_rows(blks[i]), :].astype(f32), gain[...]).astype(bf16)
            nqt[:, i * 256 : (i + 1) * 256] = part.T
        gt[...] = jnp.zeros((D, LEN), f32)

    @pl.when(n == 1)
    def _():
        sends[3].start()
        y_third.start()

    @pl.when(n == 2)
    def _():
        loads[2].wait()
        sends[0].wait_recv()
        add_into(s1, ry1)
        loop(1, wide, lambda k: zcopy(0, k).start())
        loads[0].wait()
        sends[1].wait_recv()
        add_into(c1, rx)
        y_cross.start()

    dl_o[0] = jnp.zeros((3, 2048), f32)
    do[...] = nn(d1b[...], w[0, :, 192:384]).astype(bf16)
    for h in range(3):
        hs = slice(h * DHEAD, (h + 1) * DHEAD)
        vs = slice(HD + h * DHEAD, HD + (h + 1) * DHEAD)
        dk = jnp.zeros((DHEAD, LEN), f32)
        dv = jnp.zeros((DHEAD, LEN), f32)
        for i in range(2):
            half = slice(i * 256, (i + 1) * 256)
            dp[...] = nn(do[half, hs], kv[0, vs, :])

            def grad_rows(rr, i=i, h=h, hs=hs):
                rows = pl.ds(i * 256 + rr.start, ROWS)
                delta = jnp.sum(do[rows, hs].astype(f32) * at[0, rows, hs].astype(f32), axis=1, keepdims=True)
                ds[rr, :] = (p[0, h, rows, :].astype(f32) * (dp[rr, :] - delta)).astype(bf16)

            rows_loop(256, ROWS, grad_rows, unroll=16)
            upper, lower = ds[:128, :].astype(f32), ds[128:, :].astype(f32)
            part = jnp.concatenate(
                [
                    upper[:, :896] + lower[:, 128:],
                    upper[:, 896:],
                    jnp.zeros((128, 128), f32),
                    lower[:, :128],
                ],
                axis=1,
            )
            height = 128
            while height > 1:
                height //= 2
                part = part[:height] + pltpu.roll(part[height:], SPAN - height, 1)
            where = pl.ds(pl.multiple_of(768 - 256 * blks[i], 128), SPAN)
            dl_o[0, h : h + 1, where] += pltpu.roll(part, 255, 1)
            dq[half, hs] = nt(ds[...], kv[0, hs, :]).astype(bf16)
            dk = dk + tn(q[0, half, hs], ds[...])
            dv = dv + tn(do[half, hs], p[0, h, half, :])
        dkv[hs, :] = dk.astype(bf16)
        dkv[vs, :] = dv.astype(bf16)
    gq[...] += nt(dq[...], w[0, :, 0:192])
    gt[...] += nn(w[0, :, 384:768], dkv[...])
    buf[slot, :, 0:384] = jnp.concatenate([nn(nqt[...], dq[...]), nn(d1t[...], at[0])], axis=1).astype(bf16)
    buf[slot, :, 384:768] = nt(nft[...], dkv[...]).astype(bf16)
    core.finish(gw_o)

    @pl.when(n == 3)
    def _():
        for i in range(2):
            half = slice(i * 256, (i + 1) * 256)
            g_o[half, :] = gq[half, :] + gt[:, block_rows(blks[i])].T
            gp_o[half, :] = gt[:, block_rows((pn, 3 - pn)[i])].T.astype(bf16)
        loads[1].wait()
        sends[2].wait_recv()
        add_into(c2, ry)
        loads[3].wait()
        for path in (1, 0):
            loop(1, wide, lambda k, path=path: zgot(path, k).wait_recv())

        def put(ref, cols):
            def store(r, total):
                ref[r, cols] = total.astype(bf16)

            return store

        sum_line(wide, s1.at[wi], rz1, put(e1, slice(None)))
        sum_line(wide, f2, rz2, put(e2, slice(0, 640)))
        loads[5].wait()
        y_third.wait_recv()
        e2[:, 640:1024] = s3[...] + ry3[...]
        y_cross.wait_recv()

        def add_cross(k):
            b1[k] = c1[0, k] + cy1[k]

        loop(0, wide, add_cross)
        out_got.wait_recv()
        loads[4].wait()
        for copy in (*sends, y_cross, y_third):
            copy.wait_send()
        for path in (0, 1):
            loop(1, wide, lambda k, path=path: zcopy(path, k).wait_send())


def self_backward(wide, xf, d1, w, gain, q, kv, at, p, gcr, o1, o2, o3, outp):
    rl = D // wide
    return pl.pallas_call(
        partial(self_backward_kernel, wide),
        grid=(4,),
        in_specs=[
            whole((LEN, D)),
            whole((512, D)),
            slab((D, D)),
            whole((1, D)),
            slab((512, HD)),
            slab((2 * HD, LEN)),
            slab((512, HD)),
            slab((3, 512, LEN)),
            ANY,
            ANY,
            ANY,
            ANY,
            pl.BlockSpec(memory_space=pltpu.VMEM),
        ],
        out_specs=[
            pair_slab((D, D)),
            whole((512, D)),
            whole((512, D)),
            slab((3, 2048)),
            whole((wide, rl, 256)),
            whole((wide, rl, 256)),
            whole((rl, 256)),
            whole((rl, 1024)),
            ANY,
        ],
        out_shape=[
            out((2, D, D), bf16),
            out((512, D), f32),
            out((512, D), bf16),
            out((4, 3, 2048), f32),
            out((wide, rl, 256), bf16),
            out((wide, rl, 256), bf16),
            out((rl, 256), bf16),
            out((rl, 1024), bf16),
            out((2, 256, D), bf16),
        ],
        scratch_shapes=[
            pltpu.VMEM((2, wide, rl, 256), bf16),
            pltpu.VMEM((wide, rl, 256), bf16),
            pltpu.VMEM((512, D), bf16),
            pltpu.VMEM((D, 512), bf16),
            pltpu.VMEM((D, LEN), bf16),
            pltpu.VMEM((D, 512), bf16),
            pltpu.VMEM((D, LEN), f32),
            pltpu.VMEM((512, D), f32),
            pltpu.VMEM((512, HD), bf16),
            pltpu.VMEM((256, LEN), f32),
            pltpu.VMEM((256, LEN), bf16),
            pltpu.VMEM((512, HD), bf16),
            pltpu.VMEM((2 * HD, LEN), bf16),
            pltpu.VMEM((2, D, D), bf16),
            pltpu.VMEM((2, D, D), bf16),
            pltpu.VMEM((wide, rl, 256), bf16),
            pltpu.VMEM((rl, 640), bf16),
            pltpu.VMEM((rl, 384), bf16),
            pltpu.VMEM((2, wide, rl, 256), bf16),
            pltpu.VMEM((wide, rl, 256), bf16),
            pltpu.VMEM((wide, rl, 256), bf16),
            pltpu.VMEM((rl, 384), bf16),
            pltpu.VMEM((wide, rl, 256), bf16),
            pltpu.VMEM((wide, rl, 640), bf16),
            pltpu.SemaphoreType.DMA((1,)),
            pltpu.SemaphoreType.DMA((2,)),
            pltpu.SemaphoreType.DMA((6,)),
            pltpu.SemaphoreType.DMA((6,)),
            pltpu.SemaphoreType.DMA((6,)),
            pltpu.SemaphoreType.DMA((2, wide)),
            pltpu.SemaphoreType.DMA((2, wide)),
        ],
        compiler_params=params(4),
        cost_estimate=cost(25),
        name="self_backward",
    )(xf, d1, w, gain, q, kv, at, p, gcr.reshape(2, wide, rl, D), o1, o2, o3, outp)


def reduce_kernel(
    wide, se, b1, c2, e1, e2, gxo, gxp, geo, gep, xf, d1, gain, gfeed, gcross, tg,
    gin_o, gen_o, sg_o, st_o, ff_o, cr_o, se_o,
    a1, a2, rx, ry, ry1, rzs1, rzs2, rzc1, rzc2, fs, fc, xs1, xs2, xc1, xc2, x1, x2,
    rgx, rge, tmp_in, tmp_en, back_in, back_en, rows_f, sg, st, rsg, rst, rsgz, rstz,
    load, ms, mr, ts, tr, zs, zr, ss, sr, os,
):
    d, w, n, pn, yn, dn = place_here()
    y = n // 2
    pair, line_y, diag, line_x = (d, w, pn), (d, w, yn), (d, w, dn), (1 - d, w, n)
    mine = pl.ds(pl.multiple_of(d * 256, 128), 256)
    other = pl.ds(pl.multiple_of(256 - d * 256, 128), 256)
    late = pl.ds(512, 256)
    loads = [
        pltpu.make_async_copy(se.at[:, :, :, mine], a1, load.at[0]),
        pltpu.make_async_copy(se.at[0, :, :, late], a2, load.at[1]),
        pltpu.make_async_copy(geo, tmp_en, load.at[2]),
    ]
    for copy in loads:
        copy.start()
    greet((pair, line_y, diag, line_x), wide)
    turn = lambda i, src, dst, dev: remote(src, dst, ts.at[i], tr.at[i], dev)
    put = [
        turn(0, se.at[:, :, :, other], rx, line_x),
        turn(2, se.at[1, :, :, late], ry, line_y),
        turn(3, e1, x1, line_x),
        turn(4, e2, x2, line_x),
    ]
    cross = [
        remote(gxp, rgx, ms.at[0], mr.at[0], pair),
        remote(gep, rge, ms.at[1], mr.at[1], pair),
    ]
    z_refs = ((a1, rzs1), (a2, rzs2), (b1, rzc1), (c2, rzc2))

    def zcopy(path, k):
        row = lax.rem(w + k, wide)
        src, dst = z_refs[path]
        src = src.at[0, row] if path == 0 else src.at[row]
        return remote(src, dst.at[w], zs.at[path, k], zr.at[path, w], (d, row, n))

    def zgot(path, k):
        row = lax.rem(w + k, wide)
        ref = z_refs[path][1].at[row]
        return remote(ref, ref, zs.at[path, k], zr.at[path, row], (d, row, n))

    def zstart(path):
        loop(1, wide, lambda k: zcopy(path, k).start())

    def zwait(path):
        loop(1, wide, lambda k: zgot(path, k).wait_recv())

    cross[0].start()
    cross[1].start()
    put[0].start()
    put[1].start()
    zstart(3)
    zstart(2)

    sg[...] = jnp.zeros((8, D), f32)
    sg[1:2, :] = gcross[...]
    sg[2:3, :] = gfeed[...]
    st[...] = tg[...]
    cross[0].wait_recv()
    own = (n, dn)
    for i in (1, 0):

        def back(r, i=i):
            x = xf[own[i], r, :].astype(f32)
            dx, gg = norm_back(x, gain[...], gxo[i, r, :] + rgx[i, r, :].astype(f32))
            total = d1[i, r, :] + dx
            sg[0:1, :] += gg
            if i == 0:
                rows_f[0, r, :] = total
            else:
                tmp_in[r, :] = total.astype(bf16)

        rows_loop(256, 32, back, unroll=2)
        if i == 1:
            in_send = remote(tmp_in, back_in, ms.at[3], mr.at[3], diag)
            in_send.start()
    in_local = pltpu.make_async_copy(rows_f.at[0], gin_o.at[y], os.at[0])
    in_local.start()
    cross[1].wait_recv()
    loads[2].wait()
    back_en[0] = (tmp_en[1] + rge[1].astype(f32)).astype(bf16)
    en_send = remote(back_en.at[0], back_en.at[1], ms.at[4], mr.at[4], diag)
    en_send.start()
    tmp_en[0] = tmp_en[0] + rge[0].astype(f32)
    en_local = pltpu.make_async_copy(tmp_en.at[0], gen_o.at[y], os.at[1])
    en_local.start()

    def small(j, dev):
        return (
            remote(sg, rsg.at[j], ss.at[0, j], sr.at[0, j], dev),
            remote(st, rst.at[j], ss.at[1, j], sr.at[1, j], dev),
        )

    def small_add(j, dev):
        for copy in small(j, dev):
            copy.wait()
        sg[...] += rsg[j]
        st[...] += rst[j]

    def small_line(k):
        dev = (d, lax.rem(w + k, wide), n)
        return (
            remote(sg, rsgz.at[w], ss.at[0, 3 + k], sr.at[0, 3 + w], dev),
            remote(st, rstz.at[w], ss.at[1, 3 + k], sr.at[1, 3 + w], dev),
        )

    def start_all(copies):
        for copy in copies:
            copy.start()

    start_all(small(0, pair))
    small_add(0, pair)
    start_all(small(1, line_y))
    loads[1].wait()
    put[1].wait_recv()
    add_into(a2, ry)
    zstart(1)
    loads[0].wait()
    put[0].wait_recv()
    add_into(a1, rx)
    y1 = turn(5, a1.at[1], ry1, line_y)
    y1.start()
    put[2].start()
    put[3].start()
    small_add(1, line_y)
    start_all(small(2, line_x))
    small_add(2, line_x)
    loop(1, wide, lambda k: start_all(small_line(k)))
    rsgz[w] = sg[...]
    rstz[w] = st[...]

    def keep(ref, cols):
        def store(r, total):
            ref[r, cols] = total.astype(bf16)

        return store

    everything = slice(None)
    zwait(3)
    sum_line(wide, c2.at[w], rzc2, keep(fc, late))
    f_c2 = turn(6, fc.at[:, late], xc2, line_x)
    f_c2.start()
    zwait(2)
    sum_line(wide, b1.at[w], rzc1, keep(fc, mine))
    f_c1 = turn(7, fc.at[:, mine], xc1, line_x)
    f_c1.start()
    y1.wait_recv()
    rl = e1.shape[0]

    def add_side(k):
        a1[0, k] = a1[0, k] + ry1[k]

    loop(0, wide, add_side)
    zstart(0)

    def small_wait(k):
        row = lax.rem(w + k, wide)
        for i, ref in enumerate((rsgz, rstz)):
            remote(ref.at[row], ref.at[row], ss.at[i, 3], sr.at[i, 3 + row], line_x).wait_recv()

    loop(1, wide, small_wait)
    sg_o[...] = lax.fori_loop(1, wide, lambda k, t: t + rsgz[k], rsgz[0])
    st_o[...] = lax.fori_loop(1, wide, lambda k, t: t + rstz[k], rstz[0])

    zwait(1)
    sum_line(wide, a2.at[w], rzs2, keep(fs, late))
    f_s2 = turn(8, fs.at[:, late], xs2, line_x)
    f_s2.start()

    in_send.wait_recv()

    def widen(r):
        rows_f[1, r, :] = back_in[r, :].astype(f32)

    rows_loop(256, 64, widen)
    in_last = pltpu.make_async_copy(rows_f.at[1], gin_o.at[1 - y], os.at[2])
    in_last.start()
    en_send.wait_recv()
    tmp_en[1] = back_en[1].astype(f32)
    en_last = pltpu.make_async_copy(tmp_en.at[1], gen_o.at[1 - y], os.at[3])
    en_last.start()

    put[2].wait_recv()
    put[3].wait_recv()
    ff_o[:, mine] = e1[...].astype(f32)
    ff_o[:, other] = x1[...].astype(f32)
    ff_o[:, pl.ds(512, 1024)] = e2[...].astype(f32) + x2[...].astype(f32)
    f_c1.wait_recv()
    f_c2.wait_recv()
    cr_o[:, mine] = fc[:, mine].astype(f32)
    cr_o[:, other] = xc1[...].astype(f32)
    cr_o[:, late] = fc[:, late].astype(f32) + xc2[...].astype(f32)
    zwait(0)
    sum_line(wide, a1.at[0, w], rzs1, keep(fs, mine))
    f_s1 = turn(9, fs.at[:, mine], xs1, line_x)
    f_s1.start()
    f_s2.wait_recv()
    se_o[:, mine] = fs[:, mine].astype(f32)
    se_o[:, late] = fs[:, late].astype(f32) + xs2[...].astype(f32)
    f_s1.wait_recv()
    se_o[:, other] = xs1[...].astype(f32)

    for copy in (in_local, en_local, in_last, en_last):
        copy.wait()
    for copy in (*cross, in_send, en_send, *put, y1, f_c1, f_c2, f_s1, f_s2):
        copy.wait_send()

    def finish(k):
        for path in range(4):
            zcopy(path, k).wait_send()
        for copy in small_line(k):
            copy.wait_send()

    loop(1, wide, finish)


def reduce_all(wide, se, b1, c2, e1, e2, gxo, gxp, geo, gep, xf, d1, gain, gfeed, gcross, tg):
    rl = D // wide
    se = se.reshape(2, wide, rl, D)
    sem = pltpu.SemaphoreType.DMA
    V = pl.BlockSpec(memory_space=pltpu.VMEM)
    v = lambda *shape: pltpu.VMEM(shape, bf16)
    return pl.pallas_call(
        partial(reduce_kernel, wide),
        in_specs=[ANY, V, V, V, V, V, ANY, ANY, ANY, V, V, V, V, V, V],
        out_specs=[ANY, ANY, V, V, V, V, V],
        out_shape=[
            out((2, 256, D), f32),
            out((2, 128, D), f32),
            out((8, D), f32),
            out((32, 128), f32),
            out((rl, 2 * D), f32),
            out((rl, D), f32),
            out((rl, D), f32),
        ],
        scratch_shapes=[
            v(2, wide, rl, 256),
            v(wide, rl, 256),
            v(2, wide, rl, 256),
            v(wide, rl, 256),
            v(wide, rl, 256),
            v(wide, rl, 256),
            v(wide, rl, 256),
            v(wide, rl, 256),
            v(wide, rl, 256),
            v(rl, D),
            v(rl, D),
            v(rl, 256),
            v(rl, 256),
            v(rl, 256),
            v(rl, 256),
            v(rl, 256),
            v(rl, 1024),
            v(2, 256, D),
            v(2, 128, D),
            v(256, D),
            pltpu.VMEM((2, 128, D), f32),
            v(256, D),
            v(2, 128, D),
            pltpu.VMEM((2, 256, D), f32),
            pltpu.VMEM((8, D), f32),
            pltpu.VMEM((32, 128), f32),
            pltpu.VMEM((3, 8, D), f32),
            pltpu.VMEM((3, 32, 128), f32),
            pltpu.VMEM((wide, 8, D), f32),
            pltpu.VMEM((wide, 32, 128), f32),
            sem((5,)),
            sem((5,)),
            sem((5,)),
            sem((10,)),
            sem((10,)),
            sem((4, wide)),
            sem((4, wide)),
            sem((2, 3 + wide)),
            sem((2, 3 + wide)),
            sem((4,)),
        ],
        compiler_params=pltpu.CompilerParams(
            collective_id=1, has_side_effects=True, vmem_limit_bytes=VMEM_LIMIT
        ),
        name="reduce_all",
    )(se, b1, c2, e1, e2, gxo, gxp, geo, gep, xf, d1, gain, gfeed, gcross, tg)


def on_device(
    wide, hidden_in, encoder_out, cotangent, piece_starts, valid_lengths, bucket_table,
    gain_self, gain_cross, gain_feed, relative_bias, *mats
):
    me = lax.axis_index("narrow")
    sq, sk, sv, so, cq, ck, cv, co, gate, up, down = mats
    ps = jnp.concatenate((sq, so, sk, sv), axis=1)
    pc = jnp.concatenate((cq, co, ck, cv), axis=1)
    pf = jnp.concatenate((gate, up, down), axis=1)
    tab = jnp.pad(relative_bias.T, ((0, 29), (0, 96)))
    padded = jnp.pad(bucket_table, (0, 1), constant_values=-1)
    hot = (padded[None, :] == jnp.arange(BUCKETS)[:, None]).astype(f32)
    gains = [g.reshape(1, D) for g in (gain_self, gain_cross, gain_feed)]
    (
        xf, ws, wc, _, gff, ef, q, kv, at, p, cqh, ckv, cat, cp, h1, outp, d2, gg_feed,
    ) = forward(
        wide, piece_starts, valid_lengths, hidden_in[:, 0], encoder_out[:, 0], cotangent[:, 0], tab, hot, ps, pc, pf, *gains
    )
    ws, wc = (g.reshape(4, D, D) for g in (ws, wc))
    xs, es = xf.reshape(LEN, D), ef.reshape(ENC, D)
    gcr, d1, gg_cross, geo, gep, o1, o2, o3 = cross_backward(wide, h1, es, d2, wc, gains[1], cqh, ckv, cat, cp, gff)
    gse, gxo, gxp, dl, b1, c2, e1, e2, outs = self_backward(
        wide, xs, d1, ws, gains[0], q, kv, at, p, gcr, o1, o2, o3, outp.reshape(2, 256, D)
    )
    tg = lax.dot_general(hot, dl.reshape(12, 2048), (((1,), (1,)), ((), ())), precision=precise)
    order = jnp.arange(12) // 3 ^ me ^ 1
    tg = tg.reshape(BUCKETS, 4, 3)
    tg = sum(jnp.where(order == k, jnp.tile(tg[:, k], (1, 4)), 0.0) for k in range(4))
    tg = jnp.pad(tg, ((0, 0), (0, 116)))
    two = lambda a: a.reshape(2, -1, D)
    gin, gen, sg, st, f, b, a = reduce_all(
        wide, gse, b1, c2, e1, e2, two(gxo), two(gxp), two(geo), two(gep), xf, two(d1), gains[0], gg_feed, gg_cross, tg
    )
    tg = lax.dynamic_slice_in_dim(st, me * 3, 3, axis=1)
    return (
        outs[:, None], gin[:, None], gen[:, None],
        sg[0], sg[1], sg[2], tg,
        a[:, :192], a[:, 384:576], a[:, 576:], a[:, 192:384],
        b[:, :192], b[:, 384:576], b[:, 576:], b[:, 192:384],
        f[:, :512], f[:, 512:1024], f[:, 1024:],
    )


def solution(mesh):
    rows = P(None, ("dp", "wide"), "narrow", None)
    mat = P("wide", "narrow")
    return jax.shard_map(
        partial(on_device, mesh.shape["wide"]),
        mesh=mesh,
        in_specs=(rows, rows, rows, P(None, ("dp", "wide")), P(None, ("dp", "wide")), P(), P(), P(), P(), P(None, "narrow"))
        + (mat,) * 11,
        out_specs=(rows, rows, rows, P(), P(), P(), P(None, "narrow")) + (mat,) * 11,
        check_vma=False,
    )
```

```python
import math
from functools import partial

import jax
import jax.numpy as jnp
from jax import lax
from jax.experimental import pallas as pl
from jax.experimental.pallas import tpu as pltpu
from jax.sharding import PartitionSpec as P

D = 768
HD = 192
HEADS = 12
DHEAD = 64
FFB = 512
BUCKETS = 32
LEN = 1024
ENC = 512
PIC = 256
TILES = 11
SPAN = 1280
ROWS = 16

precise = lax.Precision.HIGHEST
epsilon = 1e-06
masked_value = -1e30
f32 = jnp.float32
bf16 = jnp.bfloat16
MESH = pl.DeviceIdType.MESH
ANY = pl.BlockSpec(memory_space=pl.ANY)
VMEM_LIMIT = 60 << 20


def nn(a, b):
    return lax.dot_general(a, b, (((1,), (0,)), ((), ())), preferred_element_type=f32)


def nt(a, b):
    return lax.dot_general(a, b, (((1,), (1,)), ((), ())), preferred_element_type=f32)


def tn(a, b):
    return lax.dot_general(a, b, (((0,), (0,)), ((), ())), preferred_element_type=f32)


def rows_loop(total, step, body, unroll=1):
    def run(i, carry):
        body(pl.ds(pl.multiple_of(i * step, step), step))
        return carry

    lax.fori_loop(0, total // step, run, 0, unroll=unroll)


def normed(x, gain):
    factor = lax.rsqrt(jnp.mean(x * x, axis=1, keepdims=True) + epsilon)
    return x * factor * gain


def norm_back(x, gain, upstream):
    factor = lax.rsqrt(jnp.mean(x * x, axis=1, keepdims=True) + epsilon)
    weighted = upstream * gain
    inner = jnp.sum(weighted * x, axis=1, keepdims=True)
    dx = weighted * factor - x * (factor * factor * factor * inner * (1.0 / D))
    return dx, jnp.sum(upstream * x * factor, axis=0, keepdims=True)


def own_blocks():
    me = lax.axis_index("narrow")
    return (me, 3 - me)


def block_rows(blk):
    return pl.ds(pl.multiple_of(blk * 256, 256), 256)


def softmax_rows(v):
    e = jnp.exp(v - jnp.max(v, axis=1, keepdims=True))
    return e * (1.0 / jnp.sum(e, axis=1, keepdims=True))


def place_here():
    d, w, n = lax.axis_index("dp"), lax.axis_index("wide"), lax.axis_index("narrow")
    return d, w, n, n + 1 - 2 * lax.rem(n, 2), lax.rem(n + 2, 4), 3 - n


def remote(src, dst, send, recv, dev):
    return pltpu.make_async_remote_copy(
        src_ref=src, dst_ref=dst, send_sem=send, recv_sem=recv, device_id=dev, device_id_type=MESH
    )


def greet(devs, wide=1):
    d, w, n = place_here()[:3]
    barrier = pltpu.get_barrier_semaphore()
    for dev in devs:
        pl.semaphore_signal(barrier, inc=1, device_id=dev, device_id_type=MESH)

    def line(k, carry):
        dev = (d, lax.rem(w + k, wide), n)
        pl.semaphore_signal(barrier, inc=1, device_id=dev, device_id_type=MESH)
        return carry

    lax.fori_loop(1, wide, line, 0)
    pl.semaphore_wait(barrier, wide - 1 + len(devs))


def loop(lo, hi, body):
    def run(k, carry):
        body(k)
        return carry

    lax.fori_loop(lo, hi, run, 0)


def add_into(dst, src):
    shape = dst.shape
    rl = shape[-2]
    step = 64 if rl % 64 == 0 else rl
    lead = shape[:-2]

    def one(*index):
        for j in range(rl // step):
            spot = index + (slice(j * step, (j + 1) * step), slice(None))
            dst[spot] = dst[spot] + src[spot]

    if len(lead) == 1:
        loop(0, lead[0], one)
    else:
        for i in range(lead[0]):
            loop(0, lead[1], partial(one, i))


def sum_line(wide, own, parts, store):
    w = lax.axis_index("wide")
    rl = own.shape[0]
    step = 64 if rl % 64 == 0 else rl
    for j in range(rl // step):
        r = slice(j * step, (j + 1) * step)

        def add(k, total, r=r):
            return total + parts[lax.rem(w + k, wide), r, :].astype(f32)

        store(r, lax.fori_loop(1, wide, add, own[r, :].astype(f32)))


def core_devs():
    d, w, n, pn, yn, dn = place_here()
    return (d, w, pn)


class CoreSum:
    def __init__(self, step, buf, landed, send, recv):
        self.step, self.buf, self.landed, self.send, self.recv = step, buf, landed, send, recv
        self.side = step // 2

    def copy(self):
        return remote(
            self.buf.at[0], self.landed.at[self.side], self.send.at[0], self.recv.at[self.side], core_devs()
        )

    def finish(self, result):
        @pl.when(lax.rem(self.step, 2) == 0)
        def _():
            self.copy().start()

        @pl.when(lax.rem(self.step, 2) == 1)
        def _():
            self.copy().wait_recv()

            def add(r):
                result[0, r, :] = self.buf[1, r, :] + self.landed[self.side, r, :]

            rows_loop(D, 64, add)
            self.copy().wait_send()


def whole(shape):
    zero = (0,) * len(shape)
    return pl.BlockSpec(shape, lambda n: zero)


def slab(shape):
    zero = (0,) * len(shape)
    return pl.BlockSpec((1,) + shape, lambda n: (n,) + zero)


def pair_slab(shape):
    zero = (0,) * len(shape)
    return pl.BlockSpec((1,) + shape, lambda n: (n // 2,) + zero)


def params(collective_id=None):
    if collective_id is None:
        return pltpu.CompilerParams(dimension_semantics=("arbitrary",), vmem_limit_bytes=VMEM_LIMIT)
    return pltpu.CompilerParams(
        dimension_semantics=("arbitrary",),
        vmem_limit_bytes=VMEM_LIMIT,
        collective_id=collective_id,
        has_side_effects=True,
    )


def out(shape, dtype):
    return jax.ShapeDtypeStruct(shape, dtype)


SMEM = pl.BlockSpec(memory_space=pltpu.SMEM)


def cost(gflop):
    return pl.CostEstimate(flops=int(gflop * 1e9), bytes_accessed=20 << 20, transcendentals=0)


GELU_A = 0.7978845608028654
GELU_B = 0.044715


FORWARD_VMEM = 58 << 20
ORDER_ATT = (1, 0, 3, 2)
ORDER_FEED = (1, 0, 2, 3)


def pick(order, k):
    index = order[3]
    for i in (2, 1, 0):
        index = jnp.where(k == i, order[i], index)
    return index


def forward_kernel(
    wide, ps_s, vl_s, hid, enc, cot, tab, hot, ps, pc, pf, gains,
    xf, gs, gc, gf, gff, ef, q1, kv1, at1, p1, q2, kv2, at2, p2, h1, out_o, d2_o, gg_o,
    wbuf, stage, xv, ev, tabs, off, nf, mask, tb, s, h2, nc, nct, cv, ct, gu, da, act, dgu, acc, buf, landed,
    ls, ins, inr, ws, vs, zs, zr, ys, yr, xs, xr, cs, cr, fsend, frecv, fout,
):
    step = pl.program_id(0)
    d, w, n, pn, yn, dn = place_here()
    y = n // 2
    blks = (n, dn)
    rl = ps.shape[0]
    groups = ((ps, gs, 0, 768, True), (pc, gc, 0, 768, True), (pf, gf, 0, 1024, True), (pf, gf, 1024, 512, False))
    keep, give = (1, 3), (0, 2)
    diag, pair, line_x, line_y = (d, w, dn), (d, w, pn), (1 - d, w, n), (d, w, yn)

    def cols(g, which):
        start, width, split = groups[g][2:]
        if which == 2 or not split:
            return pl.ds(start, width)
        half = width // 2
        pos = d if which == 0 else 1 - d
        return pl.ds(pl.multiple_of(start + pos * half, 128), half)

    def own(g, which):
        return groups[g][0].at[:, cols(g, which)]

    def spot(g, slot, row, which):
        return groups[g][1].at[slot, row, :, cols(g, which)]

    def zcopy(g, k):
        dev = (d, lax.rem(w + k, wide), n)
        if g == 4:
            ref = spot(3, 3, w, 0)
            return remote(ref, ref, zs.at[4, k], zr.at[4, w], dev)
        return remote(own(g, 0), spot(g, 1, w, 0), zs.at[g, k], zr.at[g, w], dev)

    def zgot(g, row):
        ref = spot(3, 3, row, 0) if g == 4 else spot(g, 1, row, 0)
        return remote(ref, ref, zs.at[g, 0], zr.at[g, row], line_x)

    def ycopy(g, row, src=None):
        ref = spot(g, 1, row, 0)
        return remote(ref if src is None else src, spot(g, 3, row, 0), ys.at[g, row], yr.at[g, row], line_y)

    def ygot(g, row):
        return remote(spot(g, 3, row, 0), spot(g, 3, row, 0), ys.at[g, row], yr.at[g, row], line_y)

    def xcopy(g, side, row):
        ref = spot(g, keep[side], row, 0)
        return remote(ref, ref, xs.at[g, side, row], xr.at[g, side, row], line_x)

    def xgot(g, side, row):
        ref = spot(g, keep[side], row, 1)
        return remote(ref, ref, xs.at[g, side, row], xr.at[g, side, row], line_x)

    def ccopy(g, side, row, src=None):
        ref = spot(g, keep[side], row, 2)
        return remote(
            ref if src is None else src, spot(g, give[side], row, 2), cs.at[g, side, row], cr.at[g, side, row], pair
        )

    def cgot(g, side, row):
        ref = spot(g, give[side], row, 2)
        return remote(ref, ref, cs.at[g, side, row], cr.at[g, side, row], pair)

    def around(first, body):
        loop(first, wide, lambda k: body(lax.rem(w + k, wide)))

    def zsend(g):
        loop(1, wide, lambda k: zcopy(g, k).start())

    def own_sends(g):
        ycopy(g, w, own(g, 0)).start()
        ccopy(g, 0, w, own(g, 2)).start()

    def zpass(g, then):
        def one(row):
            zgot(g, row).wait_recv()
            for nxt in then:
                nxt(row).start()

        around(1, one)

    def ypass(g):
        def one(row):
            ygot(g, row).wait_recv()
            xcopy(g, 1, row).start()

        around(0, one)

    def xsend(g):
        around(1, lambda row: xcopy(g, 0, row).start())

    def xstep(g, side):
        def one(k):
            row = lax.rem(w + k, wide)
            xgot(g, side, row).wait_recv()
            ccopy(g, side, row).start()

        loop(1 - side, wide, one)

    def cwait(g, side):
        loop(0, wide, lambda k: cgot(g, side, lax.rem(w + k, wide)).wait_recv())

    straight = rl % 16 == 0
    many = 16 // math.gcd(rl, 16)

    def slab_copies(ref, slot, b):
        width = ref.shape[-1]
        if straight:
            return [
                pltpu.make_async_copy(
                    ref.at[slot, k], wbuf.at[b, pl.ds(k * rl, rl), pl.ds(0, width)], ws.at[b, k]
                )
                for k in range(wide)
            ]
        return [pltpu.make_async_copy(ref.at[slot], stage.at[:, :, pl.ds(0, width)], ws.at[b, 0])]

    def fetch(ref, slot, b):
        for copy in slab_copies(ref, slot, b):
            copy.start()

    def fetched(ref, slot, b):
        for copy in slab_copies(ref, slot, b):
            copy.wait()
        if not straight:
            width = ref.shape[-1]
            for k in range(0, wide, many):
                part = jnp.concatenate([stage[k + i, :, 0:width].astype(f32) for i in range(many)], axis=0)
                wbuf[b, k * rl : (k + many) * rl, 0:width] = part.astype(bf16)

    local = [
        pltpu.make_async_copy(src, dst, ls.at[i])
        for i, (src, dst) in enumerate(
            (
                (ps, gs.at[1, w]),
                (pc, gc.at[1, w]),
                (pf, gf.at[1, w]),
                (hid.at[y], xv.at[n]),
                (enc.at[y], ev.at[n]),
                (cot.at[y], cv.at[0]),
            )
        )
    ]
    back = [pltpu.make_async_copy(xv, xf, vs.at[0]), pltpu.make_async_copy(ev, ef, vs.at[1])]
    early = [
        remote(tab, tabs.at[0], ins.at[3], inr.at[3], pair),
        remote(tab, tabs.at[3], ins.at[4], inr.at[4], line_y),
        remote(tab, tabs.at[2], ins.at[5], inr.at[5], diag),
        remote(hid.at[1 - y], xv.at[n], ins.at[0], inr.at[0], diag),
        remote(hid.at[y], xv.at[n], ins.at[6], inr.at[6], pair),
    ]
    middle = [
        remote(enc.at[1 - y], ev.at[n], ins.at[1], inr.at[1], diag),
        remote(enc.at[y], ev.at[n], ins.at[7], inr.at[7], pair),
        remote(cot.at[1 - y], cv.at[1], ins.at[2], inr.at[2], diag),
    ]
    later = [
        remote(xv.at[dn], xv.at[dn], ins.at[8], inr.at[8], pair),
        remote(ev.at[dn], ev.at[dn], ins.at[9], inr.at[9], pair),
    ]

    def arrived(i, ref):
        remote(ref, ref, ins.at[i], inr.at[i], pair).wait_recv()

    @pl.when(step == 0)
    def _():
        for copy in local:
            copy.start()
        greet((pair, line_y, diag, line_x), wide)
        for copy in early:
            copy.start()
        zsend(0)
        own_sends(0)
        tabs[1] = tab[...]
        start, length = ps_s[y, 0], vl_s[y, 0]
        for i in range(2):

            def mask_rows(r, i=i):
                shape = (32, LEN)
                qi = blks[i] * 256 + r.start + lax.broadcasted_iota(jnp.int32, shape, 0)
                kj = lax.broadcasted_iota(jnp.int32, shape, 1)
                inside = (qi >= start) & (qi < start + PIC) & (kj >= start) & (kj < start + PIC)
                allowed = ((kj <= qi) | inside) & (kj < length)
                mask[pl.ds(i * 256 + r.start, 32), :] = jnp.where(allowed, 0.0, masked_value)

            rows_loop(256, 32, mask_rows, unroll=2)
        arrived(6, xv.at[pn])
        arrived(0, xv.at[dn])
        later[0].start()
        zpass(0, (lambda row: ycopy(0, row), lambda row: xcopy(0, 0, row)))
        zsend(1)
        arrived(8, xv.at[yn])
        local[3].wait()
        back[0].start()
        arrived(3, tabs.at[0])
        arrived(4, tabs.at[3])
        arrived(5, tabs.at[2])
        for i in range(4):

            def norm_rows(r, i=i):
                nf[pl.ds(i * 256 + r.start, 64), :] = normed(xv[i, r, :].astype(f32), gains[0:1, :]).astype(bf16)

            rows_loop(256, 64, norm_rows, unroll=4)
        for i in range(2):
            h1[i * 256 : (i + 1) * 256, :] = xv[blks[i]].astype(f32)
        xstep(0, 0)
        ypass(0)
        own_sends(1)
        middle[0].start()
        middle[1].start()
        for i in range(3):
            local[i].wait()
        fetch(gs, 1, 0)

    @pl.when(step < 4)
    def _():
        b = lax.rem(step, 2)
        slot = pick(ORDER_ATT, step)
        fetched(gs, slot, b)
        off[...] = lax.dot_general(
            tabs[slot, 0:8, 0:BUCKETS], hot[...], (((1,), (0,)), ((), ())), precision=precise, preferred_element_type=f32
        )
        kv1[0] = nn(nf[...], wbuf[b, :, 384:768]).astype(bf16).T
        for i in range(2):
            q1[0, i * 256 : (i + 1) * 256, :] = nn(nf[block_rows(blks[i]), :], wbuf[b, :, 0:192]).astype(bf16)
        for h in range(3):
            for t in range(TILES):
                line = jnp.broadcast_to(off[h : h + 1, 128 * t : 128 * t + 256], (128, 256))
                tb[t] = pltpu.roll(line, 129, 1, stride=1, stride_axis=0)[:, :128]
            hs = slice(h * DHEAD, (h + 1) * DHEAD)
            vs_ = slice(HD + h * DHEAD, HD + (h + 1) * DHEAD)
            for i in range(2):
                s[...] = nn(q1[0, i * 256 : (i + 1) * 256, hs], kv1[0, hs, :])
                for r in range(2):
                    idx = [jnp.minimum(kb - 2 * blks[i] - r, 3) + 7 for kb in range(8)]

                    def soft_rows(rr, i=i, r=r, h=h, idx=idx):
                        bias = jnp.concatenate([tb[idx[kb], rr, :] for kb in range(8)], axis=1)
                        v = s[pl.ds(r * 128 + rr.start, ROWS), :] + bias
                        v = v + mask[pl.ds(i * 256 + r * 128 + rr.start, ROWS), :]
                        p1[0, h, pl.ds(i * 256 + r * 128 + rr.start, ROWS), :] = softmax_rows(v).astype(bf16)

                    rows_loop(128, ROWS, soft_rows, unroll=8)
                at1[0, i * 256 : (i + 1) * 256, hs] = nt(
                    p1[0, h, i * 256 : (i + 1) * 256, :], kv1[0, vs_, :]
                ).astype(bf16)
        h1[...] += nt(at1[0], wbuf[b, :, 192:384])

    @pl.when(step == 0)
    def _():
        cwait(0, 0)
        fetch(gs, 0, 1)
        zpass(1, (lambda row: ycopy(1, row),))
        zsend(2)
        own_sends(2)
        own_sends(3)

    @pl.when(step == 1)
    def _():
        xstep(0, 1)
        fetch(gs, 3, 0)
        xsend(1)
        middle[2].start()

    @pl.when(step == 2)
    def _():
        cwait(0, 1)
        fetch(gs, 2, 1)
        ypass(1)
        zpass(2, (lambda row: ycopy(2, row),))
        zsend(3)
        ygot(3, w).wait_recv()
        ccopy(3, 1, w).start()
        zsend(4)

    @pl.when(step == 3)
    def _():
        xstep(1, 0)
        fetch(gc, 1, 0)
        xsend(2)
        arrived(1, ev.at[dn])
        later[1].start()
        arrived(7, ev.at[pn])
        arrived(9, ev.at[yn])
        local[4].wait()
        back[1].start()

        def norm_rows(r):
            x = h1[r, :]
            nc[r, :] = normed(x, gains[1:2, :]).astype(bf16)
            h2[r, :] = x

        rows_loop(512, 64, norm_rows, unroll=4)

    @pl.when((step >= 4) & (step < 8))
    def _():
        b = lax.rem(step, 2)
        fetched(gc, pick(ORDER_ATT, step - 4), b)
        kv2[0] = nn(ev[...].reshape(ENC, D), wbuf[b, :, 384:768]).astype(bf16).T
        q2[0] = nn(nc[...], wbuf[b, :, 0:192]).astype(bf16)
        for h in range(3):
            hs = slice(h * DHEAD, (h + 1) * DHEAD)
            vs_ = slice(HD + h * DHEAD, HD + (h + 1) * DHEAD)
            gu[:, 0:ENC] = nn(q2[0, :, hs], kv2[0, hs, :])

            def soft_rows(r, h=h):
                p2[0, h, r, :] = softmax_rows(gu[r, 0:ENC]).astype(bf16)

            rows_loop(512, 16, soft_rows, unroll=32)
            at2[0, :, hs] = nt(p2[0, h], kv2[0, vs_, :]).astype(bf16)
        h2[...] += nt(at2[0], wbuf[b, :, 192:384])

    @pl.when(step == 4)
    def _():
        cwait(1, 0)
        fetch(gc, 0, 1)

    @pl.when(step == 5)
    def _():
        xstep(1, 1)
        fetch(gc, 3, 0)
        ypass(2)

    @pl.when(step == 6)
    def _():
        cwait(1, 1)
        fetch(gc, 2, 1)

    @pl.when(step == 7)
    def _():
        xstep(2, 0)
        zpass(3, (lambda row: ccopy(3, 0, row),))
        fetch(gf, 1, 0)
        arrived(2, cv.at[1])
        local[5].wait()

        def norm_rows(r):
            x = h2[r, :]
            nc[r, :] = normed(x, gains[2:3, :]).astype(bf16)
            acc[r, :] = x
            d2_o[r, :] = jnp.zeros((64, D), f32)

        rows_loop(512, 64, norm_rows, unroll=4)
        nct[...] = nc[...].T
        ct[...] = cv[...].reshape(512, D).T

    def give_copy(side):
        return remote(buf.at[0], landed.at[side], fsend.at[side], frecv.at[side], pair)

    def put_out(side):
        return pltpu.make_async_copy(buf.at[1], gff.at[side], fout.at[side])

    def add_side(side):
        give_copy(side).wait_recv()

        def add(r):
            buf[1, r, :] = buf[1, r, :] + landed[side, r, :]

        rows_loop(D, 64, add)
        put_out(side).start()

    @pl.when(step >= 8)
    def _():
        b = lax.rem(step, 2)
        fetched(gf, pick(ORDER_FEED, step - 8), b)
        gu[...] = nn(nc[...], wbuf[b, :, : 2 * FFB])
        da[...] = nn(cv[...].reshape(512, D), wbuf[b, :, 2 * FFB :])

        def gelu_rows(r):
            gate = gu[r, :FFB]
            up = gu[r, FFB:]
            d_act = da[r, :]
            sq = gate * gate
            th = jnp.tanh(GELU_A * gate * (1.0 + GELU_B * sq))
            half = 0.5 + 0.5 * th
            gelu = gate * half
            slope = half + 0.5 * GELU_A * gate * (1.0 - th * th) * (1.0 + 3.0 * GELU_B * sq)
            act[r, :] = (gelu * up).astype(bf16)
            dgu[r, :FFB] = (d_act * up * slope).astype(bf16)
            dgu[r, FFB:] = (d_act * gelu).astype(bf16)

        rows_loop(512, 16, gelu_rows, unroll=32)
        acc[...] += nt(act[...], wbuf[b, :, 2 * FFB :])
        d2_o[...] += nt(dgu[...], wbuf[b, :, : 2 * FFB])

        @pl.when(step == 10)
        def _():
            give_copy(0).wait_send()

        @pl.when(step == 11)
        def _():
            put_out(0).wait()

        place = jnp.where((step == 8) | (step == 11), 1, 0)
        buf[place, :, : 2 * FFB] = nn(nct[...], dgu[...]).astype(bf16)
        buf[place, :, 2 * FFB :] = nn(ct[...], act[...]).astype(bf16)

    @pl.when(step == 8)
    def _():
        cwait(2, 0)
        cwait(3, 0)
        fetch(gf, 0, 1)

    @pl.when(step == 9)
    def _():
        give_copy(0).start()
        zpass(4, (lambda row: ccopy(3, 1, row),))
        xstep(2, 1)
        fetch(gf, 3, 1)
        cwait(2, 1)
        cwait(3, 1)
        fetch(gf, 2, 0)

    @pl.when(step == 10)
    def _():
        give_copy(1).start()
        add_side(0)

    @pl.when(step == 11)
    def _():
        add_side(1)
        gg_o[...] = jnp.zeros((1, D), f32)

        for i in range(2):

            def back_rows(r, i=i):
                rows = pl.ds(i * 256 + r.start, 64)
                dx, gg = norm_back(h2[rows, :], gains[2:3, :], d2_o[rows, :])
                d2_o[rows, :] = cv[i, r, :].astype(f32) + dx
                gg_o[...] += gg
                out_o[rows, :] = acc[rows, :].astype(bf16)

            rows_loop(256, 64, back_rows, unroll=2)
        for copy in back:
            copy.wait()
        put_out(1).wait()
        give_copy(1).wait_send()
        for copy in early + middle + later:
            copy.wait_send()

        def finish(row):
            for g in range(4):
                for side in range(2):
                    ccopy(g, side, row).wait_send()
            for g in range(3):
                ycopy(g, row).wait_send()
                xcopy(g, 1, row).wait_send()

        around(0, finish)
        ycopy(3, w).wait_send()

        def finish_line(k):
            row = lax.rem(w + k, wide)
            for g in range(5):
                zcopy(g, k).wait_send()
            for g in range(3):
                xcopy(g, 0, row).wait_send()

        loop(1, wide, finish_line)


def forward(wide, ps_s, vl_s, hid, enc, cot, tab, hot, ps, pc, pf, gains):
    rl = ps.shape[0]
    sem = pltpu.SemaphoreType.DMA
    V = pl.BlockSpec(memory_space=pltpu.VMEM)

    def turn(first, shape):
        zero = (0,) * len(shape)
        return pl.BlockSpec(
            (1,) + shape, lambda n: (pick(ORDER_ATT, jnp.clip(n - first, 0, 3)),) + zero
        )

    v = lambda *shape: pltpu.VMEM(shape, bf16)
    vf = lambda *shape: pltpu.VMEM(shape, f32)
    return pl.pallas_call(
        partial(forward_kernel, wide),
        grid=(12,),
        in_specs=[SMEM, SMEM, ANY, ANY, ANY, V, V, V, V, V, V],
        out_specs=[ANY] * 6
        + [turn(0, (512, HD)), turn(0, (2 * HD, LEN)), turn(0, (512, HD)), turn(0, (3, 512, LEN))]
        + [turn(4, (512, HD)), turn(4, (2 * HD, ENC)), turn(4, (512, HD)), turn(4, (3, 512, ENC))]
        + [V, V, V, V],
        out_shape=[
            out((4, 256, D), bf16),
            out((4, wide, rl, D), bf16),
            out((4, wide, rl, D), bf16),
            out((4, wide, rl, 2 * D), bf16),
            out((2, D, 3 * FFB), bf16),
            out((4, 128, D), bf16),
            out((4, 512, HD), bf16),
            out((4, 2 * HD, LEN), bf16),
            out((4, 512, HD), bf16),
            out((4, 3, 512, LEN), bf16),
            out((4, 512, HD), bf16),
            out((4, 2 * HD, ENC), bf16),
            out((4, 512, HD), bf16),
            out((4, 3, 512, ENC), bf16),
            out((512, D), f32),
            out((512, D), bf16),
            out((512, D), f32),
            out((1, D), f32),
        ],
        scratch_shapes=[
            v(2, D, 3 * FFB),
            v(wide, rl, 3 * FFB) if rl % 16 else v(16, 128),
            v(4, 256, D),
            v(4, 128, D),
            vf(4, 32, 128),
            vf(8, 2048),
            v(LEN, D),
            vf(512, LEN),
            vf(TILES, 128, 128),
            vf(256, LEN),
            vf(512, D),
            v(512, D),
            v(D, 512),
            v(2, 256, D),
            v(D, 512),
            vf(512, 2 * FFB),
            vf(512, FFB),
            v(512, FFB),
            v(512, 2 * FFB),
            vf(512, D),
            v(2, D, 3 * FFB),
            v(2, D, 3 * FFB),
            sem((6,)),
            sem((10,)),
            sem((10,)),
            sem((2, wide)),
            sem((2,)),
            sem((5, wide)),
            sem((5, wide)),
            sem((4, wide)),
            sem((4, wide)),
            sem((4, 2, wide)),
            sem((4, 2, wide)),
            sem((4, 2, wide)),
            sem((4, 2, wide)),
            sem((2,)),
            sem((2,)),
            sem((2,)),
        ],
        compiler_params=pltpu.CompilerParams(
            dimension_semantics=("arbitrary",), vmem_limit_bytes=FORWARD_VMEM, collective_id=0, has_side_effects=True
        ),
        cost_estimate=cost(60),
        name="forward",
    )(ps_s, vl_s, hid, enc, cot, tab, hot, ps, pc, pf, gains)


def cross_backward_kernel(
    wide, h1, ef, d2, w, gain, q, kv, at, p, gff,
    gw_o, d1_o, gg_o, ge_o, gep_o, o1, o2, o3,
    d2b, d2t, nct, eft, get, do, dp, ds, dq, dkv, buf, landed, rx, ry, rz, send, recv, load, fs, fr, zs, zr,
):
    n = pl.program_id(0)
    slot = lax.rem(n, 2)
    core = CoreSum(n, buf, landed, send, recv)
    d, wi, me, pn, yn, dn = place_here()
    y = me // 2
    mine = pl.ds(pl.multiple_of(d * 256, 128), 256)
    other = pl.ds(pl.multiple_of(256 - d * 256, 128), 256)
    late = pl.ds(512, 640)
    third = pl.ds(1152, 384)
    loads = [
        pltpu.make_async_copy(gff.at[:, :, :, mine], o1, load.at[0]),
        pltpu.make_async_copy(gff.at[0, :, :, late], o2, load.at[1]),
        pltpu.make_async_copy(gff.at[:, wi, :, third], o3, load.at[2]),
    ]

    def zcopy(k):
        row = lax.rem(wi + k, wide)
        return remote(gff.at[:, row, :, third], rz.at[wi], zs.at[k], zr.at[wi], (d, row, me))

    def zgot(k):
        row = lax.rem(wi + k, wide)
        return remote(rz.at[row], rz.at[row], zs.at[k], zr.at[row], (d, row, me))

    sends = [
        remote(gff.at[:, :, :, other], rx, fs.at[0], fr.at[0], (1 - d, wi, me)),
        remote(gff.at[1, :, :, late], ry, fs.at[1], fr.at[1], (d, wi, yn)),
    ]

    @pl.when(n == 0)
    def _():
        def norm_rows(r):
            d2b[r, :] = d2[r, :].astype(bf16)
            d1_o[r, :] = jnp.zeros((64, D), f32)
            dp[r, :] = normed(h1[r, :], gain[1:2, :])

        for copy in loads:
            copy.start()
        greet(((d, wi, pn), (d, wi, yn), (1 - d, wi, me)), wide)
        for copy in sends:
            copy.start()
        loop(1, wide, lambda k: zcopy(k).start())
        rows_loop(512, 64, norm_rows, unroll=4)
        nct[...] = dp[...].astype(bf16).T
        d2t[...] = d2b[...].T
        eft[...] = ef[...].T
        get[...] = jnp.zeros((D, ENC), f32)

    do[...] = nn(d2b[...], w[0, :, 192:384]).astype(bf16)
    for h in range(3):
        hs = slice(h * DHEAD, (h + 1) * DHEAD)
        vs = slice(HD + h * DHEAD, HD + (h + 1) * DHEAD)
        dp[:, :ENC] = nn(do[:, hs], kv[0, vs, :])

        def grad_rows(r, h=h, hs=hs):
            delta = jnp.sum(do[r, hs].astype(f32) * at[0, r, hs].astype(f32), axis=1, keepdims=True)
            ds[r, :] = (p[0, h, r, :].astype(f32) * (dp[r, :ENC] - delta)).astype(bf16)

        rows_loop(512, 16, grad_rows, unroll=32)
        dq[:, hs] = nt(ds[...], kv[0, hs, :]).astype(bf16)
        dkv[hs, :] = tn(q[0, :, hs], ds[...]).astype(bf16)
        dkv[vs, :] = tn(do[:, hs], p[0, h]).astype(bf16)
    d1_o[...] += nt(dq[...], w[0, :, 0:192])
    get[...] += nn(w[0, :, 384:768], dkv[...])
    buf[slot, :, 0:384] = jnp.concatenate([nn(nct[...], dq[...]), nn(d2t[...], at[0])], axis=1).astype(bf16)
    buf[slot, :, 384:768] = nt(eft[...], dkv[...]).astype(bf16)
    core.finish(gw_o)

    @pl.when(n == 3)
    def _():
        gg_o[...] = jnp.zeros((1, D), f32)

        def back_rows(r):
            dx, gg = norm_back(h1[r, :], gain[1:2, :], d1_o[r, :])
            d1_o[r, :] = d2[r, :] + dx
            gg_o[...] += gg

        rows_loop(512, 64, back_rows, unroll=2)
        for i in range(2):
            half = slice(i * 128, (i + 1) * 128)
            cols = lambda blk: pl.ds(pl.multiple_of(blk * 128, 128), 128)
            ge_o[half, :] = get[:, cols((me, 3 - me)[i])].T
            gep_o[half, :] = get[:, cols((pn, 3 - pn)[i])].T.astype(bf16)
        for copy in loads:
            copy.wait()
        for copy in sends:
            copy.wait()
        add_into(o1, rx)
        add_into(o2, ry)
        loop(1, wide, lambda k: zgot(k).wait_recv())
        rl = o3.shape[1]
        part = 64 if rl % 64 == 0 else rl
        for i in range(2):
            for j in range(rl // part):
                r = slice(j * part, (j + 1) * part)

                def add(k, total, i=i, r=r):
                    return total + rz[lax.rem(wi + k, wide), i, r, :].astype(f32)

                o3[i, r, :] = lax.fori_loop(1, wide, add, o3[i, r, :].astype(f32)).astype(bf16)
        loop(1, wide, lambda k: zcopy(k).wait_send())


def cross_backward(wide, h1, ef, d2, w, gain, q, kv, at, p, gff):
    rl = D // wide
    return pl.pallas_call(
        partial(cross_backward_kernel, wide),
        grid=(4,),
        in_specs=[
            whole((512, D)),
            whole((ENC, D)),
            whole((512, D)),
            slab((D, D)),
            whole((3, D)),
            slab((512, HD)),
            slab((2 * HD, ENC)),
            slab((512, HD)),
            slab((3, 512, ENC)),
            ANY,
        ],
        out_specs=[
            pair_slab((D, D)),
            whole((512, D)),
            whole((1, D)),
            whole((256, D)),
            whole((256, D)),
            whole((2, wide, rl, 256)),
            whole((wide, rl, 640)),
            whole((2, rl, 384)),
        ],
        out_shape=[
            out((2, D, D), bf16),
            out((512, D), f32),
            out((1, D), f32),
            out((256, D), f32),
            out((256, D), bf16),
            out((2, wide, rl, 256), bf16),
            out((wide, rl, 640), bf16),
            out((2, rl, 384), bf16),
        ],
        scratch_shapes=[
            pltpu.VMEM((512, D), bf16),
            pltpu.VMEM((D, 512), bf16),
            pltpu.VMEM((D, 512), bf16),
            pltpu.VMEM((D, ENC), bf16),
            pltpu.VMEM((D, ENC), f32),
            pltpu.VMEM((512, HD), bf16),
            pltpu.VMEM((512, D), f32),
            pltpu.VMEM((512, ENC), bf16),
            pltpu.VMEM((512, HD), bf16),
            pltpu.VMEM((2 * HD, ENC), bf16),
            pltpu.VMEM((2, D, D), bf16),
            pltpu.VMEM((2, D, D), bf16),
            pltpu.VMEM((2, wide, rl, 256), bf16),
            pltpu.VMEM((wide, rl, 640), bf16),
            pltpu.VMEM((wide, 2, rl, 384), bf16),
            pltpu.SemaphoreType.DMA((1,)),
            pltpu.SemaphoreType.DMA((2,)),
            pltpu.SemaphoreType.DMA((3,)),
            pltpu.SemaphoreType.DMA((2,)),
            pltpu.SemaphoreType.DMA((2,)),
            pltpu.SemaphoreType.DMA((wide,)),
            pltpu.SemaphoreType.DMA((wide,)),
        ],
        compiler_params=params(3),
        cost_estimate=cost(14),
        name="cross_backward",
    )(h1, ef, d2, w, gain, q, kv, at, p, gff.reshape(2, wide, rl, 3 * FFB))


def self_backward_kernel(
    wide, xf, d1, w, gain, q, kv, at, p, gcr, o1, o2, o3, outp,
    gw_o, g_o, gp_o, dl_o, b1, c2, e1, e2, out_o,
    c1, cy1, d1b, d1t, nft, nqt, gt, gq, do, dp, ds, dq, dkv, buf, landed, s1, f2, s3, rx, ry, ry1, ry3, rz1, rz2,
    send, recv, load, fs, fr, zs, zr,
):
    n = pl.program_id(0)
    blks = own_blocks()
    slot = lax.rem(n, 2)
    core = CoreSum(n, buf, landed, send, recv)
    d, wi, me, pn, yn, dn = place_here()
    y = me // 2
    mine = pl.ds(pl.multiple_of(d * 256, 128), 256)
    other = pl.ds(pl.multiple_of(256 - d * 256, 128), 256)
    late = pl.ds(512, 256)
    loads = [
        pltpu.make_async_copy(gcr.at[:, :, :, mine], c1, load.at[0]),
        pltpu.make_async_copy(gcr.at[0, :, :, late], c2, load.at[1]),
        pltpu.make_async_copy(o1.at[0], s1, load.at[2]),
        pltpu.make_async_copy(o2.at[wi], f2, load.at[3]),
        pltpu.make_async_copy(outp.at[0], out_o.at[y], load.at[4]),
        pltpu.make_async_copy(o3.at[0], s3, load.at[5]),
    ]
    sends = [
        remote(o1.at[1], ry1, fs.at[0], fr.at[0], (d, wi, yn)),
        remote(gcr.at[:, :, :, other], rx, fs.at[1], fr.at[1], (1 - d, wi, me)),
        remote(gcr.at[1, :, :, late], ry, fs.at[2], fr.at[2], (d, wi, yn)),
        remote(outp.at[1], out_o.at[y], fs.at[3], fr.at[3], (d, wi, dn)),
    ]
    out_got = remote(out_o.at[1 - y], out_o.at[1 - y], fs.at[3], fr.at[3], (d, wi, dn))
    y_cross = remote(c1.at[1], cy1, fs.at[4], fr.at[4], (d, wi, yn))
    y_third = remote(o3.at[1], ry3, fs.at[5], fr.at[5], (d, wi, yn))

    def zcopy(path, k):
        row = lax.rem(wi + k, wide)
        src, dst = ((s1, rz1), (o2, rz2))[path]
        return remote(src.at[row], dst.at[wi], zs.at[path, k], zr.at[path, wi], (d, row, me))

    def zgot(path, k):
        row = lax.rem(wi + k, wide)
        ref = (rz1, rz2)[path].at[row]
        return remote(ref, ref, zs.at[path, k], zr.at[path, row], (d, row, me))

    @pl.when(n == 0)
    def _():
        def cast_rows(r):
            d1b[r, :] = d1[r, :].astype(bf16)
            gq[r, :] = jnp.zeros((64, D), f32)

        for copy in loads:
            copy.start()
        greet(((d, wi, pn), (d, wi, yn), (1 - d, wi, me), (d, wi, dn)), wide)
        for copy in sends[:3]:
            copy.start()
        loop(1, wide, lambda k: zcopy(1, k).start())
        rows_loop(512, 64, cast_rows)
        d1t[...] = d1b[...].T
        for i in range(4):
            part = normed(xf[i * 256 : (i + 1) * 256, :].astype(f32), gain[0:1, :]).astype(bf16)
            nft[:, i * 256 : (i + 1) * 256] = part.T
        for i in range(2):
            part = normed(xf[block_rows(blks[i]), :].astype(f32), gain[0:1, :]).astype(bf16)
            nqt[:, i * 256 : (i + 1) * 256] = part.T
        gt[...] = jnp.zeros((D, LEN), f32)

    @pl.when(n == 1)
    def _():
        sends[3].start()
        y_third.start()

    @pl.when(n == 2)
    def _():
        loads[2].wait()
        sends[0].wait_recv()
        add_into(s1, ry1)
        loop(1, wide, lambda k: zcopy(0, k).start())
        loads[0].wait()
        sends[1].wait_recv()
        add_into(c1, rx)
        y_cross.start()

    dl_o[0] = jnp.zeros((3, 2048), f32)
    do[...] = nn(d1b[...], w[0, :, 192:384]).astype(bf16)
    for h in range(3):
        hs = slice(h * DHEAD, (h + 1) * DHEAD)
        vs = slice(HD + h * DHEAD, HD + (h + 1) * DHEAD)
        dk = jnp.zeros((DHEAD, LEN), f32)
        dv = jnp.zeros((DHEAD, LEN), f32)
        for i in range(2):
            half = slice(i * 256, (i + 1) * 256)
            dp[...] = nn(do[half, hs], kv[0, vs, :])

            def grad_rows(rr, i=i, h=h, hs=hs):
                rows = pl.ds(i * 256 + rr.start, ROWS)
                delta = jnp.sum(do[rows, hs].astype(f32) * at[0, rows, hs].astype(f32), axis=1, keepdims=True)
                ds[rr, :] = (p[0, h, rows, :].astype(f32) * (dp[rr, :] - delta)).astype(bf16)

            rows_loop(256, ROWS, grad_rows, unroll=16)
            upper, lower = ds[:128, :].astype(f32), ds[128:, :].astype(f32)
            part = jnp.concatenate(
                [
                    upper[:, :896] + lower[:, 128:],
                    upper[:, 896:],
                    jnp.zeros((128, 128), f32),
                    lower[:, :128],
                ],
                axis=1,
            )
            height = 128
            while height > 1:
                height //= 2
                part = part[:height] + pltpu.roll(part[height:], SPAN - height, 1)
            where = pl.ds(pl.multiple_of(768 - 256 * blks[i], 128), SPAN)
            dl_o[0, h : h + 1, where] += pltpu.roll(part, 255, 1)
            dq[half, hs] = nt(ds[...], kv[0, hs, :]).astype(bf16)
            dk = dk + tn(q[0, half, hs], ds[...])
            dv = dv + tn(do[half, hs], p[0, h, half, :])
        dkv[hs, :] = dk.astype(bf16)
        dkv[vs, :] = dv.astype(bf16)
    gq[...] += nt(dq[...], w[0, :, 0:192])
    gt[...] += nn(w[0, :, 384:768], dkv[...])
    buf[slot, :, 0:384] = jnp.concatenate([nn(nqt[...], dq[...]), nn(d1t[...], at[0])], axis=1).astype(bf16)
    buf[slot, :, 384:768] = nt(nft[...], dkv[...]).astype(bf16)
    core.finish(gw_o)

    @pl.when(n == 3)
    def _():
        for i in range(2):
            half = slice(i * 256, (i + 1) * 256)
            g_o[half, :] = gq[half, :] + gt[:, block_rows(blks[i])].T
            gp_o[half, :] = gt[:, block_rows((pn, 3 - pn)[i])].T.astype(bf16)
        loads[1].wait()
        sends[2].wait_recv()
        add_into(c2, ry)
        loads[3].wait()
        for path in (1, 0):
            loop(1, wide, lambda k, path=path: zgot(path, k).wait_recv())

        def put(ref, cols):
            def store(r, total):
                ref[r, cols] = total.astype(bf16)

            return store

        sum_line(wide, s1.at[wi], rz1, put(e1, slice(None)))
        sum_line(wide, f2, rz2, put(e2, slice(0, 640)))
        loads[5].wait()
        y_third.wait_recv()
        e2[:, 640:1024] = s3[...] + ry3[...]
        y_cross.wait_recv()

        def add_cross(k):
            b1[k] = c1[0, k] + cy1[k]

        loop(0, wide, add_cross)
        out_got.wait_recv()
        loads[4].wait()
        for copy in (*sends, y_cross, y_third):
            copy.wait_send()
        for path in (0, 1):
            loop(1, wide, lambda k, path=path: zcopy(path, k).wait_send())


def self_backward(wide, xf, d1, w, gain, q, kv, at, p, gcr, o1, o2, o3, outp):
    rl = D // wide
    return pl.pallas_call(
        partial(self_backward_kernel, wide),
        grid=(4,),
        in_specs=[
            whole((LEN, D)),
            whole((512, D)),
            slab((D, D)),
            whole((3, D)),
            slab((512, HD)),
            slab((2 * HD, LEN)),
            slab((512, HD)),
            slab((3, 512, LEN)),
            ANY,
            ANY,
            ANY,
            ANY,
            pl.BlockSpec(memory_space=pltpu.VMEM),
        ],
        out_specs=[
            pair_slab((D, D)),
            whole((512, D)),
            whole((512, D)),
            slab((3, 2048)),
            whole((wide, rl, 256)),
            whole((wide, rl, 256)),
            whole((rl, 256)),
            whole((rl, 1024)),
            ANY,
        ],
        out_shape=[
            out((2, D, D), bf16),
            out((512, D), f32),
            out((512, D), bf16),
            out((4, 3, 2048), f32),
            out((wide, rl, 256), bf16),
            out((wide, rl, 256), bf16),
            out((rl, 256), bf16),
            out((rl, 1024), bf16),
            out((2, 256, D), bf16),
        ],
        scratch_shapes=[
            pltpu.VMEM((2, wide, rl, 256), bf16),
            pltpu.VMEM((wide, rl, 256), bf16),
            pltpu.VMEM((512, D), bf16),
            pltpu.VMEM((D, 512), bf16),
            pltpu.VMEM((D, LEN), bf16),
            pltpu.VMEM((D, 512), bf16),
            pltpu.VMEM((D, LEN), f32),
            pltpu.VMEM((512, D), f32),
            pltpu.VMEM((512, HD), bf16),
            pltpu.VMEM((256, LEN), f32),
            pltpu.VMEM((256, LEN), bf16),
            pltpu.VMEM((512, HD), bf16),
            pltpu.VMEM((2 * HD, LEN), bf16),
            pltpu.VMEM((2, D, D), bf16),
            pltpu.VMEM((2, D, D), bf16),
            pltpu.VMEM((wide, rl, 256), bf16),
            pltpu.VMEM((rl, 640), bf16),
            pltpu.VMEM((rl, 384), bf16),
            pltpu.VMEM((2, wide, rl, 256), bf16),
            pltpu.VMEM((wide, rl, 256), bf16),
            pltpu.VMEM((wide, rl, 256), bf16),
            pltpu.VMEM((rl, 384), bf16),
            pltpu.VMEM((wide, rl, 256), bf16),
            pltpu.VMEM((wide, rl, 640), bf16),
            pltpu.SemaphoreType.DMA((1,)),
            pltpu.SemaphoreType.DMA((2,)),
            pltpu.SemaphoreType.DMA((6,)),
            pltpu.SemaphoreType.DMA((6,)),
            pltpu.SemaphoreType.DMA((6,)),
            pltpu.SemaphoreType.DMA((2, wide)),
            pltpu.SemaphoreType.DMA((2, wide)),
        ],
        compiler_params=params(4),
        cost_estimate=cost(25),
        name="self_backward",
    )(xf, d1, w, gain, q, kv, at, p, gcr.reshape(2, wide, rl, D), o1, o2, o3, outp)


def reduce_kernel(
    wide, se, b1, c2, e1, e2, gxo, gxp, geo, gep, xf, d1, gain, gfeed, gcross, tg,
    gin_o, gen_o, sg_o, st_o, ff_o, cr_o, se_o,
    a1, a2, rx, ry, ry1, rzs1, rzs2, rzc1, rzc2, fs, fc, xs1, xs2, xc1, xc2, x1, x2,
    rgx, rge, tmp_in, tmp_en, back_in, back_en, rows_f, sg, st, rsg, rst, rsgz, rstz,
    load, ms, mr, ts, tr, zs, zr, ss, sr, os,
):
    d, w, n, pn, yn, dn = place_here()
    y = n // 2
    pair, line_y, diag, line_x = (d, w, pn), (d, w, yn), (d, w, dn), (1 - d, w, n)
    mine = pl.ds(pl.multiple_of(d * 256, 128), 256)
    other = pl.ds(pl.multiple_of(256 - d * 256, 128), 256)
    late = pl.ds(512, 256)
    loads = [
        pltpu.make_async_copy(se.at[:, :, :, mine], a1, load.at[0]),
        pltpu.make_async_copy(se.at[0, :, :, late], a2, load.at[1]),
        pltpu.make_async_copy(geo, tmp_en, load.at[2]),
    ]
    for copy in loads:
        copy.start()
    greet((pair, line_y, diag, line_x), wide)
    turn = lambda i, src, dst, dev: remote(src, dst, ts.at[i], tr.at[i], dev)
    put = [
        turn(0, se.at[:, :, :, other], rx, line_x),
        turn(2, se.at[1, :, :, late], ry, line_y),
        turn(3, e1, x1, line_x),
        turn(4, e2, x2, line_x),
    ]
    cross = [
        remote(gxp, rgx, ms.at[0], mr.at[0], pair),
        remote(gep, rge, ms.at[1], mr.at[1], pair),
    ]
    z_refs = ((a1, rzs1), (a2, rzs2), (b1, rzc1), (c2, rzc2))

    def zcopy(path, k):
        row = lax.rem(w + k, wide)
        src, dst = z_refs[path]
        src = src.at[0, row] if path == 0 else src.at[row]
        return remote(src, dst.at[w], zs.at[path, k], zr.at[path, w], (d, row, n))

    def zgot(path, k):
        row = lax.rem(w + k, wide)
        ref = z_refs[path][1].at[row]
        return remote(ref, ref, zs.at[path, k], zr.at[path, row], (d, row, n))

    def zstart(path):
        loop(1, wide, lambda k: zcopy(path, k).start())

    def zwait(path):
        loop(1, wide, lambda k: zgot(path, k).wait_recv())

    cross[0].start()
    cross[1].start()
    put[0].start()
    put[1].start()
    zstart(3)
    zstart(2)

    sg[...] = jnp.zeros((8, D), f32)
    sg[1:2, :] = gcross[...]
    sg[2:3, :] = gfeed[...]
    st[...] = tg[...]
    cross[0].wait_recv()
    own = (n, dn)
    for i in (1, 0):

        def back(r, i=i):
            x = xf[own[i], r, :].astype(f32)
            dx, gg = norm_back(x, gain[0:1, :], gxo[i, r, :] + rgx[i, r, :].astype(f32))
            total = d1[i, r, :] + dx
            sg[0:1, :] += gg
            if i == 0:
                rows_f[0, r, :] = total
            else:
                tmp_in[r, :] = total.astype(bf16)

        rows_loop(256, 32, back, unroll=2)
        if i == 1:
            in_send = remote(tmp_in, back_in, ms.at[3], mr.at[3], diag)
            in_send.start()
    in_local = pltpu.make_async_copy(rows_f.at[0], gin_o.at[y], os.at[0])
    in_local.start()
    cross[1].wait_recv()
    loads[2].wait()
    back_en[0] = (tmp_en[1] + rge[1].astype(f32)).astype(bf16)
    en_send = remote(back_en.at[0], back_en.at[1], ms.at[4], mr.at[4], diag)
    en_send.start()
    tmp_en[0] = tmp_en[0] + rge[0].astype(f32)
    en_local = pltpu.make_async_copy(tmp_en.at[0], gen_o.at[y], os.at[1])
    en_local.start()

    def small(j, dev):
        return (
            remote(sg, rsg.at[j], ss.at[0, j], sr.at[0, j], dev),
            remote(st, rst.at[j], ss.at[1, j], sr.at[1, j], dev),
        )

    def small_add(j, dev):
        for copy in small(j, dev):
            copy.wait()
        sg[...] += rsg[j]
        st[...] += rst[j]

    def small_line(k):
        dev = (d, lax.rem(w + k, wide), n)
        return (
            remote(sg, rsgz.at[w], ss.at[0, 3 + k], sr.at[0, 3 + w], dev),
            remote(st, rstz.at[w], ss.at[1, 3 + k], sr.at[1, 3 + w], dev),
        )

    def start_all(copies):
        for copy in copies:
            copy.start()

    start_all(small(0, pair))
    small_add(0, pair)
    start_all(small(1, line_y))
    loads[1].wait()
    put[1].wait_recv()
    add_into(a2, ry)
    zstart(1)
    loads[0].wait()
    put[0].wait_recv()
    add_into(a1, rx)
    y1 = turn(5, a1.at[1], ry1, line_y)
    y1.start()
    put[2].start()
    put[3].start()
    small_add(1, line_y)
    start_all(small(2, line_x))
    small_add(2, line_x)
    loop(1, wide, lambda k: start_all(small_line(k)))
    rsgz[w] = sg[...]
    rstz[w] = st[...]

    def keep(ref, cols):
        def store(r, total):
            ref[r, cols] = total.astype(bf16)

        return store

    everything = slice(None)
    zwait(3)
    sum_line(wide, c2.at[w], rzc2, keep(fc, late))
    f_c2 = turn(6, fc.at[:, late], xc2, line_x)
    f_c2.start()
    zwait(2)
    sum_line(wide, b1.at[w], rzc1, keep(fc, mine))
    f_c1 = turn(7, fc.at[:, mine], xc1, line_x)
    f_c1.start()
    y1.wait_recv()
    rl = e1.shape[0]

    def add_side(k):
        a1[0, k] = a1[0, k] + ry1[k]

    loop(0, wide, add_side)
    zstart(0)

    def small_wait(k):
        row = lax.rem(w + k, wide)
        for i, ref in enumerate((rsgz, rstz)):
            remote(ref.at[row], ref.at[row], ss.at[i, 3], sr.at[i, 3 + row], line_x).wait_recv()

    loop(1, wide, small_wait)
    sg_o[...] = lax.fori_loop(1, wide, lambda k, t: t + rsgz[k], rsgz[0])
    st_o[...] = lax.fori_loop(1, wide, lambda k, t: t + rstz[k], rstz[0])

    zwait(1)
    sum_line(wide, a2.at[w], rzs2, keep(fs, late))
    f_s2 = turn(8, fs.at[:, late], xs2, line_x)
    f_s2.start()

    in_send.wait_recv()

    def widen(r):
        rows_f[1, r, :] = back_in[r, :].astype(f32)

    rows_loop(256, 64, widen)
    in_last = pltpu.make_async_copy(rows_f.at[1], gin_o.at[1 - y], os.at[2])
    in_last.start()
    en_send.wait_recv()
    tmp_en[1] = back_en[1].astype(f32)
    en_last = pltpu.make_async_copy(tmp_en.at[1], gen_o.at[1 - y], os.at[3])
    en_last.start()

    put[2].wait_recv()
    put[3].wait_recv()
    ff_o[:, mine] = e1[...].astype(f32)
    ff_o[:, other] = x1[...].astype(f32)
    ff_o[:, pl.ds(512, 1024)] = e2[...].astype(f32) + x2[...].astype(f32)
    f_c1.wait_recv()
    f_c2.wait_recv()
    cr_o[:, mine] = fc[:, mine].astype(f32)
    cr_o[:, other] = xc1[...].astype(f32)
    cr_o[:, late] = fc[:, late].astype(f32) + xc2[...].astype(f32)
    zwait(0)
    sum_line(wide, a1.at[0, w], rzs1, keep(fs, mine))
    f_s1 = turn(9, fs.at[:, mine], xs1, line_x)
    f_s1.start()
    f_s2.wait_recv()
    se_o[:, mine] = fs[:, mine].astype(f32)
    se_o[:, late] = fs[:, late].astype(f32) + xs2[...].astype(f32)
    f_s1.wait_recv()
    se_o[:, other] = xs1[...].astype(f32)

    for copy in (in_local, en_local, in_last, en_last):
        copy.wait()
    for copy in (*cross, in_send, en_send, *put, y1, f_c1, f_c2, f_s1, f_s2):
        copy.wait_send()

    def finish(k):
        for path in range(4):
            zcopy(path, k).wait_send()
        for copy in small_line(k):
            copy.wait_send()

    loop(1, wide, finish)


def reduce_all(wide, se, b1, c2, e1, e2, gxo, gxp, geo, gep, xf, d1, gain, gfeed, gcross, tg):
    rl = D // wide
    se = se.reshape(2, wide, rl, D)
    sem = pltpu.SemaphoreType.DMA
    V = pl.BlockSpec(memory_space=pltpu.VMEM)
    v = lambda *shape: pltpu.VMEM(shape, bf16)
    return pl.pallas_call(
        partial(reduce_kernel, wide),
        in_specs=[ANY, V, V, V, V, V, ANY, ANY, ANY, V, V, V, V, V, V],
        out_specs=[ANY, ANY, V, V, V, V, V],
        out_shape=[
            out((2, 256, D), f32),
            out((2, 128, D), f32),
            out((8, D), f32),
            out((32, 128), f32),
            out((rl, 2 * D), f32),
            out((rl, D), f32),
            out((rl, D), f32),
        ],
        scratch_shapes=[
            v(2, wide, rl, 256),
            v(wide, rl, 256),
            v(2, wide, rl, 256),
            v(wide, rl, 256),
            v(wide, rl, 256),
            v(wide, rl, 256),
            v(wide, rl, 256),
            v(wide, rl, 256),
            v(wide, rl, 256),
            v(rl, D),
            v(rl, D),
            v(rl, 256),
            v(rl, 256),
            v(rl, 256),
            v(rl, 256),
            v(rl, 256),
            v(rl, 1024),
            v(2, 256, D),
            v(2, 128, D),
            v(256, D),
            pltpu.VMEM((2, 128, D), f32),
            v(256, D),
            v(2, 128, D),
            pltpu.VMEM((2, 256, D), f32),
            pltpu.VMEM((8, D), f32),
            pltpu.VMEM((32, 128), f32),
            pltpu.VMEM((3, 8, D), f32),
            pltpu.VMEM((3, 32, 128), f32),
            pltpu.VMEM((wide, 8, D), f32),
            pltpu.VMEM((wide, 32, 128), f32),
            sem((5,)),
            sem((5,)),
            sem((5,)),
            sem((10,)),
            sem((10,)),
            sem((4, wide)),
            sem((4, wide)),
            sem((2, 3 + wide)),
            sem((2, 3 + wide)),
            sem((4,)),
        ],
        compiler_params=pltpu.CompilerParams(
            collective_id=1, has_side_effects=True, vmem_limit_bytes=VMEM_LIMIT
        ),
        name="reduce_all",
    )(se, b1, c2, e1, e2, gxo, gxp, geo, gep, xf, d1, gain, gfeed, gcross, tg)


def on_device(
    wide, hidden_in, encoder_out, cotangent, piece_starts, valid_lengths, bucket_table,
    gain_self, gain_cross, gain_feed, relative_bias, *mats
):
    me = lax.axis_index("narrow")
    sq, sk, sv, so, cq, ck, cv, co, gate, up, down = mats
    ps = jnp.concatenate((sq, so, sk, sv), axis=1)
    pc = jnp.concatenate((cq, co, ck, cv), axis=1)
    pf = jnp.concatenate((gate, up, down), axis=1)
    tab = jnp.pad(relative_bias.T, ((0, 29), (0, 96)))
    padded = jnp.pad(bucket_table, (0, 1), constant_values=-1)
    hot = (padded[None, :] == jnp.arange(BUCKETS)[:, None]).astype(f32)
    gains = jnp.stack((gain_self, gain_cross, gain_feed))
    (
        xf, ws, wc, _, gff, ef, q, kv, at, p, cqh, ckv, cat, cp, h1, outp, d2, gg_feed,
    ) = forward(
        wide, piece_starts, valid_lengths, hidden_in[:, 0], encoder_out[:, 0], cotangent[:, 0], tab, hot, ps, pc, pf, gains
    )
    ws, wc = (g.reshape(4, D, D) for g in (ws, wc))
    xs, es = xf.reshape(LEN, D), ef.reshape(ENC, D)
    gcr, d1, gg_cross, geo, gep, o1, o2, o3 = cross_backward(wide, h1, es, d2, wc, gains, cqh, ckv, cat, cp, gff)
    gse, gxo, gxp, dl, b1, c2, e1, e2, outs = self_backward(
        wide, xs, d1, ws, gains, q, kv, at, p, gcr, o1, o2, o3, outp.reshape(2, 256, D)
    )
    tg = lax.dot_general(hot, dl.reshape(12, 2048), (((1,), (1,)), ((), ())), precision=precise)
    order = jnp.arange(12) // 3 ^ me ^ 1
    tg = tg.reshape(BUCKETS, 4, 3)
    tg = sum(jnp.where(order == k, jnp.tile(tg[:, k], (1, 4)), 0.0) for k in range(4))
    tg = jnp.pad(tg, ((0, 0), (0, 116)))
    two = lambda a: a.reshape(2, -1, D)
    gin, gen, sg, st, f, b, a = reduce_all(
        wide, gse, b1, c2, e1, e2, two(gxo), two(gxp), two(geo), two(gep), xf, two(d1), gains, gg_feed, gg_cross, tg
    )
    tg = lax.dynamic_slice_in_dim(st, me * 3, 3, axis=1)
    return (
        outs[:, None], gin[:, None], gen[:, None],
        sg[0], sg[1], sg[2], tg,
        a[:, :192], a[:, 384:576], a[:, 576:], a[:, 192:384],
        b[:, :192], b[:, 384:576], b[:, 576:], b[:, 192:384],
        f[:, :512], f[:, 512:1024], f[:, 1024:],
    )


def solution(mesh):
    rows = P(None, ("dp", "wide"), "narrow", None)
    mat = P("wide", "narrow")
    return jax.shard_map(
        partial(on_device, mesh.shape["wide"]),
        mesh=mesh,
        in_specs=(rows, rows, rows, P(None, ("dp", "wide")), P(None, ("dp", "wide")), P(), P(), P(), P(), P(None, "narrow"))
        + (mat,) * 11,
        out_specs=(rows, rows, rows, P(), P(), P(), P(None, "narrow")) + (mat,) * 11,
        check_vma=False,
    )
```
